128 devices in a mesh: gx: 16 (over x, z), gy: 8 (over y, core).
Axes of the slice: x: 4, y: 4, z: 4, core: 2. Of those that a mesh axis runs over, the one named last changes fastest.
Arguments:
- basis: float32 [4, 40, 256, 1024], P(None, None, 'gx', 'gy'), may hold values from -6 to 6
- soil: int32 [40, 256, 1024], P(None, 'gx', 'gy'), may hold values from 0 to 7
- frozen: int32 [40, 256, 1024], P(None, 'gx', 'gy'), may hold values 0 or 1
- soil_table: float32 [4, 8], replicated, may hold values from 0.25 to 4
- coarse_basis: bfloat16 [16, 8, 32, 307200], P('gx', 'gy'), may hold values from -0.01171875 to 0.01171875
- coarse_inverse: float32 [4096, 4096], P(('gx', 'gy')), as said below
- active_count: int32 [16, 8], P('gx', 'gy'), may hold values from 8 to 32, as said below
Outputs:
- precond: float32 [40, 256, 1024], P(None, 'gx', 'gy')
- next_vector: float32 [40, 256, 1024], P(None, 'gx', 'gy')
- hessenberg: float32 [5], replicated
The draws below stay inside these ranges and needn't reach their ends.
Inputs may be any that keep to these rules, and one draw needn't show every extreme that they name: coarse_inverse is symmetric: entry (i, j) equals entry (j, i). A subdomain uses its first active_count coarse vectors; both 32 and 8 occur in every draw.
All inputs are finite; a program needn't handle non-finite values. No bound on the sum of `frozen` on one device may be relied on, other than what follows from the above.
Results may differ from the reference program's by a relative error of at most 0.005.
Values may be sent and summed in bfloat16 or wider, within the bound.
No kernel may reach another device: no remote copies, remote signals or barrier semaphores. Data moves between devices by JAX's collectives and lax.ppermute only.
A program may use at most 128 MiB of HBM per device.

```python
import math
import jax
import jax.numpy as jnp
from jax import lax

CX = 16
CY = 128
L = 40
OV = 16
K = 32
J = 4
NSOIL = 8
NX = 256
NY = 1024
EX = 48
EY = 160
NC = 4096
N_GX = 16
N_GY = 8


def draw_basis(key, part):
    key = jax.random.fold_in(key, 5)
    first, second = jax.random.split(key)
    shared = jax.random.normal(first, (1, L, NX, NY), jnp.float32)
    own = jax.random.normal(second, (J, L, NX, NY), jnp.float32)
    mixed = 0.6 * shared + 0.8 * own
    return jnp.clip(mixed, -6.0, 6.0).astype(jnp.float32)


def draw_coarse_inverse(key, part):
    key = jax.random.fold_in(key, 11)
    first, second = jax.random.split(key)
    raw = jax.random.normal(first, (NC, NC), jnp.float32)
    spread = (raw + raw.T) * (0.283 / math.sqrt(NC))
    matrix = spread + jnp.eye(NC, dtype=jnp.float32)
    logs = jax.random.uniform(second, (NC,), jnp.float32, math.log(4.0), math.log(40.0))
    roots = jnp.exp(0.5 * logs)
    return (roots[:, None] * matrix * roots[None, :]).astype(jnp.float32)


def draw_active_count(key, part):
    key = jax.random.fold_in(key, 23)
    first, second, third = jax.random.split(key, 3)
    total = N_GX * N_GY
    counts = jax.random.randint(first, (total,), K // 4, K + 1, dtype=jnp.int32)
    place = jax.random.randint(second, (), 0, total, dtype=jnp.int32)
    other = (place + 1 + jax.random.randint(third, (), 0, total - 1, dtype=jnp.int32)) % total
    counts = counts.at[place].set(K).at[other].set(K // 4)
    return counts.reshape(N_GX, N_GY)


def set_ends(values, stream_key, smallest, largest):
    longest = values.shape.index(max(values.shape))
    spots = []
    for shift in (0, 1):
        where = [jax.random.randint(jax.random.fold_in(stream_key, axis), (), 0, length) for axis, length in enumerate(values.shape)]
        where[longest] = (where[longest] + shift) % values.shape[longest]
        spots.append(tuple(where))
    return values.at[spots[0]].set(smallest).at[spots[1]].set(largest)


def shard_levels(stream_key, dims, cuts, smallest, high):
    factor_of, own = 1.0, jax.random.fold_in(stream_key, 6)
    for position, shards_of in cuts:
        steps = jnp.exp(jax.random.uniform(jax.random.fold_in(own, position), (shards_of,), jnp.float32, smallest / len(cuts), high / len(cuts)))
        factor_of = factor_of * jnp.repeat(steps, dims[position] // shards_of).reshape([-1 if axis == position else 1 for axis in range(len(dims))])
    return factor_of


def gaussian(rng, shape, scale, most, pieces=(), held_as=jnp.bfloat16):
    entries = jax.random.normal(rng, shape, jnp.float32) * scale
    if len(pieces) > 0:
        entries = shard_levels(rng, shape, pieces, -0.22, 0.18) * entries
    return jnp.clip(entries, min=-most, max=most).astype(held_as)


def setup_inputs(seed: int = 0) -> dict:
    keys = jax.random.split(jax.random.key(seed), 8)
    return {
        "basis": draw_basis(jax.random.fold_in(keys[7], 71), 0),
        "soil": set_ends(jax.random.randint(keys[1], (L, NX, NY), 0, NSOIL), jax.random.fold_in(keys[1], 1), 0, NSOIL - 1).astype(jnp.int32),
        "frozen": set_ends((jax.random.randint(keys[2], (L, NX, NY), 0, 2) < 1).astype(jnp.int32), jax.random.fold_in(keys[2], 1), 0, 1),
        "soil_table": jnp.clip(jnp.exp(jax.random.uniform(keys[3], (4, NSOIL), jnp.float32, math.log(0.25), math.log(4.0))), 0.25, 4.0),
        "coarse_basis": gaussian(keys[4], (N_GX, N_GY, K, L * EX * EY), (L * EX * EY) ** -0.5, 0.01171875, ((0, 16), (1, 8))),
        "coarse_inverse": draw_coarse_inverse(jax.random.fold_in(keys[7], 71), 0),
        "active_count": draw_active_count(jax.random.fold_in(keys[7], 71), 0),
    }


weight_vertical = 4.0
weight_horizontal = 1.0
epsilon = 1e-06

def harmonic(first, second):
    return 2.0 * first * second / (first + second)

def properties(soil, frozen, soil_table):
    classes = soil_table.shape[1]
    conduct = jnp.zeros(soil.shape, jnp.float32)
    storage = jnp.zeros(soil.shape, jnp.float32)
    icy = frozen == 1
    for index in range(classes):
        match = soil == index
        conduct = jnp.where(match, jnp.where(icy, soil_table[1, index], soil_table[0, index]), conduct)
        storage = jnp.where(match, jnp.where(icy, soil_table[3, index], soil_table[2, index]), storage)
    return (conduct, storage)

def vertical_faces(conduct):
    inner = weight_vertical * harmonic(conduct[:-1], conduct[1:])
    zero = jnp.zeros_like(conduct[:1])
    return (jnp.concatenate([zero, inner], axis=0), jnp.concatenate([inner, zero], axis=0))

def column_solve(diagonal, below, above, source):
    layers = source.shape[0]
    ratios = [-above[0] / diagonal[0]]
    values = [source[0] / diagonal[0]]
    for level in range(1, layers):
        denom = diagonal[level] + below[level] * ratios[level - 1]
        ratios.append(-above[level] / denom)
        values.append((source[level] + below[level] * values[level - 1]) / denom)
    result = [values[layers - 1]]
    for level in range(layers - 2, -1, -1):
        result.append(values[level] - ratios[level] * result[-1])
    return jnp.stack(result[::-1], axis=0)

def apply_operator(padded_field, padded_conduct, storage, below, above):
    field = padded_field[:, 1:-1, 1:-1]
    conduct = padded_conduct[:, 1:-1, 1:-1]
    zero = jnp.zeros_like(field[:1])
    under = jnp.concatenate([zero, field[:-1]], axis=0)
    over = jnp.concatenate([field[1:], zero], axis=0)
    total = storage * field + below * (field - under) + above * (field - over)
    sides = ((padded_field[:, :-2, 1:-1], padded_conduct[:, :-2, 1:-1]), (padded_field[:, 2:, 1:-1], padded_conduct[:, 2:, 1:-1]), (padded_field[:, 1:-1, :-2], padded_conduct[:, 1:-1, :-2]), (padded_field[:, 1:-1, 2:], padded_conduct[:, 1:-1, 2:]))
    for neighbour, neighbour_k in sides:
        total = total + weight_horizontal * harmonic(conduct, neighbour_k) * (field - neighbour)
    return total

def reference(basis, soil, frozen, soil_table, coarse_basis, coarse_inverse, active_count):
    conduct, storage = properties(soil, frozen, soil_table)
    below, above = vertical_faces(conduct)
    diagonal = storage + 4.0 * weight_horizontal * conduct + below + above
    current = basis[J - 1]
    local_part = column_solve(diagonal, below, above, current)
    half_vector = current.astype(jnp.bfloat16)
    padded_vector = jnp.pad(half_vector, ((0, 0), (OV, OV), (OV, OV)))
    subdomains = N_GX * N_GY
    active = (jnp.arange(K, dtype=jnp.int32)[None, :] < active_count.reshape(-1)[:, None]).astype(jnp.float32)
    zero_index = jnp.zeros((), jnp.int32)
    all_blocks = coarse_basis.reshape(subdomains, K, L * EX * EY)

    def block_of(index):
        col_index = (index // N_GY).astype(jnp.int32)
        row_index = (index % N_GY).astype(jnp.int32)
        block = lax.dynamic_index_in_dim(all_blocks, index.astype(jnp.int32), 0, keepdims=False)
        return (block, col_index, row_index)

    def project(index):
        block, col_index, row_index = block_of(index.astype(jnp.int32))
        window = lax.dynamic_slice(padded_vector, (zero_index, col_index * CX, row_index * CY), (L, EX, EY))
        return jnp.dot(block, window.reshape(-1), preferred_element_type=jnp.float32)
    coarse_rhs = lax.map(project, jnp.arange(subdomains, dtype=jnp.int32)) * active
    coarse_solution = jnp.dot(coarse_inverse, coarse_rhs.reshape(-1), precision=lax.Precision.HIGHEST).reshape(subdomains, K) * active
    half_solution = coarse_solution.astype(jnp.bfloat16)

    def accumulate(index, total):
        index = jnp.asarray(index).astype(jnp.int32)
        block, col_index, row_index = block_of(index)
        weights = lax.dynamic_index_in_dim(half_solution, index, 0, keepdims=False)
        spread = jnp.dot(weights, block, preferred_element_type=jnp.float32).reshape(L, EX, EY)
        start = (zero_index, col_index * CX, row_index * CY)
        present = lax.dynamic_slice(total, start, (L, EX, EY))
        return lax.dynamic_update_slice(total, present + spread, start)
    gathered = lax.fori_loop(0, subdomains, accumulate, jnp.zeros((L, NX + 2 * OV, NY + 2 * OV), jnp.float32))
    correction = gathered[:, OV:OV + NX, OV:OV + NY]
    precond = local_part + correction
    edges = ((0, 0), (1, 1), (1, 1))
    image = apply_operator(jnp.pad(precond, edges), jnp.pad(conduct, edges), storage, below, above)
    cells = L * NX * NY
    projections = jnp.einsum('jlxy,lxy->j', basis, image, precision=lax.Precision.HIGHEST) / cells
    orthogonal = image - jnp.einsum('j,jlxy->lxy', projections, basis, precision=lax.Precision.HIGHEST)
    length = jnp.sqrt(jnp.sum(orthogonal * orthogonal) / cells + epsilon)
    next_vector = orthogonal / length
    hessenberg = jnp.concatenate([projections, length[None]])
    return (precond, next_vector, hessenberg)
```

```python
import functools

import jax
import jax.numpy as jnp
from jax import lax
from jax.experimental import pallas as pl
from jax.experimental.pallas import tpu as pltpu
from jax.sharding import PartitionSpec as P

F32 = jnp.float32
BF16 = jnp.bfloat16

LAYERS, ROWS, COLS, OV, K = 40, 16, 128, 16, 32
CELLS = LAYERS * ROWS
RUNS = CELLS // 4
FLAT = 5 * RUNS
WINDOW = 7680
PART = 2560
WEIGHT_V, WEIGHT_H, EPS = 4.0, 1.0, 1e-06

VM = pl.BlockSpec(memory_space=pltpu.VMEM)
SM = pl.BlockSpec(memory_space=pltpu.SMEM)


def shape(*dims, dtype=F32):
    return jax.ShapeDtypeStruct(dims, dtype)


def call(kernel, outs, specs, args, scratch=(), out_specs=None, flops=0, moved=0, name=None):
    return pl.pallas_call(
        kernel,
        out_shape=outs,
        in_specs=specs,
        out_specs=out_specs if out_specs is not None else jax.tree.map(lambda _: VM, outs),
        scratch_shapes=list(scratch),
        compiler_params=pltpu.CompilerParams(vmem_limit_bytes=16 * 2**20),
        cost_estimate=pl.CostEstimate(flops=flops, bytes_accessed=moved, transcendentals=0),
        name=name,
    )(*args)


def lanes(rows):
    return lax.broadcasted_iota(jnp.int32, (rows, COLS), 1)


def harmonic(first, second):
    return 2.0 * first * second / (first + second)


def turn(values, amount):
    return pltpu.roll(values, amount % COLS, 1)


def pack_kernel(basis, soil, frozen, up, dn, flat, code):
    code[...] = (soil[...] + 8 * frozen[...]).astype(F32)
    at = lanes(RUNS)
    to_up = jnp.zeros((RUNS, COLS), F32)
    to_dn = to_up
    flats = [jnp.zeros((RUNS, COLS), F32) for _ in range(5)]
    for q in range(4):
        cut = 32 * q + 16
        turned = turn(basis[0, pl.ds(q, RUNS, stride=4), :], cut)
        kind = code[pl.ds(q, RUNS, stride=4), :]
        low = (at >= cut - 16) & (at < cut)
        high = (at >= cut) & (at < cut + 16)
        to_up = jnp.where(low, turned, jnp.where(at == cut, turn(kind, cut + 1), to_up))
        to_dn = jnp.where(high, turned, jnp.where(at == cut - 1, turn(kind, cut - 1), to_dn))
        flats[q] = jnp.where(at >= cut, turned, flats[q])
        flats[q + 1] = jnp.where(at < cut, turned, flats[q + 1])
    up[...] = to_up.astype(BF16)
    dn[...] = to_dn.astype(BF16)
    for j in range(5):
        flat[j * RUNS : (j + 1) * RUNS, :] = flats[j].astype(BF16)
    rows = [code[pl.ds(0, LAYERS, stride=ROWS), :], code[pl.ds(ROWS - 1, LAYERS, stride=ROWS), :]]
    flat[FLAT:, :] = jnp.concatenate(rows, axis=0).astype(BF16)


def flat_kernel(own, left, right, out):
    place = lax.axis_index("gy")
    last = lax.axis_size("gy") - 1
    at = lanes(RUNS)
    from_left = jnp.where(place > 0, left[...].astype(F32), 0.0)
    from_right = jnp.where(place < last, right[...].astype(F32), 0.0)
    for j in range(5):
        part = own[j * RUNS : (j + 1) * RUNS, :].astype(F32)
        if j < 4:
            part = jnp.where((at >= 32 * j) & (at < 32 * j + 16), from_left, part)
        if j > 0:
            part = jnp.where((at >= 32 * j - 16) & (at < 32 * j), from_right, part)
        out[j * RUNS : (j + 1) * RUNS, :] = part.astype(BF16)
    out[FLAT:, :] = own[FLAT:, :]


def project_part(coarse, vector, part, totals):
    def body(layer, totals):
        totals = list(totals)
        base = pl.multiple_of(layer * WINDOW + part * PART, 128)
        wide = jnp.concatenate(
            [
                jnp.broadcast_to(vector[pl.ds(j * RUNS + layer * 4 + m, 1), :], (8, COLS))
                for m in range(4)
                for j in range(5)
            ],
            axis=1,
        )
        for r in range(4):
            product = coarse[8 * r : 8 * r + 8, pl.ds(base, PART)].astype(F32) * wide
            for t in range(20):
                slot = 2 * r + t % 2
                totals[slot] = totals[slot] + product[:, t * COLS : (t + 1) * COLS]
        return tuple(totals)

    return lax.fori_loop(0, LAYERS, body, totals, unroll=4)


def own_rhs_kernel(coarse, own, out, vector):
    vector[...] = own[:FLAT, :].astype(F32)
    zero = jnp.zeros((8, COLS), F32)
    totals = project_part(coarse, vector, 1, (zero,) * 8)
    for r in range(4):
        out[8 * r : 8 * r + 8, :] = totals[2 * r] + totals[2 * r + 1]


def rhs_kernel(coarse, begun, before, after, count, out, vector):
    place = lax.axis_index("gx")
    last = lax.axis_size("gx") - 1
    zero = jnp.zeros((8, COLS), F32)
    totals = tuple(begun[4 * s : 4 * s + 8, :] if s % 2 == 0 else zero for s in range(8))
    vector[...] = jnp.where(place > 0, before[:FLAT, :].astype(F32), 0.0)
    totals = project_part(coarse, vector, 0, totals)
    vector[...] = jnp.where(place < last, after[:FLAT, :].astype(F32), 0.0)
    totals = project_part(coarse, vector, 2, totals)
    full = jnp.concatenate([totals[2 * r] + totals[2 * r + 1] for r in range(4)], axis=0)
    sums = jnp.sum(full, axis=1, keepdims=True)
    index = lax.broadcasted_iota(jnp.int32, (K, COLS), 0)
    keep = (lanes(K) % K == index) & (index < count[0, 0])
    row = jnp.sum(jnp.where(keep, sums, 0.0), axis=0, keepdims=True)
    out[...] = jnp.broadcast_to(row, out.shape)


def reduce_eight(parts, where):
    four, two, one = where

    def merge(a, b, mask, step):
        kept = jnp.where(mask, a, b)
        moved = jnp.where(mask, b, a)
        if step == 4:
            return kept + pltpu.roll(moved, 4, 0)
        return kept + jnp.where(mask, pltpu.roll(moved, 8 - step, 0), pltpu.roll(moved, step, 0))

    parts = [merge(parts[t], parts[t + 4], four, 4) for t in range(4)]
    parts = [merge(parts[t], parts[t + 2], two, 2) for t in range(2)]
    return merge(parts[0], parts[1], one, 1)


def spread_part(coarse, weights, part, out):
    row = lax.broadcasted_iota(jnp.int32, (8, COLS), 0)
    where = (row < 4, row % 4 < 2, row % 2 < 1)

    def body(pair, carry):
        halves = []
        for half in range(2):
            base = pl.multiple_of((2 * pair + half) * WINDOW + part * PART, 128)
            terms = [
                coarse[8 * r : 8 * r + 8, pl.ds(base, PART)].astype(F32) * weights[r]
                for r in range(4)
            ]
            halves.append((terms[0] + terms[1]) + (terms[2] + terms[3]))
        for j in range(5):
            tiles = [
                halves[half][:, (5 * m + j) * COLS : (5 * m + j + 1) * COLS]
                for half in range(2)
                for m in range(4)
            ]
            start = pl.multiple_of(j * RUNS + 8 * pair, 8)
            out[pl.ds(start, 8), :] = reduce_eight(tiles, where)
        return carry

    lax.fori_loop(0, LAYERS // 2, body, 0, unroll=2)


def spread_kernel(
    coarse, inverse, gathered, count, local, own, up, dn, up2, dn2, edge, rhs, low, high
):
    at = lanes(K)
    rows = jnp.zeros((K, COLS), F32)
    for e in range(4):
        rows = jnp.where(at // K == e, gathered[pl.ds(e, K, stride=4), :], rows)
    rhs[...] = rows
    total = jnp.zeros((K, COLS), F32)
    for i in range(K):
        total = total + inverse[:, i * COLS : (i + 1) * COLS] * rhs[i : i + 1, :]
    solved = jnp.sum(total, axis=1, keepdims=True)
    index = lax.broadcasted_iota(jnp.int32, (K, COLS), 0)
    solved = jnp.where(index < count[0, 0], solved, 0.0).astype(BF16).astype(F32)
    weights = [
        jnp.concatenate([solved[8 * r : 8 * r + 8, :]] * (PART // COLS), axis=1) for r in range(4)
    ]
    spread_part(coarse, weights, 0, low)
    spread_part(coarse, weights, 2, high)
    spread_part(coarse, weights, 1, own)
    at = lanes(LAYERS)

    def strip(ref, j, m):
        return ref[pl.ds(j * RUNS + m, LAYERS, stride=4), :]

    def both(first, second):
        return jnp.concatenate([first, second], axis=0)

    def put(ref, whole, ring):
        ref[:FLAT, :] = whole[...].astype(BF16)
        top = ring.astype(BF16)
        ref[FLAT : FLAT + 80, :] = top
        ref[FLAT + 80 :, :] = (ring - top.astype(F32)).astype(BF16)

    last = strip(local, 3, 3)
    put(
        up,
        high,
        both(
            strip(own, 3, 3) + jnp.where(at >= 112, last, 0.0),
            strip(own, 4, 3) + jnp.where(at < 112, last, 0.0),
        ),
    )
    first = strip(local, 0, 0)
    put(
        dn,
        low,
        both(
            strip(own, 0, 0) + jnp.where(at >= 16, first, 0.0),
            strip(own, 1, 0) + jnp.where(at < 16, first, 0.0),
        ),
    )
    up2[...] = both(strip(high, 3, 3), strip(high, 4, 3)).astype(BF16)
    dn2[...] = both(strip(low, 0, 0), strip(low, 1, 0)).astype(BF16)
    edge[:80, :] = both(strip(low, 3, 3), strip(low, 4, 3))
    edge[80:, :] = both(strip(high, 0, 0), strip(high, 1, 0))


def fold_rows_kernel(own, edge, local, before, after, before2, after2, field, rim, up, dn):
    place = lax.axis_index("gx")
    last = lax.axis_size("gx") - 1
    at = lanes(RUNS)
    whole = []
    for j in range(5):
        cut = slice(j * RUNS, (j + 1) * RUNS)
        part = (
            own[cut, :]
            + jnp.where(place > 0, before[cut, :].astype(F32), 0.0)
            + jnp.where(place < last, after[cut, :].astype(F32), 0.0)
        )
        if j < 4:
            part = part + jnp.where(at >= 32 * j + 16, local[cut, :], 0.0)
        if j > 0:
            behind = local[(j - 1) * RUNS : j * RUNS, :]
            part = part + jnp.where(at < 32 * j - 16, behind, 0.0)
        whole.append(part)
    to_up = jnp.zeros((RUNS, COLS), F32)
    to_dn = to_up
    for q in range(4):
        field[q * RUNS : (q + 1) * RUNS, :] = jnp.where(
            at >= 32 * q + 16, whole[q], whole[q + 1]
        )
        band = (at >= 32 * q) & (at < 32 * q + 32)
        to_up = jnp.where(band, whole[q + 1], to_up)
        to_dn = jnp.where(band, whole[q], to_dn)
    up[:RUNS, :] = to_up
    dn[:RUNS, :] = to_dn

    def ring(ours, near, far, valid):
        return (
            ours
            + near[FLAT : FLAT + 80, :].astype(F32)
            + near[FLAT + 80 :, :].astype(F32)
            + jnp.where(valid, far[...].astype(F32), 0.0)
        )

    top = ring(edge[:80, :], before, before2, place > 1)
    bottom = ring(edge[80:, :], after, after2, place < last - 1)
    at = lanes(LAYERS)
    half = LAYERS
    rim[:half, :] = jnp.where(at >= 112, top[:half], top[half:])
    rim[half:, :] = jnp.where(at >= 16, bottom[:half], bottom[half:])
    up[RUNS:, :] = jnp.where(at >= 96, top[half:], bottom[half:])
    dn[RUNS:, :] = jnp.where(at >= 96, top[:half], bottom[:half])


def look_up(kind, table, rows):
    value = jnp.zeros(kind.shape, F32)
    for index in range(8):
        value = jnp.where(kind == index, table[rows[0], index], value)
        value = jnp.where(kind == index + 8, table[rows[1], index], value)
    return value


def columns_kernel(basis, soil, frozen, table, conduct, diagonal, above, local, gram, ratio, value):
    kind = soil[...] + 8 * frozen[...]
    conduct[...] = look_up(kind, table, (0, 1))
    diagonal[...] = look_up(kind, table, (2, 3))
    zero = jnp.zeros((ROWS, COLS), F32)
    grams = [jnp.zeros((8, COLS), F32) for _ in range(10)]
    below = zero
    last_ratio = zero
    last_value = zero
    for level in range(LAYERS):
        cut = slice(level * ROWS, (level + 1) * ROWS)
        own = conduct[cut, :]
        over = zero
        if level < LAYERS - 1:
            over = WEIGHT_V * harmonic(own, conduct[(level + 1) * ROWS : (level + 2) * ROWS, :])
        above[cut, :] = over
        sides = diagonal[cut, :] + below + over
        diagonal[cut, :] = sides
        denom = sides + 4.0 * WEIGHT_H * own + below * last_ratio
        inverse = 1.0 / denom
        last_ratio = -over * inverse
        last_value = (basis[3, cut, :] + below * last_value) * inverse
        ratio[cut, :] = last_ratio
        value[cut, :] = last_value
        below = over
        vectors = [basis[j, cut, :] for j in range(4)]
        slot = 0
        for i in range(4):
            for j in range(i, 4):
                square = vectors[i] * vectors[j]
                grams[slot] = grams[slot] + (square[:8] + square[8:])
                slot += 1
    for level in range(LAYERS - 2, -1, -1):
        cut = slice(level * ROWS, (level + 1) * ROWS)
        last_value = value[cut, :] - ratio[cut, :] * last_value
        value[cut, :] = last_value
    for q in range(4):
        local[q * RUNS : (q + 1) * RUNS, :] = turn(value[pl.ds(q, RUNS, stride=4), :], 32 * q + 16)
    for slot in range(10):
        gram[8 * slot : 8 * slot + 8, :] = grams[slot]


def faces_kernel(conduct, diagonal, table, left, right, before, after, faces, total, side):
    gx, gy = lax.axis_index("gx"), lax.axis_index("gy")
    last_x, last_y = lax.axis_size("gx") - 1, lax.axis_size("gy") - 1
    at = lanes(RUNS)
    from_left, from_right = left[...].astype(F32), right[...].astype(F32)
    kinds = jnp.zeros((RUNS, COLS), F32)
    for q in range(4):
        kinds = jnp.where(at == 32 * q + 16, from_left, kinds)
        kinds = jnp.where(at == 32 * q + 15, from_right, kinds)
    known = look_up(kinds.astype(jnp.int32), table, (0, 1))
    for q in range(4):
        side[pl.ds(q, RUNS, stride=4), :] = turn(known, -(32 * q + 16))
    row_before = look_up(before[FLAT:, :].astype(F32).astype(jnp.int32), table, (0, 1))
    row_after = look_up(after[FLAT:, :].astype(F32).astype(jnp.int32), table, (0, 1))
    at = lanes(ROWS)
    row = lax.broadcasted_iota(jnp.int32, (ROWS, COLS), 0)
    for level in range(LAYERS):
        cut = slice(level * ROWS, (level + 1) * ROWS)
        own = conduct[cut, :]
        aside = side[cut, :]
        over = row_before[LAYERS + level : LAYERS + level + 1, :]
        under = row_after[level : level + 1, :]
        weights = [
            jnp.where((at > 0) | (gy > 0), harmonic(own, jnp.where(at == 0, aside, turn(own, 1))), 0.0),
            jnp.where(
                (at < COLS - 1) | (gy < last_y),
                harmonic(own, jnp.where(at == COLS - 1, aside, turn(own, -1))),
                0.0,
            ),
            jnp.where(
                (row > 0) | (gx > 0),
                harmonic(own, jnp.where(row == 0, over, pltpu.roll(own, 1, 0))),
                0.0,
            ),
            jnp.where(
                (row < ROWS - 1) | (gx < last_x),
                harmonic(own, jnp.where(row == ROWS - 1, under, pltpu.roll(own, ROWS - 1, 0))),
                0.0,
            ),
        ]
        for index in range(4):
            faces[index, cut, :] = WEIGHT_H * weights[index]
        total[cut, :] = diagonal[cut, :] + WEIGHT_H * (
            (weights[0] + weights[1]) + (weights[2] + weights[3])
        )


def image_kernel(
    field, rim, up, dn, left, right, basis, faces, total, above, gram, precond, image, sums, side
):
    gy = lax.axis_index("gy")
    last_y = lax.axis_size("gy") - 1
    at = lanes(RUNS)
    from_left = jnp.where(gy > 0, left[...], 0.0)
    from_right = jnp.where(gy < last_y, right[...], 0.0)
    to_left = dn[...] + from_left
    to_right = up[...] + from_right
    for q in range(4):
        cut = 32 * q + 16
        turned = field[q * RUNS : (q + 1) * RUNS, :]
        turned = turned + jnp.where((at >= cut) & (at < cut + 16), from_left[:RUNS], 0.0)
        turned = turned + jnp.where((at >= cut - 16) & (at < cut), from_right[:RUNS], 0.0)
        precond[pl.ds(q, RUNS, stride=4), :] = turn(turned, -cut)
        edges = jnp.where(at == cut - 1, to_left[:RUNS], to_right[:RUNS])
        side[pl.ds(q, RUNS, stride=4), :] = turn(edges, -cut)
    at = lanes(LAYERS)
    rim_left, rim_right = from_left[RUNS:], from_right[RUNS:]
    over = rim[:LAYERS, :]
    over = over + jnp.where(at >= 112, rim_left, 0.0)
    over = turn(over + jnp.where((at >= 96) & (at < 112), rim_right, 0.0), -112)
    under = rim[LAYERS:, :]
    under = under + jnp.where((at >= 16) & (at < 32), rim_left, 0.0)
    under = turn(under + jnp.where(at < 16, rim_right, 0.0), -16)
    at = lanes(ROWS)
    row = lax.broadcasted_iota(jnp.int32, (ROWS, COLS), 0)
    totals = [jnp.zeros((8, COLS), F32) for _ in range(5)]
    for level in range(LAYERS):
        cut = slice(level * ROWS, (level + 1) * ROWS)
        own = precond[cut, :]
        aside = side[cut, :]
        result = total[cut, :] * own
        result = result - faces[0, cut, :] * jnp.where(at == 0, turn(aside, 1), turn(own, 1))
        result = result - faces[1, cut, :] * jnp.where(
            at == COLS - 1, turn(aside, -1), turn(own, -1)
        )
        result = result - faces[2, cut, :] * jnp.where(
            row == 0, over[level : level + 1, :], pltpu.roll(own, 1, 0)
        )
        result = result - faces[3, cut, :] * jnp.where(
            row == ROWS - 1, under[level : level + 1, :], pltpu.roll(own, ROWS - 1, 0)
        )
        if level > 0:
            back = slice((level - 1) * ROWS, level * ROWS)
            result = result - above[back, :] * precond[back, :]
        if level < LAYERS - 1:
            ahead = slice((level + 1) * ROWS, (level + 2) * ROWS)
            result = result - above[cut, :] * precond[ahead, :]
        image[cut, :] = result
        for j in range(5):
            product = (basis[j, cut, :] if j < 4 else result) * result
            totals[j] = totals[j] + (product[:8] + product[8:])
    totals += [gram[8 * slot : 8 * slot + 8, :] for slot in range(10)]
    totals.append(jnp.zeros((8, COLS), F32))
    rows = jnp.concatenate([jnp.sum(part, axis=0, keepdims=True) for part in totals], axis=0)
    column = jnp.sum(rows, axis=1, keepdims=True)
    keep = lanes(ROWS) == lax.broadcasted_iota(jnp.int32, (ROWS, COLS), 0)
    line = jnp.sum(jnp.where(keep, column, 0.0), axis=0, keepdims=True)
    sums[...] = jnp.broadcast_to(line, sums.shape)


def next_kernel(gathered, image, basis, out, hessenberg):
    cells = float(CELLS * COLS * lax.axis_size("gx") * lax.axis_size("gy"))
    line = jnp.sum(gathered[...], axis=0, keepdims=True) / cells
    entry = [line[:, i : i + 1] for i in range(15)]
    project = entry[:4]
    square = entry[4]
    for j in range(4):
        square = square - 2.0 * project[j] * project[j]
    slot = 5
    for i in range(4):
        for j in range(i, 4):
            square = square + (1.0 if i == j else 2.0) * project[i] * project[j] * entry[slot]
            slot += 1
    length = jnp.sqrt(jnp.maximum(square, 0.0) + EPS)
    at = lanes(1)
    found = jnp.where(at == 4, length, jnp.where(at < 4, line, 0.0))
    for i in range(5):
        hessenberg[i] = found[0, i]
    inverse = 1.0 / length
    scaled = [project[j] * inverse for j in range(4)]
    for level in range(LAYERS):
        cut = slice(level * ROWS, (level + 1) * ROWS)
        value = image[cut, :] * inverse
        for j in range(4):
            value = value - scaled[j] * basis[j, cut, :]
        out[cut, :] = value


def shift(values, axis, step):
    count = lax.axis_size(axis)
    return lax.ppermute(values, axis, [(i, (i + step) % count) for i in range(count)])


def exchange(lines):
    size = lines.shape[0]
    out = lax.all_to_all(lines.reshape(size, 1, COLS), ("gx", "gy"), 0, 0)
    return out.reshape(size, COLS)


def on_device(basis, soil, frozen, soil_table, coarse_basis, coarse_inverse, active_count):
    basis = basis.reshape(4, CELLS, COLS)
    soil, frozen = soil.reshape(CELLS, COLS), frozen.reshape(CELLS, COLS)
    coarse = pltpu.with_memory_space_constraint(coarse_basis.reshape(K, -1), pltpu.VMEM)
    devices = lax.axis_size("gx") * lax.axis_size("gy")

    def pack(basis_ref, *refs):
        pack_kernel(basis_ref, *refs)

    one = pl.BlockSpec((1, CELLS, COLS), lambda i: (3, 0, 0))
    whole = pl.BlockSpec((CELLS, COLS), lambda i: (0, 0))
    up, dn, flat = pl.pallas_call(
        pack,
        grid=(1,),
        in_specs=[one, whole, whole],
        out_specs=[
            pl.BlockSpec((RUNS, COLS), lambda i: (0, 0)),
            pl.BlockSpec((RUNS, COLS), lambda i: (0, 0)),
            pl.BlockSpec((FLAT + 80, COLS), lambda i: (0, 0)),
        ],
        out_shape=[
            shape(RUNS, COLS, dtype=BF16),
            shape(RUNS, COLS, dtype=BF16),
            shape(FLAT + 80, COLS, dtype=BF16),
        ],
        scratch_shapes=[pltpu.VMEM((CELLS, COLS), F32)],
        compiler_params=pltpu.CompilerParams(vmem_limit_bytes=16 * 2**20),
        name="pack",
    )(basis, soil, frozen)
    left, right = shift(up, "gy", 1), shift(dn, "gy", -1)
    conduct, diagonal, above, local, gram = call(
        columns_kernel,
        [shape(CELLS, COLS)] * 4 + [shape(80, COLS)],
        [VM, VM, VM, SM],
        (basis, soil, frozen, soil_table),
        [pltpu.VMEM((CELLS, COLS), F32)] * 2,
        flops=10_000_000,
        moved=4_000_000,
        name="columns",
    )
    flat = call(
        flat_kernel, shape(FLAT + 80, COLS, dtype=BF16), [VM] * 3, (flat, left, right), name="flat"
    )
    before, after = shift(flat, "gx", 1), shift(flat, "gx", -1)
    begun = call(
        own_rhs_kernel,
        shape(K, COLS),
        [VM] * 2,
        (coarse, flat),
        [pltpu.VMEM((FLAT, COLS), F32)],
        flops=6_000_000,
        moved=6_000_000,
        name="own_rhs",
    )
    lines = call(
        rhs_kernel,
        shape(devices, COLS),
        [VM] * 4 + [SM],
        (coarse, begun, before, after, active_count),
        [pltpu.VMEM((FLAT, COLS), F32)],
        flops=12_000_000,
        moved=12_000_000,
        name="rhs",
    )
    gathered = exchange(lines)
    message = shape(FLAT + 160, COLS, dtype=BF16)
    small = shape(80, COLS, dtype=BF16)
    own, up, dn, up2, dn2, edge = call(
        spread_kernel,
        [shape(FLAT, COLS), message, message, small, small, shape(160, COLS)],
        [VM, VM, VM, SM, VM],
        (coarse, coarse_inverse, gathered, active_count, local),
        [pltpu.VMEM((K, COLS), F32)] + [pltpu.VMEM((FLAT, COLS), F32)] * 2,
        flops=40_000_000,
        moved=20_000_000,
        name="spread",
    )
    near = shift(up, "gx", 1), shift(dn, "gx", -1)
    far = shift(up2, "gx", 2), shift(dn2, "gx", -2)
    faces, total = call(
        faces_kernel,
        [shape(4, CELLS, COLS), shape(CELLS, COLS)],
        [VM, VM, SM, VM, VM, VM, VM],
        (conduct, diagonal, soil_table, left, right, before, after),
        [pltpu.VMEM((CELLS, COLS), F32)],
        flops=4_000_000,
        moved=2_000_000,
        name="faces",
    )
    field, rim, up, dn = call(
        fold_rows_kernel,
        [shape(CELLS, COLS), shape(80, COLS), shape(RUNS + LAYERS, COLS), shape(RUNS + LAYERS, COLS)],
        [VM] * 7,
        (own, edge, local, *near, *far),
        name="fold_rows",
    )
    left, right = shift(up, "gy", 1), shift(dn, "gy", -1)
    precond, image, sums = call(
        image_kernel,
        [shape(CELLS, COLS), shape(CELLS, COLS), shape(devices, COLS)],
        [VM] * 11,
        (field, rim, up, dn, left, right, basis, faces, total, above, gram),
        [pltpu.VMEM((CELLS, COLS), F32)],
        name="image",
    )
    gathered = exchange(sums)
    following, hessenberg = call(
        next_kernel,
        [shape(CELLS, COLS), shape(5)],
        [VM] * 3,
        (gathered, image, basis),
        out_specs=[VM, SM],
        name="next",
    )
    tile = (LAYERS, ROWS, COLS)
    return precond.reshape(tile), following.reshape(tile), hessenberg


def solution(mesh):
    placed = (
        P(None, None, "gx", "gy"),
        P(None, "gx", "gy"),
        P(None, "gx", "gy"),
        P(),
        P("gx", "gy", None, None),
        P(("gx", "gy"), None),
        P("gx", "gy"),
    )
    return jax.shard_map(
        on_device,
        mesh=mesh,
        in_specs=placed,
        out_specs=(P(None, "gx", "gy"), P(None, "gx", "gy"), P()),
        check_vma=False,
    )
```

```python
import functools

import jax
import jax.numpy as jnp
from jax import lax
from jax.experimental import pallas as pl
from jax.experimental.pallas import tpu as pltpu
from jax.sharding import PartitionSpec as P

F32 = jnp.float32
BF16 = jnp.bfloat16

LAYERS, ROWS, COLS, OV, K = 40, 16, 128, 16, 32
CELLS = LAYERS * ROWS
RUNS = CELLS // 4
FLAT = 5 * RUNS
WINDOW = 7680
EARLY = 10
CHUNK = 10
PART = 2560
WEIGHT_V, WEIGHT_H, EPS = 4.0, 1.0, 1e-06

VM = pl.BlockSpec(memory_space=pltpu.VMEM)
SM = pl.BlockSpec(memory_space=pltpu.SMEM)
HB = pl.BlockSpec(memory_space=pltpu.HBM)


def shape(*dims, dtype=F32):
    return jax.ShapeDtypeStruct(dims, dtype)


def call(kernel, outs, specs, args, scratch=(), out_specs=None, flops=0, moved=0, name=None):
    return pl.pallas_call(
        kernel,
        out_shape=outs,
        in_specs=specs,
        out_specs=out_specs if out_specs is not None else jax.tree.map(lambda _: VM, outs),
        scratch_shapes=list(scratch),
        compiler_params=pltpu.CompilerParams(vmem_limit_bytes=16 * 2**20),
        cost_estimate=pl.CostEstimate(flops=flops, bytes_accessed=moved, transcendentals=0),
        name=name,
    )(*args)


def lanes(rows):
    return lax.broadcasted_iota(jnp.int32, (rows, COLS), 1)


def harmonic(first, second):
    return 2.0 * first * second / (first + second)


def turn(values, amount):
    return pltpu.roll(values, amount % COLS, 1)


def pack_kernel(basis_in, soil_in, frozen_in, up, dn, flat, basis, soil, frozen, code, arrived):
    copies = [
        pltpu.make_async_copy(basis_in.at[3], basis, arrived.at[0]),
        pltpu.make_async_copy(soil_in, soil, arrived.at[1]),
        pltpu.make_async_copy(frozen_in, frozen, arrived.at[2]),
    ]
    for copy in copies:
        copy.start()
    for copy in copies:
        copy.wait()
    code[...] = (soil[...] + 8 * frozen[...]).astype(F32)
    at = lanes(RUNS)
    to_up = jnp.zeros((RUNS, COLS), F32)
    to_dn = to_up
    flats = [jnp.zeros((RUNS, COLS), F32) for _ in range(5)]
    for q in range(4):
        cut = 32 * q + 16
        turned = turn(basis[pl.ds(q, RUNS, stride=4), :], cut)
        kind = code[pl.ds(q, RUNS, stride=4), :]
        low = (at >= cut - 16) & (at < cut)
        high = (at >= cut) & (at < cut + 16)
        to_up = jnp.where(low, turned, jnp.where(at == cut, turn(kind, cut + 1), to_up))
        to_dn = jnp.where(high, turned, jnp.where(at == cut - 1, turn(kind, cut - 1), to_dn))
        flats[q] = jnp.where(at >= cut, turned, flats[q])
        flats[q + 1] = jnp.where(at < cut, turned, flats[q + 1])
    up[...] = to_up.astype(BF16)
    dn[...] = to_dn.astype(BF16)
    for j in range(5):
        flat[j * RUNS : (j + 1) * RUNS, :] = flats[j].astype(BF16)
    rows = [code[pl.ds(0, LAYERS, stride=ROWS), :], code[pl.ds(ROWS - 1, LAYERS, stride=ROWS), :]]
    flat[FLAT:, :] = jnp.concatenate(rows, axis=0).astype(BF16)


def flat_kernel(own, left, right, out):
    place = lax.axis_index("gy")
    last = lax.axis_size("gy") - 1
    at = lanes(RUNS)
    from_left = jnp.where(place > 0, left[...].astype(F32), 0.0)
    from_right = jnp.where(place < last, right[...].astype(F32), 0.0)
    for j in range(5):
        part = own[j * RUNS : (j + 1) * RUNS, :].astype(F32)
        if j < 4:
            part = jnp.where((at >= 32 * j) & (at < 32 * j + 16), from_left, part)
        if j > 0:
            part = jnp.where((at >= 32 * j - 16) & (at < 32 * j), from_right, part)
        out[j * RUNS : (j + 1) * RUNS, :] = part.astype(BF16)
    out[FLAT:, :] = own[FLAT:, :]


def project_part(coarse, vector, part, totals, first, begin, count):
    def body(layer, totals):
        totals = list(totals)
        base = pl.multiple_of((begin + layer) * WINDOW + part * PART, 128)
        row = (first + begin + layer) * 4
        wide = jnp.concatenate(
            [
                jnp.broadcast_to(vector[pl.ds(j * RUNS + row + m, 1), :], (8, COLS))
                for m in range(4)
                for j in range(5)
            ],
            axis=1,
        )
        for r in range(4):
            product = coarse[8 * r : 8 * r + 8, pl.ds(base, PART)].astype(F32) * wide
            for t in range(20):
                slot = 2 * r + t % 2
                totals[slot] = totals[slot] + product[:, t * COLS : (t + 1) * COLS]
        return tuple(totals)

    return lax.fori_loop(0, count, body, totals, unroll=5)


def early_kernel(source, out, arrived):
    copy = pltpu.make_async_copy(source.at[:, : EARLY * WINDOW], out, arrived)
    copy.start()
    copy.wait()


def load_kernel(
    source,
    early,
    own,
    basis,
    soil,
    frozen,
    table,
    late,
    begun,
    conduct,
    diagonal,
    above,
    local,
    gram,
    vector,
    ratio,
    value,
    arrived,
):
    copies = []
    for index in range((LAYERS - EARLY) // CHUNK):
        begin, size = index * CHUNK * WINDOW, CHUNK * WINDOW
        copies.append(
            pltpu.make_async_copy(
                source.at[:, EARLY * WINDOW + begin : EARLY * WINDOW + begin + size],
                late.at[:, begin : begin + size],
                arrived.at[index],
            )
        )
    for copy in copies:
        copy.start()
    columns_kernel(
        basis, soil, frozen, table, conduct, diagonal, above, local, gram, ratio, value
    )
    vector[...] = own[:FLAT, :].astype(F32)
    totals = (jnp.zeros((8, COLS), F32),) * 8
    totals = project_part(early, vector, 1, totals, 0, 0, EARLY)
    for index, copy in enumerate(copies):
        copy.wait()
        totals = project_part(late, vector, 1, totals, EARLY, index * CHUNK, CHUNK)
    for r in range(4):
        begun[8 * r : 8 * r + 8, :] = totals[2 * r] + totals[2 * r + 1]


def rhs_kernel(early, late, begun, before, after, count, out, vector):
    place = lax.axis_index("gx")
    last = lax.axis_size("gx") - 1
    zero = jnp.zeros((8, COLS), F32)
    totals = tuple(begun[4 * s : 4 * s + 8, :] if s % 2 == 0 else zero for s in range(8))
    vector[...] = jnp.where(place > 0, before[:FLAT, :].astype(F32), 0.0)
    totals = project_part(early, vector, 0, totals, 0, 0, EARLY)
    totals = project_part(late, vector, 0, totals, EARLY, 0, LAYERS - EARLY)
    vector[...] = jnp.where(place < last, after[:FLAT, :].astype(F32), 0.0)
    totals = project_part(early, vector, 2, totals, 0, 0, EARLY)
    totals = project_part(late, vector, 2, totals, EARLY, 0, LAYERS - EARLY)
    full = jnp.concatenate([totals[2 * r] + totals[2 * r + 1] for r in range(4)], axis=0)
    sums = jnp.sum(full, axis=1, keepdims=True)
    index = lax.broadcasted_iota(jnp.int32, (K, COLS), 0)
    keep = (lanes(K) % K == index) & (index < count[0, 0])
    row = jnp.sum(jnp.where(keep, sums, 0.0), axis=0, keepdims=True)
    out[...] = jnp.broadcast_to(row, out.shape)


def reduce_eight(parts, where):
    four, two, one = where

    def merge(a, b, mask, step):
        kept = jnp.where(mask, a, b)
        moved = jnp.where(mask, b, a)
        if step == 4:
            return kept + pltpu.roll(moved, 4, 0)
        return kept + jnp.where(mask, pltpu.roll(moved, 8 - step, 0), pltpu.roll(moved, step, 0))

    parts = [merge(parts[t], parts[t + 4], four, 4) for t in range(4)]
    parts = [merge(parts[t], parts[t + 2], two, 2) for t in range(2)]
    return merge(parts[0], parts[1], one, 1)


def reduction_masks():
    row = lax.broadcasted_iota(jnp.int32, (8, COLS), 0)
    return row < 4, row % 4 < 2, row % 2 < 1


def combine(coarse, base, width, weights):
    terms = [
        coarse[8 * r : 8 * r + 8, pl.ds(base, width)].astype(F32) * weights[r][:, :width]
        for r in range(4)
    ]
    return (terms[0] + terms[1]) + (terms[2] + terms[3])


def spread_part(coarse, weights, part, out, first, count):
    where = reduction_masks()

    def body(pair, carry):
        halves = []
        for half in range(2):
            base = pl.multiple_of((2 * pair + half) * WINDOW + part * PART, 128)
            halves.append(combine(coarse, base, PART, weights))
        for j in range(5):
            tiles = [
                halves[half][:, (5 * m + j) * COLS : (5 * m + j + 1) * COLS]
                for half in range(2)
                for m in range(4)
            ]
            start = pl.multiple_of(j * RUNS + 4 * first + 8 * pair, 8)
            out[pl.ds(start, 8), :] = reduce_eight(tiles, where)
        return carry

    lax.fori_loop(0, count // 2, body, 0, unroll=5)


def spread_ends(coarse, weights, out, first, count):
    where = reduction_masks()

    def body(pair, carry):
        tiles = []
        for half in range(2):
            base = (2 * pair + half) * WINDOW + PART
            for begin in (0, 18 * COLS):
                both = combine(coarse, pl.multiple_of(base + begin, 128), 2 * COLS, weights)
                tiles += [both[:, :COLS], both[:, COLS:]]
        start = pl.multiple_of(4 * first + 8 * pair, 8)
        out[pl.ds(start, 8), :] = reduce_eight(tiles, where)
        return carry

    lax.fori_loop(0, count // 2, body, 0, unroll=5)


def widen(weights):
    return [
        jnp.concatenate([weights[8 * r : 8 * r + 8, :]] * (PART // COLS), axis=1) for r in range(4)
    ]


def spread_kernel(
    early, late, inverse, gathered, count, local, weights, up, dn, up2, dn2, edge, rhs, low, high, ends
):
    at = lanes(K)
    rows = jnp.zeros((K, COLS), F32)
    for e in range(4):
        rows = jnp.where(at // K == e, gathered[pl.ds(e, K, stride=4), :], rows)
    rhs[...] = rows
    total = jnp.zeros((K, COLS), F32)
    for i in range(K):
        total = total + inverse[:, i * COLS : (i + 1) * COLS] * rhs[i : i + 1, :]
    solved = jnp.sum(total, axis=1, keepdims=True)
    index = lax.broadcasted_iota(jnp.int32, (K, COLS), 0)
    solved = jnp.where(index < count[0, 0], solved, 0.0).astype(BF16).astype(F32)
    weights[...] = solved
    wide = widen(solved)
    for coarse, first, size in ((early, 0, EARLY), (late, EARLY, LAYERS - EARLY)):
        spread_part(coarse, wide, 0, low, first, size)
        spread_part(coarse, wide, 2, high, first, size)
        spread_ends(coarse, wide, ends, first, size)
    at = lanes(LAYERS)

    def strip(ref, j, m):
        return ref[pl.ds(j * RUNS + m, LAYERS, stride=4), :]

    def both(first, second):
        return jnp.concatenate([first, second], axis=0)

    def put(ref, whole, ring):
        ref[:FLAT, :] = whole[...].astype(BF16)
        top = ring.astype(BF16)
        ref[FLAT : FLAT + 80, :] = top
        ref[FLAT + 80 :, :] = (ring - top.astype(F32)).astype(BF16)

    def end(index):
        return ends[pl.ds(index, LAYERS, stride=4), :]

    last = strip(local, 3, 3)
    put(
        up,
        high,
        both(
            end(2) + jnp.where(at >= 112, last, 0.0),
            end(3) + jnp.where(at < 112, last, 0.0),
        ),
    )
    first = strip(local, 0, 0)
    put(
        dn,
        low,
        both(
            end(0) + jnp.where(at >= 16, first, 0.0),
            end(1) + jnp.where(at < 16, first, 0.0),
        ),
    )
    up2[...] = both(strip(high, 3, 3), strip(high, 4, 3)).astype(BF16)
    dn2[...] = both(strip(low, 0, 0), strip(low, 1, 0)).astype(BF16)
    edge[:80, :] = both(strip(low, 3, 3), strip(low, 4, 3))
    edge[80:, :] = both(strip(high, 0, 0), strip(high, 1, 0))


def own_spread_kernel(early, late, weights, own):
    wide = widen(weights[...])
    spread_part(early, wide, 1, own, 0, EARLY)
    spread_part(late, wide, 1, own, EARLY, LAYERS - EARLY)


def fold_rows_kernel(own, edge, local, before, after, before2, after2, field, rim, up, dn):
    place = lax.axis_index("gx")
    last = lax.axis_size("gx") - 1
    at = lanes(RUNS)
    whole = []
    for j in range(5):
        cut = slice(j * RUNS, (j + 1) * RUNS)
        part = (
            own[cut, :]
            + jnp.where(place > 0, before[cut, :].astype(F32), 0.0)
            + jnp.where(place < last, after[cut, :].astype(F32), 0.0)
        )
        if j < 4:
            part = part + jnp.where(at >= 32 * j + 16, local[cut, :], 0.0)
        if j > 0:
            behind = local[(j - 1) * RUNS : j * RUNS, :]
            part = part + jnp.where(at < 32 * j - 16, behind, 0.0)
        whole.append(part)
    to_up = jnp.zeros((RUNS, COLS), F32)
    to_dn = to_up
    for q in range(4):
        field[q * RUNS : (q + 1) * RUNS, :] = jnp.where(
            at >= 32 * q + 16, whole[q], whole[q + 1]
        )
        band = (at >= 32 * q) & (at < 32 * q + 32)
        to_up = jnp.where(band, whole[q + 1], to_up)
        to_dn = jnp.where(band, whole[q], to_dn)
    up[:RUNS, :] = to_up
    dn[:RUNS, :] = to_dn

    def ring(ours, near, far, valid):
        return (
            ours
            + near[FLAT : FLAT + 80, :].astype(F32)
            + near[FLAT + 80 :, :].astype(F32)
            + jnp.where(valid, far[...].astype(F32), 0.0)
        )

    top = ring(edge[:80, :], before, before2, place > 1)
    bottom = ring(edge[80:, :], after, after2, place < last - 1)
    at = lanes(LAYERS)
    half = LAYERS
    rim[:half, :] = jnp.where(at >= 112, top[:half], top[half:])
    rim[half:, :] = jnp.where(at >= 16, bottom[:half], bottom[half:])
    up[RUNS:, :] = jnp.where(at >= 96, top[half:], bottom[half:])
    dn[RUNS:, :] = jnp.where(at >= 96, top[:half], bottom[:half])


def look_up(kind, table, rows):
    value = jnp.zeros(kind.shape, F32)
    for index in range(8):
        value = jnp.where(kind == index, table[rows[0], index], value)
        value = jnp.where(kind == index + 8, table[rows[1], index], value)
    return value


def columns_kernel(basis, soil, frozen, table, conduct, diagonal, above, local, gram, ratio, value):
    kind = soil[...] + 8 * frozen[...]
    conduct[...] = look_up(kind, table, (0, 1))
    diagonal[...] = look_up(kind, table, (2, 3))
    zero = jnp.zeros((ROWS, COLS), F32)
    grams = [jnp.zeros((8, COLS), F32) for _ in range(10)]
    below = zero
    last_ratio = zero
    last_value = zero
    for level in range(LAYERS):
        cut = slice(level * ROWS, (level + 1) * ROWS)
        own = conduct[cut, :]
        over = zero
        if level < LAYERS - 1:
            over = WEIGHT_V * harmonic(own, conduct[(level + 1) * ROWS : (level + 2) * ROWS, :])
        above[cut, :] = over
        sides = diagonal[cut, :] + below + over
        diagonal[cut, :] = sides
        denom = sides + 4.0 * WEIGHT_H * own + below * last_ratio
        inverse = 1.0 / denom
        last_ratio = -over * inverse
        last_value = (basis[3, cut, :] + below * last_value) * inverse
        ratio[cut, :] = last_ratio
        value[cut, :] = last_value
        below = over
        vectors = [basis[j, cut, :] for j in range(4)]
        slot = 0
        for i in range(4):
            for j in range(i, 4):
                square = vectors[i] * vectors[j]
                grams[slot] = grams[slot] + (square[:8] + square[8:])
                slot += 1
    for level in range(LAYERS - 2, -1, -1):
        cut = slice(level * ROWS, (level + 1) * ROWS)
        last_value = value[cut, :] - ratio[cut, :] * last_value
        value[cut, :] = last_value
    for q in range(4):
        local[q * RUNS : (q + 1) * RUNS, :] = turn(value[pl.ds(q, RUNS, stride=4), :], 32 * q + 16)
    for slot in range(10):
        gram[8 * slot : 8 * slot + 8, :] = grams[slot]


def faces_kernel(conduct, diagonal, table, left, right, before, after, faces, total, side):
    gx, gy = lax.axis_index("gx"), lax.axis_index("gy")
    last_x, last_y = lax.axis_size("gx") - 1, lax.axis_size("gy") - 1
    at = lanes(RUNS)
    from_left, from_right = left[...].astype(F32), right[...].astype(F32)
    kinds = jnp.zeros((RUNS, COLS), F32)
    for q in range(4):
        kinds = jnp.where(at == 32 * q + 16, from_left, kinds)
        kinds = jnp.where(at == 32 * q + 15, from_right, kinds)
    known = look_up(kinds.astype(jnp.int32), table, (0, 1))
    for q in range(4):
        side[pl.ds(q, RUNS, stride=4), :] = turn(known, -(32 * q + 16))
    row_before = look_up(before[FLAT:, :].astype(F32).astype(jnp.int32), table, (0, 1))
    row_after = look_up(after[FLAT:, :].astype(F32).astype(jnp.int32), table, (0, 1))
    at = lanes(ROWS)
    row = lax.broadcasted_iota(jnp.int32, (ROWS, COLS), 0)
    for level in range(LAYERS):
        cut = slice(level * ROWS, (level + 1) * ROWS)
        own = conduct[cut, :]
        aside = side[cut, :]
        over = row_before[LAYERS + level : LAYERS + level + 1, :]
        under = row_after[level : level + 1, :]
        weights = [
            jnp.where((at > 0) | (gy > 0), harmonic(own, jnp.where(at == 0, aside, turn(own, 1))), 0.0),
            jnp.where(
                (at < COLS - 1) | (gy < last_y),
                harmonic(own, jnp.where(at == COLS - 1, aside, turn(own, -1))),
                0.0,
            ),
            jnp.where(
                (row > 0) | (gx > 0),
                harmonic(own, jnp.where(row == 0, over, pltpu.roll(own, 1, 0))),
                0.0,
            ),
            jnp.where(
                (row < ROWS - 1) | (gx < last_x),
                harmonic(own, jnp.where(row == ROWS - 1, under, pltpu.roll(own, ROWS - 1, 0))),
                0.0,
            ),
        ]
        for index in range(4):
            faces[index, cut, :] = WEIGHT_H * weights[index]
        total[cut, :] = diagonal[cut, :] + WEIGHT_H * (
            (weights[0] + weights[1]) + (weights[2] + weights[3])
        )


def image_kernel(
    field, rim, up, dn, left, right, basis, faces, total, above, gram, precond, image, sums, side
):
    gy = lax.axis_index("gy")
    last_y = lax.axis_size("gy") - 1
    at = lanes(RUNS)
    from_left = jnp.where(gy > 0, left[...], 0.0)
    from_right = jnp.where(gy < last_y, right[...], 0.0)
    to_left = dn[...] + from_left
    to_right = up[...] + from_right
    for q in range(4):
        cut = 32 * q + 16
        turned = field[q * RUNS : (q + 1) * RUNS, :]
        turned = turned + jnp.where((at >= cut) & (at < cut + 16), from_left[:RUNS], 0.0)
        turned = turned + jnp.where((at >= cut - 16) & (at < cut), from_right[:RUNS], 0.0)
        precond[pl.ds(q, RUNS, stride=4), :] = turn(turned, -cut)
        edges = jnp.where(at == cut - 1, to_left[:RUNS], to_right[:RUNS])
        side[pl.ds(q, RUNS, stride=4), :] = turn(edges, -cut)
    at = lanes(LAYERS)
    rim_left, rim_right = from_left[RUNS:], from_right[RUNS:]
    over = rim[:LAYERS, :]
    over = over + jnp.where(at >= 112, rim_left, 0.0)
    over = turn(over + jnp.where((at >= 96) & (at < 112), rim_right, 0.0), -112)
    under = rim[LAYERS:, :]
    under = under + jnp.where((at >= 16) & (at < 32), rim_left, 0.0)
    under = turn(under + jnp.where(at < 16, rim_right, 0.0), -16)
    at = lanes(ROWS)
    row = lax.broadcasted_iota(jnp.int32, (ROWS, COLS), 0)
    totals = [jnp.zeros((8, COLS), F32) for _ in range(5)]
    for level in range(LAYERS):
        cut = slice(level * ROWS, (level + 1) * ROWS)
        own = precond[cut, :]
        aside = side[cut, :]
        result = total[cut, :] * own
        result = result - faces[0, cut, :] * jnp.where(at == 0, turn(aside, 1), turn(own, 1))
        result = result - faces[1, cut, :] * jnp.where(
            at == COLS - 1, turn(aside, -1), turn(own, -1)
        )
        result = result - faces[2, cut, :] * jnp.where(
            row == 0, over[level : level + 1, :], pltpu.roll(own, 1, 0)
        )
        result = result - faces[3, cut, :] * jnp.where(
            row == ROWS - 1, under[level : level + 1, :], pltpu.roll(own, ROWS - 1, 0)
        )
        if level > 0:
            back = slice((level - 1) * ROWS, level * ROWS)
            result = result - above[back, :] * precond[back, :]
        if level < LAYERS - 1:
            ahead = slice((level + 1) * ROWS, (level + 2) * ROWS)
            result = result - above[cut, :] * precond[ahead, :]
        image[cut, :] = result
        for j in range(5):
            product = (basis[j, cut, :] if j < 4 else result) * result
            totals[j] = totals[j] + (product[:8] + product[8:])
    totals += [gram[8 * slot : 8 * slot + 8, :] for slot in range(10)]
    totals.append(jnp.zeros((8, COLS), F32))
    rows = jnp.concatenate([jnp.sum(part, axis=0, keepdims=True) for part in totals], axis=0)
    column = jnp.sum(rows, axis=1, keepdims=True)
    keep = lanes(ROWS) == lax.broadcasted_iota(jnp.int32, (ROWS, COLS), 0)
    line = jnp.sum(jnp.where(keep, column, 0.0), axis=0, keepdims=True)
    sums[...] = jnp.broadcast_to(line, sums.shape)


def next_kernel(gathered, image, basis, out, hessenberg):
    cells = float(CELLS * COLS * lax.axis_size("gx") * lax.axis_size("gy"))
    line = jnp.sum(gathered[...], axis=0, keepdims=True) / cells
    entry = [line[:, i : i + 1] for i in range(15)]
    project = entry[:4]
    square = entry[4]
    for j in range(4):
        square = square - 2.0 * project[j] * project[j]
    slot = 5
    for i in range(4):
        for j in range(i, 4):
            square = square + (1.0 if i == j else 2.0) * project[i] * project[j] * entry[slot]
            slot += 1
    length = jnp.sqrt(jnp.maximum(square, 0.0) + EPS)
    at = lanes(1)
    found = jnp.where(at == 4, length, jnp.where(at < 4, line, 0.0))
    for i in range(5):
        hessenberg[i] = found[0, i]
    inverse = 1.0 / length
    scaled = [project[j] * inverse for j in range(4)]
    for level in range(LAYERS):
        cut = slice(level * ROWS, (level + 1) * ROWS)
        value = image[cut, :] * inverse
        for j in range(4):
            value = value - scaled[j] * basis[j, cut, :]
        out[cut, :] = value


def shift(values, axis, step):
    count = lax.axis_size(axis)
    return lax.ppermute(values, axis, [(i, (i + step) % count) for i in range(count)])


def exchange(lines):
    size = lines.shape[0]
    out = lax.all_to_all(lines.reshape(size, 1, COLS), ("gx", "gy"), 0, 0)
    return out.reshape(size, COLS)


def on_device(basis, soil, frozen, soil_table, coarse_basis, coarse_inverse, active_count):
    basis = basis.reshape(4, CELLS, COLS)
    soil, frozen = soil.reshape(CELLS, COLS), frozen.reshape(CELLS, COLS)
    source = pltpu.with_memory_space_constraint(coarse_basis.reshape(K, -1), pltpu.HBM)
    devices = lax.axis_size("gx") * lax.axis_size("gy")
    field_space = pltpu.VMEM((CELLS, COLS), F32)
    kinds = pltpu.VMEM((CELLS, COLS), jnp.int32)
    up, dn, flat = call(
        pack_kernel,
        [
            shape(RUNS, COLS, dtype=BF16),
            shape(RUNS, COLS, dtype=BF16),
            shape(FLAT + 80, COLS, dtype=BF16),
        ],
        [HB] * 3,
        [pltpu.with_memory_space_constraint(x, pltpu.HBM) for x in (basis, soil, frozen)],
        [field_space, kinds, kinds, field_space, pltpu.SemaphoreType.DMA((3,))],
        name="pack",
    )
    left, right = shift(up, "gy", 1), shift(dn, "gy", -1)
    early = call(
        early_kernel,
        pltpu.VMEM((K, EARLY * WINDOW), BF16),
        [HB],
        (source,),
        [pltpu.SemaphoreType.DMA],
        out_specs=VM,
        moved=10_000_000,
        name="early",
    )
    early, flat = lax.optimization_barrier((early, flat))
    flat = call(
        flat_kernel, shape(FLAT + 80, COLS, dtype=BF16), [VM] * 3, (flat, left, right), name="flat"
    )
    before, after = shift(flat, "gx", 1), shift(flat, "gx", -1)
    late, begun, conduct, diagonal, above, local, gram = call(
        load_kernel,
        [pltpu.VMEM((K, (LAYERS - EARLY) * WINDOW), BF16), shape(K, COLS)]
        + [shape(CELLS, COLS)] * 4
        + [shape(80, COLS)],
        [HB] + [VM] * 5 + [SM],
        (source, early, flat, basis, soil, frozen, soil_table),
        [
            pltpu.VMEM((FLAT, COLS), F32),
            field_space,
            field_space,
            pltpu.SemaphoreType.DMA(((LAYERS - EARLY) // CHUNK,)),
        ],
        out_specs=[VM] * 7,
        flops=16_000_000,
        moved=20_000_000,
        name="load",
    )
    lines = call(
        rhs_kernel,
        shape(devices, COLS),
        [VM] * 5 + [SM],
        (early, late, begun, before, after, active_count),
        [pltpu.VMEM((FLAT, COLS), F32)],
        flops=12_000_000,
        moved=12_000_000,
        name="rhs",
    )
    gathered = exchange(lines)
    message = shape(FLAT + 160, COLS, dtype=BF16)
    small = shape(80, COLS, dtype=BF16)
    weights, up, dn, up2, dn2, edge = call(
        spread_kernel,
        [shape(K, COLS), message, message, small, small, shape(160, COLS)],
        [VM, VM, VM, VM, SM, VM],
        (early, late, coarse_inverse, gathered, active_count, local),
        [
            pltpu.VMEM((K, COLS), F32),
            pltpu.VMEM((FLAT, COLS), F32),
            pltpu.VMEM((FLAT, COLS), F32),
            pltpu.VMEM((RUNS, COLS), F32),
        ],
        flops=40_000_000,
        moved=20_000_000,
        name="spread",
    )
    near = shift(up, "gx", 1), shift(dn, "gx", -1)
    far = shift(up2, "gx", 2), shift(dn2, "gx", -2)
    own = call(
        own_spread_kernel,
        shape(FLAT, COLS),
        [VM] * 3,
        (early, late, weights),
        flops=20_000_000,
        moved=7_000_000,
        name="own_spread",
    )
    conduct, diagonal, weights = lax.optimization_barrier((conduct, diagonal, weights))
    faces, total = call(
        faces_kernel,
        [shape(4, CELLS, COLS), shape(CELLS, COLS)],
        [VM, VM, SM, VM, VM, VM, VM],
        (conduct, diagonal, soil_table, left, right, before, after),
        [field_space],
        flops=4_000_000,
        moved=2_000_000,
        name="faces",
    )
    field, rim, up, dn = call(
        fold_rows_kernel,
        [shape(CELLS, COLS), shape(80, COLS), shape(RUNS + LAYERS, COLS), shape(RUNS + LAYERS, COLS)],
        [VM] * 7,
        (own, edge, local, *near, *far),
        name="fold_rows",
    )
    left, right = shift(up, "gy", 1), shift(dn, "gy", -1)
    precond, image, sums = call(
        image_kernel,
        [shape(CELLS, COLS), shape(CELLS, COLS), shape(devices, COLS)],
        [VM] * 11,
        (field, rim, up, dn, left, right, basis, faces, total, above, gram),
        [field_space],
        name="image",
    )
    gathered = exchange(sums)
    following, hessenberg = call(
        next_kernel,
        [shape(CELLS, COLS), shape(5)],
        [VM] * 3,
        (gathered, image, basis),
        out_specs=[VM, SM],
        name="next",
    )
    tile = (LAYERS, ROWS, COLS)
    return precond.reshape(tile), following.reshape(tile), hessenberg


def solution(mesh):
    placed = (
        P(None, None, "gx", "gy"),
        P(None, "gx", "gy"),
        P(None, "gx", "gy"),
        P(),
        P("gx", "gy", None, None),
        P(("gx", "gy"), None),
        P("gx", "gy"),
    )
    return jax.shard_map(
        on_device,
        mesh=mesh,
        in_specs=placed,
        out_specs=(P(None, "gx", "gy"), P(None, "gx", "gy"), P()),
        check_vma=False,
    )
```

```python
import functools

import jax
import jax.numpy as jnp
from jax import lax
from jax.experimental import pallas as pl
from jax.experimental.pallas import tpu as pltpu
from jax.sharding import PartitionSpec as P

F32 = jnp.float32
BF16 = jnp.bfloat16

LAYERS, ROWS, COLS, OV, K = 40, 16, 128, 16, 32
CELLS = LAYERS * ROWS
RUNS = CELLS // 4
FLAT = 5 * RUNS
WINDOW = 7680
EARLY = 12
CHUNK = 14
PAD = FLAT + 48
SIDE = RUNS + 48
ENDS = FLAT + 80
PART = 2560
WEIGHT_V, WEIGHT_H, EPS = 4.0, 1.0, 1e-06

VM = pl.BlockSpec(memory_space=pltpu.VMEM)
SM = pl.BlockSpec(memory_space=pltpu.SMEM)
HB = pl.BlockSpec(memory_space=pltpu.HBM)


def shape(*dims, dtype=F32):
    return jax.ShapeDtypeStruct(dims, dtype)


def call(kernel, outs, specs, args, scratch=(), out_specs=None, flops=0, moved=0, name=None):
    return pl.pallas_call(
        kernel,
        out_shape=outs,
        in_specs=specs,
        out_specs=out_specs if out_specs is not None else jax.tree.map(lambda _: VM, outs),
        scratch_shapes=list(scratch),
        compiler_params=pltpu.CompilerParams(vmem_limit_bytes=16 * 2**20),
        cost_estimate=pl.CostEstimate(flops=flops, bytes_accessed=moved, transcendentals=0),
        name=name,
    )(*args)


def lanes(rows):
    return lax.broadcasted_iota(jnp.int32, (rows, COLS), 1)


def harmonic(first, second):
    return 2.0 * first * second / (first + second)


def steps(count):
    return max(n for n in range(1, 8) if count % n == 0)


def turn(values, amount):
    return pltpu.roll(values, amount % COLS, 1)


def pack_kernel(
    basis_in,
    soil_in,
    frozen_in,
    first,
    second,
    flat,
    kinds,
    basis,
    code,
    soil,
    frozen,
    arrived,
):
    copies = [
        pltpu.make_async_copy(basis_in.at[3], basis, arrived.at[0]),
        pltpu.make_async_copy(soil_in, soil, arrived.at[1]),
        pltpu.make_async_copy(frozen_in, frozen, arrived.at[2]),
    ]
    for copy in copies:
        copy.start()
    for copy in copies:
        copy.wait()
    code[...] = (soil[...] + 8 * frozen[...]).astype(F32)
    at = lanes(RUNS)
    to_up = jnp.zeros((RUNS, COLS), F32)
    to_dn = to_up
    flats = [jnp.zeros((RUNS, COLS), F32) for _ in range(5)]
    for q in range(4):
        cut = 32 * q + 16
        turned = turn(basis[pl.ds(q, RUNS, stride=4), :], cut)
        kind = code[pl.ds(q, RUNS, stride=4), :]
        low = (at >= cut - 16) & (at < cut)
        high = (at >= cut) & (at < cut + 16)
        to_up = jnp.where(low, turned, jnp.where(at == cut, turn(kind, cut + 1), to_up))
        to_dn = jnp.where(high, turned, jnp.where(at == cut - 1, turn(kind, cut - 1), to_dn))
        flats[q] = jnp.where(at >= cut, turned, flats[q])
        flats[q + 1] = jnp.where(at < cut, turned, flats[q + 1])
    even = lax.axis_index("gy") % 2 == 0
    first[...] = jnp.where(even, to_up, to_dn).astype(BF16)
    second[...] = jnp.where(even, to_dn, to_up).astype(BF16)
    for j in range(5):
        flat[j * RUNS : (j + 1) * RUNS, :] = flats[j].astype(BF16)
    spare = jnp.zeros((PAD - FLAT - LAYERS, COLS), F32)
    for index, row in enumerate((0, ROWS - 1)):
        line = jnp.concatenate([code[pl.ds(row, LAYERS, stride=ROWS), :], spare], axis=0)
        kinds[index] = line


def sides(even, first, second):
    return jnp.where(even, second, first), jnp.where(even, first, second)


def flat_kernel(own, kinds, from_first, from_second, first, second):
    place = lax.axis_index("gy")
    last = lax.axis_size("gy") - 1
    at = lanes(RUNS)
    from_left, from_right = sides(
        place % 2 == 0, from_first[...].astype(F32), from_second[...].astype(F32)
    )
    from_left = jnp.where(place > 0, from_left, 0.0)
    from_right = jnp.where(place < last, from_right, 0.0)
    for j in range(5):
        part = own[j * RUNS : (j + 1) * RUNS, :].astype(F32)
        if j < 4:
            part = jnp.where((at >= 32 * j) & (at < 32 * j + 16), from_left, part)
        if j > 0:
            part = jnp.where((at >= 32 * j - 16) & (at < 32 * j), from_right, part)
        first[j * RUNS : (j + 1) * RUNS, :] = part.astype(BF16)
        second[j * RUNS : (j + 1) * RUNS, :] = part.astype(BF16)
    even = lax.axis_index("gx") % 2 == 0
    first[FLAT:, :] = jnp.where(even, kinds[1], kinds[0]).astype(BF16)
    second[FLAT:, :] = jnp.where(even, kinds[0], kinds[1]).astype(BF16)


def project_part(coarse, vector, part, totals, first, begin, count):
    def body(layer, totals):
        totals = list(totals)
        base = pl.multiple_of((begin + layer) * WINDOW + part * PART, 128)
        row = (first + begin + layer) * 4
        wide = jnp.concatenate(
            [
                jnp.broadcast_to(vector[pl.ds(j * RUNS + row + m, 1), :], (8, COLS))
                for m in range(4)
                for j in range(5)
            ],
            axis=1,
        )
        for r in range(4):
            product = coarse[8 * r : 8 * r + 8, pl.ds(base, PART)].astype(F32) * wide
            for t in range(20):
                slot = 2 * r + t % 2
                totals[slot] = totals[slot] + product[:, t * COLS : (t + 1) * COLS]
        return tuple(totals)

    return lax.fori_loop(0, count, body, totals, unroll=steps(count))


def early_kernel(
    source,
    table_in,
    basis,
    code,
    out,
    conduct,
    diagonal,
    above,
    local,
    ratio,
    value,
    table,
    arrived,
):
    small = pltpu.make_async_copy(table_in, table, arrived.at[0])
    small.start()
    copy = pltpu.make_async_copy(source.at[:, : EARLY * WINDOW], out, arrived.at[1])
    copy.start()
    small.wait()
    solve_columns(basis, code, table, conduct, diagonal, above, local, ratio, value)
    copy.wait()


def multiply_out(basis, gram):
    def body(level, grams):
        grams = list(grams)
        cut = pl.ds(pl.multiple_of(level * ROWS, ROWS), ROWS)
        vectors = [basis[j, cut, :] for j in range(4)]
        slot = 0
        for i in range(4):
            for j in range(i, 4):
                square = vectors[i] * vectors[j]
                grams[slot] = grams[slot] + (square[:8] + square[8:])
                slot += 1
        return tuple(grams)

    zero = jnp.zeros((8, COLS), F32)
    grams = lax.fori_loop(0, LAYERS, body, (zero,) * 10, unroll=4)
    for slot in range(10):
        gram[8 * slot : 8 * slot + 8, :] = grams[slot]


def load_kernel(source, basis_in, early, own, late, basis, begun, gram, vector, arrived):
    ready = pltpu.make_async_copy(basis_in, basis, arrived.at[0])
    ready.start()
    copies = []
    for index in range((LAYERS - EARLY) // CHUNK):
        begin, size = index * CHUNK * WINDOW, CHUNK * WINDOW
        copies.append(
            pltpu.make_async_copy(
                source.at[:, EARLY * WINDOW + begin : EARLY * WINDOW + begin + size],
                late.at[:, begin : begin + size],
                arrived.at[index + 1],
            )
        )
    for copy in copies:
        copy.start()
    vector[...] = own[:FLAT, :].astype(F32)
    totals = (jnp.zeros((8, COLS), F32),) * 8
    totals = project_part(early, vector, 1, totals, 0, 0, EARLY)
    ready.wait()
    multiply_out(basis, gram)
    for index, copy in enumerate(copies):
        copy.wait()
        totals = project_part(late, vector, 1, totals, EARLY, index * CHUNK, CHUNK)
    for r in range(4):
        begun[8 * r : 8 * r + 8, :] = totals[2 * r] + totals[2 * r + 1]


def project_neighbour(early, late, whole, vector, upper, valid, totals):
    vector[...] = jnp.where(valid, whole[:FLAT, :].astype(F32), 0.0)
    part = jnp.where(upper, 2, 0)
    totals = project_part(early, vector, part, totals, 0, 0, EARLY)
    return project_part(late, vector, part, totals, EARLY, 0, LAYERS - EARLY)


def unfold(begun):
    zero = jnp.zeros((8, COLS), F32)
    return tuple(begun[4 * s : 4 * s + 8, :] if s % 2 == 0 else zero for s in range(8))


def first_rhs_kernel(early, late, begun, whole, out, vector):
    upper = lax.axis_index("gx") % 2 == 0
    totals = project_neighbour(early, late, whole, vector, upper, True, unfold(begun))
    for r in range(4):
        out[8 * r : 8 * r + 8, :] = totals[2 * r] + totals[2 * r + 1]


def second_rhs_kernel(early, late, begun, whole, count, out, vector):
    place = lax.axis_index("gx")
    valid = (place > 0) & (place < lax.axis_size("gx") - 1)
    totals = project_neighbour(early, late, whole, vector, place % 2 == 1, valid, unfold(begun))
    full = jnp.concatenate([totals[2 * r] + totals[2 * r + 1] for r in range(4)], axis=0)
    sums = jnp.sum(full, axis=1, keepdims=True)
    index = lax.broadcasted_iota(jnp.int32, (K, COLS), 0)
    keep = (lanes(K) % K == index) & (index < count[...])
    row = jnp.sum(jnp.where(keep, sums, 0.0), axis=0, keepdims=True)
    out[...] = jnp.broadcast_to(row, out.shape)


def reduce_eight(parts, where):
    four, two, one = where

    def merge(a, b, mask, step):
        kept = jnp.where(mask, a, b)
        moved = jnp.where(mask, b, a)
        if step == 4:
            return kept + pltpu.roll(moved, 4, 0)
        return kept + jnp.where(mask, pltpu.roll(moved, 8 - step, 0), pltpu.roll(moved, step, 0))

    parts = [merge(parts[t], parts[t + 4], four, 4) for t in range(4)]
    parts = [merge(parts[t], parts[t + 2], two, 2) for t in range(2)]
    return merge(parts[0], parts[1], one, 1)


def reduction_masks():
    row = lax.broadcasted_iota(jnp.int32, (8, COLS), 0)
    return row < 4, row % 4 < 2, row % 2 < 1


def combine(coarse, base, width, weights):
    terms = [
        coarse[8 * r : 8 * r + 8, pl.ds(base, width)].astype(F32) * weights[r][:, :width]
        for r in range(4)
    ]
    return (terms[0] + terms[1]) + (terms[2] + terms[3])


def spread_part(coarse, weights, part, out, first, count):
    where = reduction_masks()

    def body(pair, carry):
        halves = []
        for half in range(2):
            base = pl.multiple_of((2 * pair + half) * WINDOW + part * PART, 128)
            halves.append(combine(coarse, base, PART, weights))
        for j in range(5):
            tiles = [
                halves[half][:, (5 * m + j) * COLS : (5 * m + j + 1) * COLS]
                for half in range(2)
                for m in range(4)
            ]
            start = pl.multiple_of(j * RUNS + 4 * first + 8 * pair, 8)
            out[pl.ds(start, 8), :] = reduce_eight(tiles, where)
        return carry

    lax.fori_loop(0, count // 2, body, 0, unroll=steps(count // 2))


def spread_ends(coarse, weights, begin, out, first, count):
    where = reduction_masks()

    def body(four, carry):
        tiles = []
        for layer in range(4):
            base = (4 * four + layer) * WINDOW + PART + begin
            both = combine(coarse, pl.multiple_of(base, 128), 2 * COLS, weights)
            tiles += [both[:, :COLS], both[:, COLS:]]
        start = pl.multiple_of(2 * first + 8 * four, 8)
        out[pl.ds(start, 8), :] = reduce_eight(tiles, where)
        return carry

    lax.fori_loop(0, count // 4, body, 0, unroll=steps(count // 4))


def widen(weights):
    return [
        jnp.concatenate([weights[8 * r : 8 * r + 8, :]] * (PART // COLS), axis=1) for r in range(4)
    ]


def solve(inverse, gathered, count, rhs):
    at = lanes(K)
    rows = jnp.zeros((K, COLS), F32)
    for e in range(4):
        rows = jnp.where(at // K == e, gathered[pl.ds(e, K, stride=4), :], rows)
    rhs[...] = rows
    total = jnp.zeros((K, COLS), F32)
    for i in range(K):
        total = total + inverse[:, i * COLS : (i + 1) * COLS] * rhs[i : i + 1, :]
    solved = jnp.sum(total, axis=1, keepdims=True)
    index = lax.broadcasted_iota(jnp.int32, (K, COLS), 0)
    return jnp.where(index < count[...], solved, 0.0).astype(BF16).astype(F32)


def spread_to(upper, early, late, solved, local, message, near, whole, ends):
    wide = widen(solved)
    part, begin = jnp.where(upper, 2, 0), jnp.where(upper, 18 * COLS, 0)
    for coarse, start, size in ((early, 0, EARLY), (late, EARLY, LAYERS - EARLY)):
        spread_part(coarse, wide, part, whole, start, size)
        spread_ends(coarse, wide, begin, ends, start, size)
    message[:FLAT, :] = whole[...].astype(BF16)

    def strip(ref, j, m):
        return ref[pl.ds(j * RUNS + m, LAYERS, stride=4), :]

    def both(first, second):
        return jnp.concatenate([first, second], axis=0)

    at = lanes(LAYERS)
    cut = jnp.where(upper, 112, 16)
    row = jnp.where(upper, strip(local, 3, 3), strip(local, 0, 0))
    ours = [ends[pl.ds(index, LAYERS, stride=2), :] for index in range(2)]
    message[FLAT:, :] = both(
        ours[0] + jnp.where(at >= cut, row, 0.0), ours[1] + jnp.where(at < cut, row, 0.0)
    ).astype(BF16)
    top = both(strip(whole, 0, 0), strip(whole, 1, 0))
    bottom = both(strip(whole, 3, 3), strip(whole, 4, 3))
    near[...] = jnp.where(upper, top, bottom)
    return jnp.where(upper, bottom, top)


def second_spread_kernel(
    early, late, inverse, gathered, count, local, weights, message, near, far, rhs, whole, ends
):
    solved = solve(inverse, gathered, count, rhs)
    weights[...] = solved
    upper = lax.axis_index("gx") % 2 == 1
    far[...] = spread_to(upper, early, late, solved, local, message, near, whole, ends)


def first_spread_kernel(
    early, late, weights, local, far, message, near, far_first, far_second, whole, ends
):
    place = lax.axis_index("gx")
    upper = place % 2 == 0
    own = spread_to(upper, early, late, weights[...], local, message, near, whole, ends)
    swapped = (place % 4 == 1) | (place % 4 == 2)
    far_first[...] = jnp.where(swapped, far[...], own).astype(BF16)
    far_second[...] = jnp.where(swapped, own, far[...]).astype(BF16)


def own_spread_kernel(early, late, weights, own):
    wide = widen(weights[...])
    spread_part(early, wide, 1, own, 0, EARLY)
    spread_part(late, wide, 1, own, EARLY, LAYERS - EARLY)


def fold_rows_kernel(
    own,
    near_first,
    near_second,
    local,
    from_first,
    from_second,
    far_first,
    far_second,
    field,
    rim,
    up,
    dn,
    first,
    second,
):
    place = lax.axis_index("gx")
    last = lax.axis_size("gx") - 1
    even, lower = place % 2 == 0, place % 4 < 2
    at = lanes(RUNS)
    whole = []
    for j in range(5):
        cut = slice(j * RUNS, (j + 1) * RUNS)
        before, after = sides(even, from_first[cut, :].astype(F32), from_second[cut, :].astype(F32))
        part = own[cut, :] + jnp.where(place > 0, before, 0.0)
        part = part + jnp.where(place < last, after, 0.0)
        if j < 4:
            part = part + jnp.where(at >= 32 * j + 16, local[cut, :], 0.0)
        if j > 0:
            behind = local[(j - 1) * RUNS : j * RUNS, :]
            part = part + jnp.where(at < 32 * j - 16, behind, 0.0)
        whole.append(part)
    to_up = jnp.zeros((RUNS, COLS), F32)
    to_dn = to_up
    for q in range(4):
        field[q * RUNS : (q + 1) * RUNS, :] = jnp.where(
            at >= 32 * q + 16, whole[q], whole[q + 1]
        )
        band = (at >= 32 * q) & (at < 32 * q + 32)
        to_up = jnp.where(band, whole[q + 1], to_up)
        to_dn = jnp.where(band, whole[q], to_dn)
    up[:RUNS, :] = to_up
    dn[:RUNS, :] = to_dn

    before, after = sides(even, from_first[FLAT:, :].astype(F32), from_second[FLAT:, :].astype(F32))
    before2, after2 = sides(lower, far_first[...].astype(F32), far_second[...].astype(F32))
    near_before, near_after = sides(even, near_first[...], near_second[...])
    top = near_before + before + jnp.where(place > 1, before2, 0.0)
    bottom = near_after + after + jnp.where(place < last - 1, after2, 0.0)
    at = lanes(LAYERS)
    half = LAYERS
    rim[:half, :] = jnp.where(at >= 112, top[:half], top[half:])
    rim[half:, :] = jnp.where(at >= 16, bottom[:half], bottom[half:])
    up[RUNS:, :] = jnp.where(at >= 96, top[half:], bottom[half:])
    dn[RUNS:, :] = jnp.where(at >= 96, top[:half], bottom[:half])
    even = lax.axis_index("gy") % 2 == 0
    spare = jnp.zeros((SIDE - RUNS - LAYERS, COLS), F32)
    to_up = jnp.concatenate([up[...], spare], axis=0)
    to_dn = jnp.concatenate([dn[...], spare], axis=0)
    first[...] = jnp.where(even, to_up, to_dn).astype(BF16)
    second[...] = jnp.where(even, to_dn, to_up).astype(BF16)


def look_up(kind, table, rows):
    value = jnp.zeros(kind.shape, F32)
    for index in range(8):
        value = jnp.where(kind == index, table[rows[0], index], value)
        value = jnp.where(kind == index + 8, table[rows[1], index], value)
    return value


def solve_columns(basis, code, table, conduct, diagonal, above, local, ratio, value):
    def body(index, carry):
        cut = pl.ds(pl.multiple_of(index * 64, 64), 64)
        kind = code[cut, :]
        conduct[cut, :] = look_up(kind, table, (0, 1))
        diagonal[cut, :] = look_up(kind, table, (2, 3))
        return carry

    lax.fori_loop(0, CELLS // 64, body, 0)
    zero = jnp.zeros((ROWS, COLS), F32)
    below = zero
    last_ratio = zero
    last_value = zero
    for level in range(LAYERS):
        cut = slice(level * ROWS, (level + 1) * ROWS)
        own = conduct[cut, :]
        over = zero
        if level < LAYERS - 1:
            over = WEIGHT_V * harmonic(own, conduct[(level + 1) * ROWS : (level + 2) * ROWS, :])
        above[cut, :] = over
        sides = diagonal[cut, :] + below + over
        diagonal[cut, :] = sides
        denom = sides + 4.0 * WEIGHT_H * own + below * last_ratio
        inverse = 1.0 / denom
        last_ratio = -over * inverse
        last_value = (basis[cut, :] + below * last_value) * inverse
        ratio[cut, :] = last_ratio
        value[cut, :] = last_value
        below = over
    for level in range(LAYERS - 2, -1, -1):
        cut = slice(level * ROWS, (level + 1) * ROWS)
        last_value = value[cut, :] - ratio[cut, :] * last_value
        value[cut, :] = last_value
    for q in range(4):
        local[q * RUNS : (q + 1) * RUNS, :] = turn(value[pl.ds(q, RUNS, stride=4), :], 32 * q + 16)


def faces_kernel(
    conduct,
    diagonal,
    table,
    first_y,
    second_y,
    first_x,
    second_x,
    faces,
    total,
    side,
):
    gx, gy = lax.axis_index("gx"), lax.axis_index("gy")
    last_x, last_y = lax.axis_size("gx") - 1, lax.axis_size("gy") - 1
    at = lanes(RUNS)
    from_left, from_right = sides(
        gy % 2 == 0, first_y[...].astype(F32), second_y[...].astype(F32)
    )
    kinds = jnp.zeros((RUNS, COLS), F32)
    for q in range(4):
        kinds = jnp.where(at == 32 * q + 16, from_left, kinds)
        kinds = jnp.where(at == 32 * q + 15, from_right, kinds)
    known = look_up(kinds.astype(jnp.int32), table, (0, 1))
    for q in range(4):
        side[pl.ds(q, RUNS, stride=4), :] = turn(known, -(32 * q + 16))
    before, after = sides(
        gx % 2 == 0, first_x[FLAT:, :].astype(F32), second_x[FLAT:, :].astype(F32)
    )
    row_before = look_up(before.astype(jnp.int32), table, (0, 1))
    row_after = look_up(after.astype(jnp.int32), table, (0, 1))
    at = lanes(ROWS)
    row = lax.broadcasted_iota(jnp.int32, (ROWS, COLS), 0)
    for level in range(LAYERS):
        cut = slice(level * ROWS, (level + 1) * ROWS)
        own = conduct[cut, :]
        aside = side[cut, :]
        over = row_before[level : level + 1, :]
        under = row_after[level : level + 1, :]
        weights = [
            jnp.where((at > 0) | (gy > 0), harmonic(own, jnp.where(at == 0, aside, turn(own, 1))), 0.0),
            jnp.where(
                (at < COLS - 1) | (gy < last_y),
                harmonic(own, jnp.where(at == COLS - 1, aside, turn(own, -1))),
                0.0,
            ),
            jnp.where(
                (row > 0) | (gx > 0),
                harmonic(own, jnp.where(row == 0, over, pltpu.roll(own, 1, 0))),
                0.0,
            ),
            jnp.where(
                (row < ROWS - 1) | (gx < last_x),
                harmonic(own, jnp.where(row == ROWS - 1, under, pltpu.roll(own, ROWS - 1, 0))),
                0.0,
            ),
        ]
        for index in range(4):
            faces[index, cut, :] = WEIGHT_H * weights[index]
        total[cut, :] = diagonal[cut, :] + WEIGHT_H * (
            (weights[0] + weights[1]) + (weights[2] + weights[3])
        )


def image_kernel(
    field,
    rim,
    up,
    dn,
    from_first,
    from_second,
    basis,
    faces,
    total,
    above,
    gram,
    precond,
    image,
    sums,
    side,
):
    gy = lax.axis_index("gy")
    last_y = lax.axis_size("gy") - 1
    at = lanes(RUNS)
    from_left, from_right = sides(
        gy % 2 == 0,
        from_first[...].astype(F32)[: RUNS + LAYERS],
        from_second[...].astype(F32)[: RUNS + LAYERS],
    )
    from_left = jnp.where(gy > 0, from_left, 0.0)
    from_right = jnp.where(gy < last_y, from_right, 0.0)
    to_left = dn[...] + from_left
    to_right = up[...] + from_right
    for q in range(4):
        cut = 32 * q + 16
        turned = field[q * RUNS : (q + 1) * RUNS, :]
        turned = turned + jnp.where((at >= cut) & (at < cut + 16), from_left[:RUNS], 0.0)
        turned = turned + jnp.where((at >= cut - 16) & (at < cut), from_right[:RUNS], 0.0)
        precond[pl.ds(q, RUNS, stride=4), :] = turn(turned, -cut)
        edges = jnp.where(at == cut - 1, to_left[:RUNS], to_right[:RUNS])
        side[pl.ds(q, RUNS, stride=4), :] = turn(edges, -cut)
    at = lanes(LAYERS)
    rim_left, rim_right = from_left[RUNS:], from_right[RUNS:]
    over = rim[:LAYERS, :]
    over = over + jnp.where(at >= 112, rim_left, 0.0)
    over = turn(over + jnp.where((at >= 96) & (at < 112), rim_right, 0.0), -112)
    under = rim[LAYERS:, :]
    under = under + jnp.where((at >= 16) & (at < 32), rim_left, 0.0)
    under = turn(under + jnp.where(at < 16, rim_right, 0.0), -16)
    at = lanes(ROWS)
    row = lax.broadcasted_iota(jnp.int32, (ROWS, COLS), 0)
    totals = [jnp.zeros((8, COLS), F32) for _ in range(5)]
    for level in range(LAYERS):
        cut = slice(level * ROWS, (level + 1) * ROWS)
        own = precond[cut, :]
        aside = side[cut, :]
        result = total[cut, :] * own
        result = result - faces[0, cut, :] * jnp.where(at == 0, turn(aside, 1), turn(own, 1))
        result = result - faces[1, cut, :] * jnp.where(
            at == COLS - 1, turn(aside, -1), turn(own, -1)
        )
        result = result - faces[2, cut, :] * jnp.where(
            row == 0, over[level : level + 1, :], pltpu.roll(own, 1, 0)
        )
        result = result - faces[3, cut, :] * jnp.where(
            row == ROWS - 1, under[level : level + 1, :], pltpu.roll(own, ROWS - 1, 0)
        )
        if level > 0:
            back = slice((level - 1) * ROWS, level * ROWS)
            result = result - above[back, :] * precond[back, :]
        if level < LAYERS - 1:
            ahead = slice((level + 1) * ROWS, (level + 2) * ROWS)
            result = result - above[cut, :] * precond[ahead, :]
        image[cut, :] = result
        for j in range(5):
            product = (basis[j, cut, :] if j < 4 else result) * result
            totals[j] = totals[j] + (product[:8] + product[8:])
    totals += [gram[8 * slot : 8 * slot + 8, :] for slot in range(10)]
    totals.append(jnp.zeros((8, COLS), F32))
    rows = jnp.concatenate([jnp.sum(part, axis=0, keepdims=True) for part in totals], axis=0)
    column = jnp.sum(rows, axis=1, keepdims=True)
    keep = lanes(ROWS) == lax.broadcasted_iota(jnp.int32, (ROWS, COLS), 0)
    line = jnp.sum(jnp.where(keep, column, 0.0), axis=0, keepdims=True)
    sums[...] = jnp.broadcast_to(line, sums.shape)


def next_kernel(gathered, image, basis, out, hessenberg):
    cells = float(CELLS * COLS * lax.axis_size("gx") * lax.axis_size("gy"))
    line = jnp.sum(gathered[...], axis=0, keepdims=True) / cells
    entry = [line[:, i : i + 1] for i in range(15)]
    project = entry[:4]
    square = entry[4]
    for j in range(4):
        square = square - 2.0 * project[j] * project[j]
    slot = 5
    for i in range(4):
        for j in range(i, 4):
            square = square + (1.0 if i == j else 2.0) * project[i] * project[j] * entry[slot]
            slot += 1
    length = jnp.sqrt(jnp.maximum(square, 0.0) + EPS)
    at = lanes(1)
    found = jnp.where(at == 4, length, jnp.where(at < 4, line, 0.0))
    for i in range(5):
        hessenberg[i] = found[0, i]
    inverse = 1.0 / length
    scaled = [project[j] * inverse for j in range(4)]
    for level in range(LAYERS):
        cut = slice(level * ROWS, (level + 1) * ROWS)
        value = image[cut, :] * inverse
        for j in range(4):
            value = value - scaled[j] * basis[j, cut, :]
        out[cut, :] = value


def swap(values, partner):
    across, along = lax.axis_size("gx"), lax.axis_size("gy")
    pairs = []
    for a in range(across):
        for b in range(along):
            c, d = partner(a, b)
            if not 0 <= d < along:
                c, d = a ^ 1, b
            if not 0 <= c < across:
                c, d = a, b ^ 1
            pairs.append((a * along + b, c * along + d))
    return lax.ppermute(values, ("gx", "gy"), pairs)


def swap_y(first, second):
    return (
        swap(first, lambda a, b: (a, b ^ 1)),
        swap(second, lambda a, b: (a, ((b + 1) ^ 1) - 1)),
    )


def swap_x_first(values):
    return swap(values, lambda a, b: (a ^ 1, b))


def swap_x_second(values):
    return swap(values, lambda a, b: (((a + 1) ^ 1) - 1, b))


def swap_far(first, second):
    return (
        swap(first, lambda a, b: (a ^ 2, b)),
        swap(second, lambda a, b: (((a + 2) ^ 2) - 2, b)),
    )


def exchange(lines):
    size = lines.shape[0]
    out = lax.all_to_all(lines.reshape(size, 1, COLS), ("gx", "gy"), 0, 0)
    return out.reshape(size, COLS)


def on_device(basis, soil, frozen, soil_table, coarse_basis, coarse_inverse, active_count):
    basis = basis.reshape(4, CELLS, COLS)
    soil, frozen = soil.reshape(CELLS, COLS), frozen.reshape(CELLS, COLS)
    source = pltpu.with_memory_space_constraint(coarse_basis.reshape(K, -1), pltpu.HBM)
    devices = lax.axis_size("gx") * lax.axis_size("gy")
    field_space = pltpu.VMEM((CELLS, COLS), F32)
    kinds = pltpu.VMEM((CELLS, COLS), jnp.int32)
    basis, soil, frozen = (
        pltpu.with_memory_space_constraint(x, pltpu.HBM) for x in (basis, soil, frozen)
    )
    first, second, flat, kinds_x, current, code = call(
        pack_kernel,
        [
            shape(RUNS, COLS, dtype=BF16),
            shape(RUNS, COLS, dtype=BF16),
            shape(FLAT, COLS, dtype=BF16),
            shape(2, PAD - FLAT, COLS),
            pltpu.VMEM((CELLS, COLS), F32),
            pltpu.VMEM((CELLS, COLS), F32),
        ],
        [HB] * 3,
        (basis, soil, frozen),
        [kinds, kinds, pltpu.SemaphoreType.DMA((3,))],
        out_specs=[VM] * 6,
        name="pack",
    )
    from_y = swap_y(first, second)
    early, conduct, diagonal, above, local = call(
        early_kernel,
        [pltpu.VMEM((K, EARLY * WINDOW), BF16)] + [shape(CELLS, COLS)] * 4,
        [HB, HB, VM, VM],
        (source, pltpu.with_memory_space_constraint(soil_table, pltpu.HBM), current, code),
        [
            field_space,
            field_space,
            pltpu.SMEM((4, 8), F32),
            pltpu.SemaphoreType.DMA((2,)),
        ],
        out_specs=[VM] * 5,
        moved=10_000_000,
        name="early",
    )
    early, flat = lax.optimization_barrier((early, flat))
    flat, second = call(
        flat_kernel, [shape(PAD, COLS, dtype=BF16)] * 2, [VM] * 4, (flat, kinds_x, *from_y), name="flat"
    )
    from_second = swap_x_second(second)
    from_x = swap_x_first(flat), from_second
    late, basis, begun, gram = call(
        load_kernel,
        [
            pltpu.VMEM((K, (LAYERS - EARLY) * WINDOW), BF16),
            pltpu.VMEM((4, CELLS, COLS), F32),
            shape(K, COLS),
            shape(80, COLS),
        ],
        [HB, HB, VM, VM],
        (source, basis, early, flat),
        [
            pltpu.VMEM((FLAT, COLS), F32),
            pltpu.SemaphoreType.DMA(((LAYERS - EARLY) // CHUNK + 1,)),
        ],
        out_specs=[VM] * 4,
        flops=16_000_000,
        moved=20_000_000,
        name="load",
    )
    vector = pltpu.VMEM((FLAT, COLS), F32)
    begun = call(
        first_rhs_kernel,
        shape(K, COLS),
        [VM] * 4,
        (early, late, begun, from_x[0]),
        [vector],
        flops=6_000_000,
        moved=6_000_000,
        name="first_rhs",
    )
    lines = call(
        second_rhs_kernel,
        shape(devices, COLS),
        [VM] * 5,
        (early, late, begun, from_x[1], active_count),
        [vector],
        flops=6_000_000,
        moved=6_000_000,
        name="second_rhs",
    )
    gathered = exchange(lines)
    message = shape(ENDS, COLS, dtype=BF16)
    ends = pltpu.VMEM((2 * LAYERS, COLS), F32)
    weights, second, near_second, far = call(
        second_spread_kernel,
        [shape(K, COLS), message, shape(80, COLS), shape(80, COLS)],
        [VM] * 6,
        (early, late, coarse_inverse, gathered, active_count, local),
        [pltpu.VMEM((K, COLS), F32), vector, ends],
        flops=20_000_000,
        moved=8_000_000,
        name="second_spread",
    )
    from_second = swap_x_second(second)
    first, near_first, far_first, far_second = call(
        first_spread_kernel,
        [message, shape(80, COLS)] + [shape(80, COLS, dtype=BF16)] * 2,
        [VM] * 5,
        (early, late, weights, local, far),
        [vector, ends],
        flops=20_000_000,
        moved=8_000_000,
        name="first_spread",
    )
    near = swap_x_first(first), from_second
    far = swap_far(far_first, far_second)
    own = call(
        own_spread_kernel,
        shape(FLAT, COLS),
        [VM] * 3,
        (early, late, weights),
        flops=20_000_000,
        moved=7_000_000,
        name="own_spread",
    )
    conduct, diagonal, weights = lax.optimization_barrier((conduct, diagonal, weights))
    faces, total = call(
        faces_kernel,
        [shape(4, CELLS, COLS), shape(CELLS, COLS)],
        [VM, VM, SM, VM, VM, VM, VM],
        (conduct, diagonal, soil_table, *from_y, *from_x),
        [field_space],
        flops=4_000_000,
        moved=2_000_000,
        name="faces",
    )
    field, rim, up, dn, first, second = call(
        fold_rows_kernel,
        [shape(CELLS, COLS), shape(80, COLS)]
        + [shape(RUNS + LAYERS, COLS)] * 2
        + [shape(SIDE, COLS, dtype=BF16)] * 2,
        [VM] * 8,
        (own, near_first, near_second, local, *near, *far),
        name="fold_rows",
    )
    from_y = swap_y(first, second)
    precond, image, sums = call(
        image_kernel,
        [shape(CELLS, COLS), shape(CELLS, COLS), shape(devices, COLS)],
        [VM] * 11,
        (field, rim, up, dn, *from_y, basis, faces, total, above, gram),
        [field_space],
        name="image",
    )
    gathered = exchange(sums)
    following, hessenberg = call(
        next_kernel,
        [shape(CELLS, COLS), shape(5)],
        [VM] * 3,
        (gathered, image, basis),
        out_specs=[VM, SM],
        name="next",
    )
    tile = (LAYERS, ROWS, COLS)
    return precond.reshape(tile), following.reshape(tile), hessenberg


def solution(mesh):
    placed = (
        P(None, None, "gx", "gy"),
        P(None, "gx", "gy"),
        P(None, "gx", "gy"),
        P(),
        P("gx", "gy", None, None),
        P(("gx", "gy"), None),
        P("gx", "gy"),
    )
    return jax.shard_map(
        on_device,
        mesh=mesh,
        in_specs=placed,
        out_specs=(P(None, "gx", "gy"), P(None, "gx", "gy"), P()),
        check_vma=False,
    )
```

```python
import functools

import jax
import jax.numpy as jnp
from jax import lax
from jax.experimental import pallas as pl
from jax.experimental.pallas import tpu as pltpu
from jax.sharding import PartitionSpec as P

F32 = jnp.float32
BF16 = jnp.bfloat16

LAYERS, ROWS, COLS, OV, K = 40, 16, 128, 16, 32
CELLS = LAYERS * ROWS
RUNS = CELLS // 4
FLAT = 5 * RUNS
WINDOW = 7680
EARLY = 8
CHUNK = 16
PAD = FLAT + 48
SIDE = RUNS + 48
ENDS = FLAT + 80
PART = 2560
WEIGHT_V, WEIGHT_H, EPS = 4.0, 1.0, 1e-06

VM = pl.BlockSpec(memory_space=pltpu.VMEM)
SM = pl.BlockSpec(memory_space=pltpu.SMEM)
HB = pl.BlockSpec(memory_space=pltpu.HBM)


def shape(*dims, dtype=F32):
    return jax.ShapeDtypeStruct(dims, dtype)


def call(kernel, outs, specs, args, scratch=(), out_specs=None, flops=0, moved=0, name=None):
    return pl.pallas_call(
        kernel,
        out_shape=outs,
        in_specs=specs,
        out_specs=out_specs if out_specs is not None else jax.tree.map(lambda _: VM, outs),
        scratch_shapes=list(scratch),
        compiler_params=pltpu.CompilerParams(vmem_limit_bytes=16 * 2**20),
        cost_estimate=pl.CostEstimate(flops=flops, bytes_accessed=moved, transcendentals=0),
        name=name,
    )(*args)


def lanes(rows):
    return lax.broadcasted_iota(jnp.int32, (rows, COLS), 1)


def harmonic(first, second):
    return 2.0 * first * second / (first + second)


def steps(count):
    return max(n for n in range(1, 8) if count % n == 0)


def turn(values, amount):
    return pltpu.roll(values, amount % COLS, 1)


def pack_kernel(
    basis_in,
    soil_in,
    frozen_in,
    first,
    second,
    flat,
    kinds,
    basis,
    code,
    soil,
    frozen,
    arrived,
):
    copies = [
        pltpu.make_async_copy(basis_in.at[3], basis, arrived.at[0]),
        pltpu.make_async_copy(soil_in, soil, arrived.at[1]),
        pltpu.make_async_copy(frozen_in, frozen, arrived.at[2]),
    ]
    for copy in copies:
        copy.start()
    for copy in copies:
        copy.wait()
    code[...] = (soil[...] + 8 * frozen[...]).astype(F32)
    at = lanes(RUNS)
    to_up = jnp.zeros((RUNS, COLS), F32)
    to_dn = to_up
    flats = [jnp.zeros((RUNS, COLS), F32) for _ in range(5)]
    for q in range(4):
        cut = 32 * q + 16
        turned = turn(basis[pl.ds(q, RUNS, stride=4), :], cut)
        kind = code[pl.ds(q, RUNS, stride=4), :]
        low = (at >= cut - 16) & (at < cut)
        high = (at >= cut) & (at < cut + 16)
        to_up = jnp.where(low, turned, jnp.where(at == cut, turn(kind, cut + 1), to_up))
        to_dn = jnp.where(high, turned, jnp.where(at == cut - 1, turn(kind, cut - 1), to_dn))
        flats[q] = jnp.where(at >= cut, turned, flats[q])
        flats[q + 1] = jnp.where(at < cut, turned, flats[q + 1])
    even = lax.axis_index("gy") % 2 == 0
    first[...] = jnp.where(even, to_up, to_dn).astype(BF16)
    second[...] = jnp.where(even, to_dn, to_up).astype(BF16)
    for j in range(5):
        flat[j * RUNS : (j + 1) * RUNS, :] = flats[j].astype(BF16)
    spare = jnp.zeros((PAD - FLAT - LAYERS, COLS), F32)
    for index, row in enumerate((0, ROWS - 1)):
        line = jnp.concatenate([code[pl.ds(row, LAYERS, stride=ROWS), :], spare], axis=0)
        kinds[index] = line


def sides(even, first, second):
    return jnp.where(even, second, first), jnp.where(even, first, second)


def flat_kernel(own, kinds, from_first, from_second, first, second):
    place = lax.axis_index("gy")
    last = lax.axis_size("gy") - 1
    at = lanes(RUNS)
    from_left, from_right = sides(
        place % 2 == 0, from_first[...].astype(F32), from_second[...].astype(F32)
    )
    from_left = jnp.where(place > 0, from_left, 0.0)
    from_right = jnp.where(place < last, from_right, 0.0)
    for j in range(5):
        part = own[j * RUNS : (j + 1) * RUNS, :].astype(F32)
        if j < 4:
            part = jnp.where((at >= 32 * j) & (at < 32 * j + 16), from_left, part)
        if j > 0:
            part = jnp.where((at >= 32 * j - 16) & (at < 32 * j), from_right, part)
        first[j * RUNS : (j + 1) * RUNS, :] = part.astype(BF16)
        second[j * RUNS : (j + 1) * RUNS, :] = part.astype(BF16)
    even = lax.axis_index("gx") % 2 == 0
    first[FLAT:, :] = jnp.where(even, kinds[1], kinds[0]).astype(BF16)
    second[FLAT:, :] = jnp.where(even, kinds[0], kinds[1]).astype(BF16)


def project_part(coarse, vector, part, totals, first, begin, count):
    def body(layer, totals):
        totals = list(totals)
        base = pl.multiple_of((begin + layer) * WINDOW + part * PART, 128)
        row = (first + begin + layer) * 4
        wide = jnp.concatenate(
            [
                jnp.broadcast_to(vector[pl.ds(j * RUNS + row + m, 1), :], (8, COLS))
                for m in range(4)
                for j in range(5)
            ],
            axis=1,
        )
        for r in range(4):
            product = coarse[8 * r : 8 * r + 8, pl.ds(base, PART)].astype(F32) * wide
            for t in range(20):
                slot = 2 * r + t % 2
                totals[slot] = totals[slot] + product[:, t * COLS : (t + 1) * COLS]
        return tuple(totals)

    return lax.fori_loop(0, count, body, totals, unroll=steps(count))


def early_kernel(
    source,
    table_in,
    basis,
    code,
    out,
    conduct,
    diagonal,
    above,
    local,
    ratio,
    value,
    table,
    arrived,
):
    small = pltpu.make_async_copy(table_in, table, arrived.at[0])
    small.start()
    copy = pltpu.make_async_copy(source.at[:, : EARLY * WINDOW], out, arrived.at[1])
    copy.start()
    small.wait()
    solve_columns(basis, code, table, conduct, diagonal, above, local, ratio, value)
    copy.wait()


def multiply_out(basis, gram):
    def body(level, grams):
        grams = list(grams)
        cut = pl.ds(pl.multiple_of(level * ROWS, ROWS), ROWS)
        vectors = [basis[j, cut, :] for j in range(4)]
        slot = 0
        for i in range(4):
            for j in range(i, 4):
                square = vectors[i] * vectors[j]
                grams[slot] = grams[slot] + (square[:8] + square[8:])
                slot += 1
        return tuple(grams)

    zero = jnp.zeros((8, COLS), F32)
    grams = lax.fori_loop(0, LAYERS, body, (zero,) * 10, unroll=4)
    for slot in range(10):
        gram[8 * slot : 8 * slot + 8, :] = grams[slot]


def load_kernel(source, basis_in, early, own, late, basis, begun, gram, vector, arrived):
    ready = pltpu.make_async_copy(basis_in, basis, arrived.at[0])
    ready.start()
    copies = []
    for index in range((LAYERS - EARLY) // CHUNK):
        begin, size = index * CHUNK * WINDOW, CHUNK * WINDOW
        copies.append(
            pltpu.make_async_copy(
                source.at[:, EARLY * WINDOW + begin : EARLY * WINDOW + begin + size],
                late.at[:, begin : begin + size],
                arrived.at[index + 1],
            )
        )
    for copy in copies:
        copy.start()
    vector[...] = own[:FLAT, :].astype(F32)
    totals = (jnp.zeros((8, COLS), F32),) * 8
    totals = project_part(early, vector, 1, totals, 0, 0, EARLY)
    ready.wait()
    multiply_out(basis, gram)
    for index, copy in enumerate(copies):
        copy.wait()
        totals = project_part(late, vector, 1, totals, EARLY, index * CHUNK, CHUNK)
    for r in range(4):
        begun[8 * r : 8 * r + 8, :] = totals[2 * r] + totals[2 * r + 1]


def project_neighbour(early, late, whole, vector, upper, valid, totals):
    vector[...] = jnp.where(valid, whole[:FLAT, :].astype(F32), 0.0)
    part = jnp.where(upper, 2, 0)
    totals = project_part(early, vector, part, totals, 0, 0, EARLY)
    return project_part(late, vector, part, totals, EARLY, 0, LAYERS - EARLY)


def unfold(begun):
    zero = jnp.zeros((8, COLS), F32)
    return tuple(begun[4 * s : 4 * s + 8, :] if s % 2 == 0 else zero for s in range(8))


def first_rhs_kernel(early, late, begun, whole, out, vector):
    upper = lax.axis_index("gx") % 2 == 0
    totals = project_neighbour(early, late, whole, vector, upper, True, unfold(begun))
    for r in range(4):
        out[8 * r : 8 * r + 8, :] = totals[2 * r] + totals[2 * r + 1]


def second_rhs_kernel(early, late, begun, whole, count, out, vector):
    place = lax.axis_index("gx")
    valid = (place > 0) & (place < lax.axis_size("gx") - 1)
    totals = project_neighbour(early, late, whole, vector, place % 2 == 1, valid, unfold(begun))
    full = jnp.concatenate([totals[2 * r] + totals[2 * r + 1] for r in range(4)], axis=0)
    sums = jnp.sum(full, axis=1, keepdims=True)
    index = lax.broadcasted_iota(jnp.int32, (K, COLS), 0)
    keep = (lanes(K) % K == index) & (index < count[...])
    row = jnp.sum(jnp.where(keep, sums, 0.0), axis=0, keepdims=True)
    out[...] = jnp.broadcast_to(row, out.shape)


def reduce_eight(parts, where):
    four, two, one = where

    def merge(a, b, mask, step):
        kept = jnp.where(mask, a, b)
        moved = jnp.where(mask, b, a)
        if step == 4:
            return kept + pltpu.roll(moved, 4, 0)
        return kept + jnp.where(mask, pltpu.roll(moved, 8 - step, 0), pltpu.roll(moved, step, 0))

    parts = [merge(parts[t], parts[t + 4], four, 4) for t in range(4)]
    parts = [merge(parts[t], parts[t + 2], two, 2) for t in range(2)]
    return merge(parts[0], parts[1], one, 1)


def reduction_masks():
    row = lax.broadcasted_iota(jnp.int32, (8, COLS), 0)
    return row < 4, row % 4 < 2, row % 2 < 1


def combine(coarse, base, width, weights):
    terms = [
        coarse[8 * r : 8 * r + 8, pl.ds(base, width)].astype(F32) * weights[r][:, :width]
        for r in range(4)
    ]
    return (terms[0] + terms[1]) + (terms[2] + terms[3])


def spread_part(coarse, weights, part, out, first, count):
    where = reduction_masks()

    def body(pair, carry):
        halves = []
        for half in range(2):
            base = pl.multiple_of((2 * pair + half) * WINDOW + part * PART, 128)
            halves.append(combine(coarse, base, PART, weights))
        for j in range(5):
            tiles = [
                halves[half][:, (5 * m + j) * COLS : (5 * m + j + 1) * COLS]
                for half in range(2)
                for m in range(4)
            ]
            start = pl.multiple_of(j * RUNS + 4 * first + 8 * pair, 8)
            out[pl.ds(start, 8), :] = reduce_eight(tiles, where)
        return carry

    lax.fori_loop(0, count // 2, body, 0, unroll=steps(count // 2))


def spread_ends(coarse, weights, begin, out, first, count):
    where = reduction_masks()

    def body(four, carry):
        tiles = []
        for layer in range(4):
            base = (4 * four + layer) * WINDOW + PART + begin
            both = combine(coarse, pl.multiple_of(base, 128), 2 * COLS, weights)
            tiles += [both[:, :COLS], both[:, COLS:]]
        start = pl.multiple_of(2 * first + 8 * four, 8)
        out[pl.ds(start, 8), :] = reduce_eight(tiles, where)
        return carry

    lax.fori_loop(0, count // 4, body, 0, unroll=steps(count // 4))


def widen(weights):
    return [
        jnp.concatenate([weights[8 * r : 8 * r + 8, :]] * (PART // COLS), axis=1) for r in range(4)
    ]


def solve(inverse, gathered, count, rhs):
    at = lanes(K)
    rows = jnp.zeros((K, COLS), F32)
    for e in range(4):
        rows = jnp.where(at // K == e, gathered[pl.ds(e, K, stride=4), :], rows)
    rhs[...] = rows
    total = jnp.zeros((K, COLS), F32)
    for i in range(K):
        total = total + inverse[:, i * COLS : (i + 1) * COLS] * rhs[i : i + 1, :]
    solved = jnp.sum(total, axis=1, keepdims=True)
    index = lax.broadcasted_iota(jnp.int32, (K, COLS), 0)
    return jnp.where(index < count[...], solved, 0.0).astype(BF16).astype(F32)


def spread_to(upper, early, late, solved, local, message, near, whole, ends):
    wide = widen(solved)
    part, begin = jnp.where(upper, 2, 0), jnp.where(upper, 18 * COLS, 0)
    for coarse, start, size in ((early, 0, EARLY), (late, EARLY, LAYERS - EARLY)):
        spread_part(coarse, wide, part, whole, start, size)
        spread_ends(coarse, wide, begin, ends, start, size)
    message[:FLAT, :] = whole[...].astype(BF16)

    def strip(ref, j, m):
        return ref[pl.ds(j * RUNS + m, LAYERS, stride=4), :]

    def both(first, second):
        return jnp.concatenate([first, second], axis=0)

    at = lanes(LAYERS)
    cut = jnp.where(upper, 112, 16)
    row = jnp.where(upper, strip(local, 3, 3), strip(local, 0, 0))
    ours = [ends[pl.ds(index, LAYERS, stride=2), :] for index in range(2)]
    message[FLAT:, :] = both(
        ours[0] + jnp.where(at >= cut, row, 0.0), ours[1] + jnp.where(at < cut, row, 0.0)
    ).astype(BF16)
    top = both(strip(whole, 0, 0), strip(whole, 1, 0))
    bottom = both(strip(whole, 3, 3), strip(whole, 4, 3))
    near[...] = jnp.where(upper, top, bottom)
    return jnp.where(upper, bottom, top)


def first_spread_kernel(
    early, late, inverse, gathered, count, local, weights, message, near, far, rhs, whole, ends
):
    solved = solve(inverse, gathered, count, rhs)
    weights[...] = solved
    upper = lax.axis_index("gx") % 2 == 0
    far[...] = spread_to(upper, early, late, solved, local, message, near, whole, ends)


def second_spread_kernel(
    early, late, weights, local, far, message, near, far_first, far_second, whole, ends
):
    place = lax.axis_index("gx")
    upper = place % 2 == 1
    own = spread_to(upper, early, late, weights[...], local, message, near, whole, ends)
    swapped = (place % 4 == 1) | (place % 4 == 2)
    far_first[...] = jnp.where(swapped, own, far[...]).astype(BF16)
    far_second[...] = jnp.where(swapped, far[...], own).astype(BF16)


def own_spread_kernel(early, late, weights, own):
    wide = widen(weights[...])
    spread_part(early, wide, 1, own, 0, EARLY)
    spread_part(late, wide, 1, own, EARLY, LAYERS - EARLY)


def fold_rows_kernel(
    own,
    near_first,
    near_second,
    local,
    from_first,
    from_second,
    far_second,
    far_first,
    field,
    rim,
    up,
    dn,
    first,
    second,
):
    place = lax.axis_index("gx")
    last = lax.axis_size("gx") - 1
    even, lower = place % 2 == 0, place % 4 < 2
    at = lanes(RUNS)
    whole = []
    for j in range(5):
        cut = slice(j * RUNS, (j + 1) * RUNS)
        before, after = sides(even, from_first[cut, :].astype(F32), from_second[cut, :].astype(F32))
        part = own[cut, :] + jnp.where(place > 0, before, 0.0)
        part = part + jnp.where(place < last, after, 0.0)
        if j < 4:
            part = part + jnp.where(at >= 32 * j + 16, local[cut, :], 0.0)
        if j > 0:
            behind = local[(j - 1) * RUNS : j * RUNS, :]
            part = part + jnp.where(at < 32 * j - 16, behind, 0.0)
        whole.append(part)
    to_up = jnp.zeros((RUNS, COLS), F32)
    to_dn = to_up
    for q in range(4):
        field[q * RUNS : (q + 1) * RUNS, :] = jnp.where(
            at >= 32 * q + 16, whole[q], whole[q + 1]
        )
        band = (at >= 32 * q) & (at < 32 * q + 32)
        to_up = jnp.where(band, whole[q + 1], to_up)
        to_dn = jnp.where(band, whole[q], to_dn)
    up[:RUNS, :] = to_up
    dn[:RUNS, :] = to_dn

    before, after = sides(even, from_first[FLAT:, :].astype(F32), from_second[FLAT:, :].astype(F32))
    before2, after2 = sides(lower, far_first[...].astype(F32), far_second[...].astype(F32))
    near_before, near_after = sides(even, near_first[...], near_second[...])
    top = near_before + before + jnp.where(place > 1, before2, 0.0)
    bottom = near_after + after + jnp.where(place < last - 1, after2, 0.0)
    at = lanes(LAYERS)
    half = LAYERS
    rim[:half, :] = jnp.where(at >= 112, top[:half], top[half:])
    rim[half:, :] = jnp.where(at >= 16, bottom[:half], bottom[half:])
    up[RUNS:, :] = jnp.where(at >= 96, top[half:], bottom[half:])
    dn[RUNS:, :] = jnp.where(at >= 96, top[:half], bottom[:half])
    even = lax.axis_index("gy") % 2 == 0
    spare = jnp.zeros((SIDE - RUNS - LAYERS, COLS), F32)
    to_up = jnp.concatenate([up[...], spare], axis=0)
    to_dn = jnp.concatenate([dn[...], spare], axis=0)
    first[...] = jnp.where(even, to_up, to_dn).astype(BF16)
    second[...] = jnp.where(even, to_dn, to_up).astype(BF16)


def look_up(kind, table, rows):
    value = jnp.zeros(kind.shape, F32)
    for index in range(8):
        value = jnp.where(kind == index, table[rows[0], index], value)
        value = jnp.where(kind == index + 8, table[rows[1], index], value)
    return value


def solve_columns(basis, code, table, conduct, diagonal, above, local, ratio, value):
    def body(index, carry):
        cut = pl.ds(pl.multiple_of(index * 64, 64), 64)
        kind = code[cut, :]
        conduct[cut, :] = look_up(kind, table, (0, 1))
        diagonal[cut, :] = look_up(kind, table, (2, 3))
        return carry

    lax.fori_loop(0, CELLS // 64, body, 0)
    zero = jnp.zeros((ROWS, COLS), F32)
    below = zero
    last_ratio = zero
    last_value = zero
    for level in range(LAYERS):
        cut = slice(level * ROWS, (level + 1) * ROWS)
        own = conduct[cut, :]
        over = zero
        if level < LAYERS - 1:
            over = WEIGHT_V * harmonic(own, conduct[(level + 1) * ROWS : (level + 2) * ROWS, :])
        above[cut, :] = over
        sides = diagonal[cut, :] + below + over
        diagonal[cut, :] = sides
        denom = sides + 4.0 * WEIGHT_H * own + below * last_ratio
        inverse = 1.0 / denom
        last_ratio = -over * inverse
        last_value = (basis[cut, :] + below * last_value) * inverse
        ratio[cut, :] = last_ratio
        value[cut, :] = last_value
        below = over
    for level in range(LAYERS - 2, -1, -1):
        cut = slice(level * ROWS, (level + 1) * ROWS)
        last_value = value[cut, :] - ratio[cut, :] * last_value
        value[cut, :] = last_value
    for q in range(4):
        local[q * RUNS : (q + 1) * RUNS, :] = turn(value[pl.ds(q, RUNS, stride=4), :], 32 * q + 16)


def faces_kernel(
    conduct,
    diagonal,
    table,
    first_y,
    second_y,
    first_x,
    second_x,
    faces,
    total,
    side,
):
    gx, gy = lax.axis_index("gx"), lax.axis_index("gy")
    last_x, last_y = lax.axis_size("gx") - 1, lax.axis_size("gy") - 1
    at = lanes(RUNS)
    from_left, from_right = sides(
        gy % 2 == 0, first_y[...].astype(F32), second_y[...].astype(F32)
    )
    kinds = jnp.zeros((RUNS, COLS), F32)
    for q in range(4):
        kinds = jnp.where(at == 32 * q + 16, from_left, kinds)
        kinds = jnp.where(at == 32 * q + 15, from_right, kinds)
    known = look_up(kinds.astype(jnp.int32), table, (0, 1))
    for q in range(4):
        side[pl.ds(q, RUNS, stride=4), :] = turn(known, -(32 * q + 16))
    before, after = sides(
        gx % 2 == 0, first_x[FLAT:, :].astype(F32), second_x[FLAT:, :].astype(F32)
    )
    row_before = look_up(before.astype(jnp.int32), table, (0, 1))
    row_after = look_up(after.astype(jnp.int32), table, (0, 1))
    at = lanes(ROWS)
    row = lax.broadcasted_iota(jnp.int32, (ROWS, COLS), 0)
    for level in range(LAYERS):
        cut = slice(level * ROWS, (level + 1) * ROWS)
        own = conduct[cut, :]
        aside = side[cut, :]
        over = row_before[level : level + 1, :]
        under = row_after[level : level + 1, :]
        weights = [
            jnp.where((at > 0) | (gy > 0), harmonic(own, jnp.where(at == 0, aside, turn(own, 1))), 0.0),
            jnp.where(
                (at < COLS - 1) | (gy < last_y),
                harmonic(own, jnp.where(at == COLS - 1, aside, turn(own, -1))),
                0.0,
            ),
            jnp.where(
                (row > 0) | (gx > 0),
                harmonic(own, jnp.where(row == 0, over, pltpu.roll(own, 1, 0))),
                0.0,
            ),
            jnp.where(
                (row < ROWS - 1) | (gx < last_x),
                harmonic(own, jnp.where(row == ROWS - 1, under, pltpu.roll(own, ROWS - 1, 0))),
                0.0,
            ),
        ]
        for index in range(4):
            faces[index, cut, :] = WEIGHT_H * weights[index]
        total[cut, :] = diagonal[cut, :] + WEIGHT_H * (
            (weights[0] + weights[1]) + (weights[2] + weights[3])
        )


def image_kernel(
    field,
    rim,
    up,
    dn,
    from_first,
    from_second,
    basis,
    faces,
    total,
    above,
    gram,
    precond,
    image,
    sums,
    side,
):
    gy = lax.axis_index("gy")
    last_y = lax.axis_size("gy") - 1
    at = lanes(RUNS)
    from_left, from_right = sides(
        gy % 2 == 0,
        from_first[...].astype(F32)[: RUNS + LAYERS],
        from_second[...].astype(F32)[: RUNS + LAYERS],
    )
    from_left = jnp.where(gy > 0, from_left, 0.0)
    from_right = jnp.where(gy < last_y, from_right, 0.0)
    to_left = dn[...] + from_left
    to_right = up[...] + from_right
    for q in range(4):
        cut = 32 * q + 16
        turned = field[q * RUNS : (q + 1) * RUNS, :]
        turned = turned + jnp.where((at >= cut) & (at < cut + 16), from_left[:RUNS], 0.0)
        turned = turned + jnp.where((at >= cut - 16) & (at < cut), from_right[:RUNS], 0.0)
        precond[pl.ds(q, RUNS, stride=4), :] = turn(turned, -cut)
        edges = jnp.where(at == cut - 1, to_left[:RUNS], to_right[:RUNS])
        side[pl.ds(q, RUNS, stride=4), :] = turn(edges, -cut)
    at = lanes(LAYERS)
    rim_left, rim_right = from_left[RUNS:], from_right[RUNS:]
    over = rim[:LAYERS, :]
    over = over + jnp.where(at >= 112, rim_left, 0.0)
    over = turn(over + jnp.where((at >= 96) & (at < 112), rim_right, 0.0), -112)
    under = rim[LAYERS:, :]
    under = under + jnp.where((at >= 16) & (at < 32), rim_left, 0.0)
    under = turn(under + jnp.where(at < 16, rim_right, 0.0), -16)
    at = lanes(ROWS)
    row = lax.broadcasted_iota(jnp.int32, (ROWS, COLS), 0)
    totals = [jnp.zeros((8, COLS), F32) for _ in range(5)]
    for level in range(LAYERS):
        cut = slice(level * ROWS, (level + 1) * ROWS)
        own = precond[cut, :]
        aside = side[cut, :]
        result = total[cut, :] * own
        result = result - faces[0, cut, :] * turn(jnp.where(at == COLS - 1, aside, own), 1)
        result = result - faces[1, cut, :] * turn(jnp.where(at == 0, aside, own), -1)
        result = result - faces[2, cut, :] * jnp.where(
            row == 0, over[level : level + 1, :], pltpu.roll(own, 1, 0)
        )
        result = result - faces[3, cut, :] * jnp.where(
            row == ROWS - 1, under[level : level + 1, :], pltpu.roll(own, ROWS - 1, 0)
        )
        if level > 0:
            back = slice((level - 1) * ROWS, level * ROWS)
            result = result - above[back, :] * precond[back, :]
        if level < LAYERS - 1:
            ahead = slice((level + 1) * ROWS, (level + 2) * ROWS)
            result = result - above[cut, :] * precond[ahead, :]
        image[cut, :] = result
        for j in range(5):
            product = (basis[j, cut, :] if j < 4 else result) * result
            totals[j] = totals[j] + (product[:8] + product[8:])
    totals += [gram[8 * slot : 8 * slot + 8, :] for slot in range(10)]
    totals.append(jnp.zeros((8, COLS), F32))
    rows = jnp.concatenate([jnp.sum(part, axis=0, keepdims=True) for part in totals], axis=0)
    column = jnp.sum(rows, axis=1, keepdims=True)
    keep = lanes(ROWS) == lax.broadcasted_iota(jnp.int32, (ROWS, COLS), 0)
    line = jnp.sum(jnp.where(keep, column, 0.0), axis=0, keepdims=True)
    sums[...] = jnp.broadcast_to(line, sums.shape)


def next_kernel(gathered, image, basis, out, hessenberg):
    cells = float(CELLS * COLS * lax.axis_size("gx") * lax.axis_size("gy"))
    line = jnp.sum(gathered[...], axis=0, keepdims=True) / cells
    entry = [line[:, i : i + 1] for i in range(15)]
    project = entry[:4]
    square = entry[4]
    for j in range(4):
        square = square - 2.0 * project[j] * project[j]
    slot = 5
    for i in range(4):
        for j in range(i, 4):
            square = square + (1.0 if i == j else 2.0) * project[i] * project[j] * entry[slot]
            slot += 1
    length = jnp.sqrt(jnp.maximum(square, 0.0) + EPS)
    at = lanes(1)
    found = jnp.where(at == 4, length, jnp.where(at < 4, line, 0.0))
    for i in range(5):
        hessenberg[i] = found[0, i]
    inverse = 1.0 / length
    scaled = [project[j] * inverse for j in range(4)]
    for level in range(LAYERS):
        cut = slice(level * ROWS, (level + 1) * ROWS)
        value = image[cut, :] * inverse
        for j in range(4):
            value = value - scaled[j] * basis[j, cut, :]
        out[cut, :] = value


def swap(values, partner):
    across, along = lax.axis_size("gx"), lax.axis_size("gy")
    pairs = []
    for a in range(across):
        for b in range(along):
            c, d = partner(a, b)
            if not 0 <= d < along:
                c, d = a ^ 1, b
            if not 0 <= c < across:
                c, d = a, b ^ 1
            pairs.append((a * along + b, c * along + d))
    return lax.ppermute(values, ("gx", "gy"), pairs)


def swap_y(first, second):
    from_second = swap(second, lambda a, b: (a, ((b + 1) ^ 1) - 1))
    return swap(first, lambda a, b: (a, b ^ 1)), from_second


def swap_x_first(values):
    return swap(values, lambda a, b: (a ^ 1, b))


def swap_x_second(values):
    return swap(values, lambda a, b: (((a + 1) ^ 1) - 1, b))


def swap_far(first, second):
    from_second = swap(second, lambda a, b: (((a + 2) ^ 2) - 2, b))
    return swap(first, lambda a, b: (a ^ 2, b)), from_second


def exchange(lines):
    size = lines.shape[0]
    out = lax.all_to_all(lines.reshape(size, 1, COLS), ("gx", "gy"), 0, 0)
    return out.reshape(size, COLS)


def on_device(basis, soil, frozen, soil_table, coarse_basis, coarse_inverse, active_count):
    basis = basis.reshape(4, CELLS, COLS)
    soil, frozen = soil.reshape(CELLS, COLS), frozen.reshape(CELLS, COLS)
    source = pltpu.with_memory_space_constraint(coarse_basis.reshape(K, -1), pltpu.HBM)
    devices = lax.axis_size("gx") * lax.axis_size("gy")
    field_space = pltpu.VMEM((CELLS, COLS), F32)
    kinds = pltpu.VMEM((CELLS, COLS), jnp.int32)
    basis, soil, frozen = (
        pltpu.with_memory_space_constraint(x, pltpu.HBM) for x in (basis, soil, frozen)
    )
    first, second, flat, kinds_x, current, code = call(
        pack_kernel,
        [
            shape(RUNS, COLS, dtype=BF16),
            shape(RUNS, COLS, dtype=BF16),
            shape(FLAT, COLS, dtype=BF16),
            shape(2, PAD - FLAT, COLS),
            pltpu.VMEM((CELLS, COLS), F32),
            pltpu.VMEM((CELLS, COLS), F32),
        ],
        [HB] * 3,
        (basis, soil, frozen),
        [kinds, kinds, pltpu.SemaphoreType.DMA((3,))],
        out_specs=[VM] * 6,
        name="pack",
    )
    from_y = swap_y(first, second)
    early, conduct, diagonal, above, local = call(
        early_kernel,
        [pltpu.VMEM((K, EARLY * WINDOW), BF16)] + [shape(CELLS, COLS)] * 4,
        [HB, HB, VM, VM],
        (source, pltpu.with_memory_space_constraint(soil_table, pltpu.HBM), current, code),
        [
            field_space,
            field_space,
            pltpu.SMEM((4, 8), F32),
            pltpu.SemaphoreType.DMA((2,)),
        ],
        out_specs=[VM] * 5,
        moved=10_000_000,
        name="early",
    )
    early, flat = lax.optimization_barrier((early, flat))
    flat, second = call(
        flat_kernel, [shape(PAD, COLS, dtype=BF16)] * 2, [VM] * 4, (flat, kinds_x, *from_y), name="flat"
    )
    from_second = swap_x_second(second)
    from_x = swap_x_first(flat), from_second
    late, basis, begun, gram = call(
        load_kernel,
        [
            pltpu.VMEM((K, (LAYERS - EARLY) * WINDOW), BF16),
            pltpu.VMEM((4, CELLS, COLS), F32),
            shape(K, COLS),
            shape(80, COLS),
        ],
        [HB, HB, VM, VM],
        (source, basis, early, flat),
        [
            pltpu.VMEM((FLAT, COLS), F32),
            pltpu.SemaphoreType.DMA(((LAYERS - EARLY) // CHUNK + 1,)),
        ],
        out_specs=[VM] * 4,
        flops=16_000_000,
        moved=20_000_000,
        name="load",
    )
    vector = pltpu.VMEM((FLAT, COLS), F32)
    begun = call(
        first_rhs_kernel,
        shape(K, COLS),
        [VM] * 4,
        (early, late, begun, from_x[0]),
        [vector],
        flops=6_000_000,
        moved=6_000_000,
        name="first_rhs",
    )
    lines = call(
        second_rhs_kernel,
        shape(devices, COLS),
        [VM] * 5,
        (early, late, begun, from_x[1], active_count),
        [vector],
        flops=6_000_000,
        moved=6_000_000,
        name="second_rhs",
    )
    gathered = exchange(lines)
    message = shape(ENDS, COLS, dtype=BF16)
    ends = pltpu.VMEM((2 * LAYERS, COLS), F32)
    weights, first, near_first, far = call(
        first_spread_kernel,
        [shape(K, COLS), message, shape(80, COLS), shape(80, COLS)],
        [VM] * 6,
        (early, late, coarse_inverse, gathered, active_count, local),
        [pltpu.VMEM((K, COLS), F32), vector, ends],
        flops=20_000_000,
        moved=8_000_000,
        name="first_spread",
    )
    from_first = swap_x_first(first)
    second, near_second, far_first, far_second = call(
        second_spread_kernel,
        [message, shape(80, COLS)] + [shape(80, COLS, dtype=BF16)] * 2,
        [VM] * 5,
        (early, late, weights, local, far),
        [vector, ends],
        flops=20_000_000,
        moved=8_000_000,
        name="second_spread",
    )
    near = from_first, swap_x_second(second)
    far = swap_far(far_first, far_second)
    own = call(
        own_spread_kernel,
        shape(FLAT, COLS),
        [VM] * 3,
        (early, late, weights),
        flops=20_000_000,
        moved=7_000_000,
        name="own_spread",
    )
    conduct, diagonal, weights = lax.optimization_barrier((conduct, diagonal, weights))
    faces, total = call(
        faces_kernel,
        [shape(4, CELLS, COLS), shape(CELLS, COLS)],
        [VM, VM, SM, VM, VM, VM, VM],
        (conduct, diagonal, soil_table, *from_y, *from_x),
        [field_space],
        flops=4_000_000,
        moved=2_000_000,
        name="faces",
    )
    field, rim, up, dn, first, second = call(
        fold_rows_kernel,
        [shape(CELLS, COLS), shape(80, COLS)]
        + [shape(RUNS + LAYERS, COLS)] * 2
        + [shape(SIDE, COLS, dtype=BF16)] * 2,
        [VM] * 8,
        (own, near_first, near_second, local, *near, far[1], far[0]),
        name="fold_rows",
    )
    from_y = swap_y(first, second)
    precond, image, sums = call(
        image_kernel,
        [shape(CELLS, COLS), shape(CELLS, COLS), shape(devices, COLS)],
        [VM] * 11,
        (field, rim, up, dn, *from_y, basis, faces, total, above, gram),
        [field_space],
        name="image",
    )
    gathered = exchange(sums)
    following, hessenberg = call(
        next_kernel,
        [shape(CELLS, COLS), shape(5)],
        [VM] * 3,
        (gathered, image, basis),
        out_specs=[VM, SM],
        name="next",
    )
    tile = (LAYERS, ROWS, COLS)
    return precond.reshape(tile), following.reshape(tile), hessenberg


def solution(mesh):
    placed = (
        P(None, None, "gx", "gy"),
        P(None, "gx", "gy"),
        P(None, "gx", "gy"),
        P(),
        P("gx", "gy", None, None),
        P(("gx", "gy"), None),
        P("gx", "gy"),
    )
    return jax.shard_map(
        on_device,
        mesh=mesh,
        in_specs=placed,
        out_specs=(P(None, "gx", "gy"), P(None, "gx", "gy"), P()),
        check_vma=False,
    )
```

```python
import functools

import jax
import jax.numpy as jnp
from jax import lax
from jax.experimental import pallas as pl
from jax.experimental.pallas import tpu as pltpu
from jax.sharding import PartitionSpec as P

F32 = jnp.float32
BF16 = jnp.bfloat16

LAYERS, ROWS, COLS, OV, K = 40, 16, 128, 16, 32
CELLS = LAYERS * ROWS
RUNS = CELLS // 4
FLAT = 5 * RUNS
WINDOW = 7680
EARLY = 8
CHUNK = 16
PAD = FLAT + 48
SIDE = RUNS + 48
ENDS = FLAT + 80
PART = 2560
WEIGHT_V, WEIGHT_H, EPS = 4.0, 1.0, 1e-06

VM = pl.BlockSpec(memory_space=pltpu.VMEM)
SM = pl.BlockSpec(memory_space=pltpu.SMEM)
HB = pl.BlockSpec(memory_space=pltpu.HBM)


def shape(*dims, dtype=F32):
    return jax.ShapeDtypeStruct(dims, dtype)


def call(kernel, outs, specs, args, scratch=(), out_specs=None, flops=0, moved=0, name=None):
    return pl.pallas_call(
        kernel,
        out_shape=outs,
        in_specs=specs,
        out_specs=out_specs if out_specs is not None else jax.tree.map(lambda _: VM, outs),
        scratch_shapes=list(scratch),
        compiler_params=pltpu.CompilerParams(vmem_limit_bytes=16 * 2**20),
        cost_estimate=pl.CostEstimate(flops=flops, bytes_accessed=moved, transcendentals=0),
        name=name,
    )(*args)


def lanes(rows):
    return lax.broadcasted_iota(jnp.int32, (rows, COLS), 1)


def harmonic(first, second):
    return 2.0 * first * second / (first + second)


def steps(count):
    return max(n for n in range(1, 9) if count % n == 0)


def turn(values, amount):
    return pltpu.roll(values, amount % COLS, 1)


def pack_kernel(
    basis_in,
    soil_in,
    frozen_in,
    first,
    second,
    flat,
    kinds,
    basis,
    code,
    soil,
    frozen,
    arrived,
):
    copies = [
        pltpu.make_async_copy(basis_in.at[3], basis, arrived.at[0]),
        pltpu.make_async_copy(soil_in, soil, arrived.at[1]),
        pltpu.make_async_copy(frozen_in, frozen, arrived.at[2]),
    ]
    for copy in copies:
        copy.start()
    for copy in copies:
        copy.wait()
    code[...] = (soil[...] + 8 * frozen[...]).astype(F32)
    at = lanes(RUNS)
    to_up = jnp.zeros((RUNS, COLS), F32)
    to_dn = to_up
    flats = [jnp.zeros((RUNS, COLS), F32) for _ in range(5)]
    for q in range(4):
        cut = 32 * q + 16
        turned = turn(basis[pl.ds(q, RUNS, stride=4), :], cut)
        kind = code[pl.ds(q, RUNS, stride=4), :]
        low = (at >= cut - 16) & (at < cut)
        high = (at >= cut) & (at < cut + 16)
        to_up = jnp.where(low, turned, jnp.where(at == cut, turn(kind, cut + 1), to_up))
        to_dn = jnp.where(high, turned, jnp.where(at == cut - 1, turn(kind, cut - 1), to_dn))
        flats[q] = jnp.where(at >= cut, turned, flats[q])
        flats[q + 1] = jnp.where(at < cut, turned, flats[q + 1])
    even = lax.axis_index("gy") % 2 == 0
    first[...] = jnp.where(even, to_up, to_dn).astype(BF16)
    second[...] = jnp.where(even, to_dn, to_up).astype(BF16)
    for j in range(5):
        flat[j * RUNS : (j + 1) * RUNS, :] = flats[j].astype(BF16)
    spare = jnp.zeros((PAD - FLAT - LAYERS, COLS), F32)
    for index, row in enumerate((0, ROWS - 1)):
        line = jnp.concatenate([code[pl.ds(row, LAYERS, stride=ROWS), :], spare], axis=0)
        kinds[index] = line


def sides(even, first, second):
    return jnp.where(even, second, first), jnp.where(even, first, second)


def flat_kernel(own, kinds, from_first, from_second, first, second):
    place = lax.axis_index("gy")
    last = lax.axis_size("gy") - 1
    at = lanes(RUNS)
    from_left, from_right = sides(
        place % 2 == 0, from_first[...].astype(F32), from_second[...].astype(F32)
    )
    from_left = jnp.where(place > 0, from_left, 0.0)
    from_right = jnp.where(place < last, from_right, 0.0)
    for j in range(5):
        part = own[j * RUNS : (j + 1) * RUNS, :].astype(F32)
        if j < 4:
            part = jnp.where((at >= 32 * j) & (at < 32 * j + 16), from_left, part)
        if j > 0:
            part = jnp.where((at >= 32 * j - 16) & (at < 32 * j), from_right, part)
        first[j * RUNS : (j + 1) * RUNS, :] = part.astype(BF16)
        second[j * RUNS : (j + 1) * RUNS, :] = part.astype(BF16)
    even = lax.axis_index("gx") % 2 == 0
    first[FLAT:, :] = jnp.where(even, kinds[1], kinds[0]).astype(BF16)
    second[FLAT:, :] = jnp.where(even, kinds[0], kinds[1]).astype(BF16)


def project_part(coarse, vector, part, totals, first, begin, count):
    def body(layer, totals):
        totals = list(totals)
        base = pl.multiple_of((begin + layer) * WINDOW + part * PART, 128)
        row = (first + begin + layer) * 4
        wide = jnp.concatenate(
            [
                jnp.broadcast_to(vector[pl.ds(j * RUNS + row + m, 1), :], (8, COLS))
                for m in range(4)
                for j in range(5)
            ],
            axis=1,
        )
        for r in range(4):
            product = coarse[8 * r : 8 * r + 8, pl.ds(base, PART)].astype(F32) * wide
            for t in range(20):
                slot = 2 * r + t % 2
                totals[slot] = totals[slot] + product[:, t * COLS : (t + 1) * COLS]
        return tuple(totals)

    return lax.fori_loop(0, count, body, totals, unroll=steps(count))


def early_kernel(
    source,
    table_in,
    basis,
    code,
    out,
    conduct,
    diagonal,
    above,
    local,
    ratio,
    value,
    table,
    arrived,
):
    small = pltpu.make_async_copy(table_in, table, arrived.at[0])
    small.start()
    copy = pltpu.make_async_copy(source.at[:, : EARLY * WINDOW], out, arrived.at[1])
    copy.start()
    small.wait()
    solve_columns(basis, code, table, conduct, diagonal, above, local, ratio, value)
    copy.wait()


def multiply_out(basis, gram):
    def body(level, grams):
        grams = list(grams)
        cut = pl.ds(pl.multiple_of(level * ROWS, ROWS), ROWS)
        vectors = [basis[j, cut, :] for j in range(4)]
        slot = 0
        for i in range(4):
            for j in range(i, 4):
                square = vectors[i] * vectors[j]
                grams[slot] = grams[slot] + (square[:8] + square[8:])
                slot += 1
        return tuple(grams)

    zero = jnp.zeros((8, COLS), F32)
    grams = lax.fori_loop(0, LAYERS, body, (zero,) * 10, unroll=4)
    for slot in range(10):
        gram[8 * slot : 8 * slot + 8, :] = grams[slot]


def load_kernel(source, early, own, late, begun, vector, arrived):
    copies = []
    for index in range((LAYERS - EARLY) // CHUNK):
        begin, size = index * CHUNK * WINDOW, CHUNK * WINDOW
        copies.append(
            pltpu.make_async_copy(
                source.at[:, EARLY * WINDOW + begin : EARLY * WINDOW + begin + size],
                late.at[:, begin : begin + size],
                arrived.at[index],
            )
        )
    for copy in copies:
        copy.start()
    vector[...] = own[:FLAT, :].astype(F32)
    totals = (jnp.zeros((8, COLS), F32),) * 8
    totals = project_part(early, vector, 1, totals, 0, 0, EARLY)
    for index, copy in enumerate(copies):
        copy.wait()
        totals = project_part(late, vector, 1, totals, EARLY, index * CHUNK, CHUNK)
    for r in range(4):
        begun[8 * r : 8 * r + 8, :] = totals[2 * r] + totals[2 * r + 1]


def project_neighbour(early, late, whole, vector, upper, valid, totals):
    vector[...] = jnp.where(valid, whole[:FLAT, :].astype(F32), 0.0)
    part = jnp.where(upper, 2, 0)
    totals = project_part(early, vector, part, totals, 0, 0, EARLY)
    return project_part(late, vector, part, totals, EARLY, 0, LAYERS - EARLY)


def unfold(begun):
    zero = jnp.zeros((8, COLS), F32)
    return tuple(begun[4 * s : 4 * s + 8, :] if s % 2 == 0 else zero for s in range(8))


def first_rhs_kernel(early, late, begun, whole, out, vector):
    upper = lax.axis_index("gx") % 2 == 0
    totals = project_neighbour(early, late, whole, vector, upper, True, unfold(begun))
    for r in range(4):
        out[8 * r : 8 * r + 8, :] = totals[2 * r] + totals[2 * r + 1]


def second_rhs_kernel(early, late, begun, whole, count, out, vector):
    place = lax.axis_index("gx")
    valid = (place > 0) & (place < lax.axis_size("gx") - 1)
    totals = project_neighbour(early, late, whole, vector, place % 2 == 1, valid, unfold(begun))
    full = jnp.concatenate([totals[2 * r] + totals[2 * r + 1] for r in range(4)], axis=0)
    sums = jnp.sum(full, axis=1, keepdims=True)
    index = lax.broadcasted_iota(jnp.int32, (K, COLS), 0)
    keep = (lanes(K) % K == index) & (index < count[...])
    row = jnp.sum(jnp.where(keep, sums, 0.0), axis=0, keepdims=True)
    out[...] = jnp.broadcast_to(row, out.shape)


def reduce_eight(parts, where):
    four, two, one = where

    def merge(a, b, mask, step):
        kept = jnp.where(mask, a, b)
        moved = jnp.where(mask, b, a)
        if step == 4:
            return kept + pltpu.roll(moved, 4, 0)
        return kept + jnp.where(mask, pltpu.roll(moved, 8 - step, 0), pltpu.roll(moved, step, 0))

    parts = [merge(parts[t], parts[t + 4], four, 4) for t in range(4)]
    parts = [merge(parts[t], parts[t + 2], two, 2) for t in range(2)]
    return merge(parts[0], parts[1], one, 1)


def reduction_masks():
    row = lax.broadcasted_iota(jnp.int32, (8, COLS), 0)
    return row < 4, row % 4 < 2, row % 2 < 1


def combine(coarse, base, width, weights):
    terms = [
        coarse[8 * r : 8 * r + 8, pl.ds(base, width)].astype(F32) * weights[r][:, :width]
        for r in range(4)
    ]
    return (terms[0] + terms[1]) + (terms[2] + terms[3])


def spread_part(coarse, weights, part, out, first, count):
    where = reduction_masks()

    def body(pair, carry):
        halves = []
        for half in range(2):
            base = pl.multiple_of((2 * pair + half) * WINDOW + part * PART, 128)
            halves.append(combine(coarse, base, PART, weights))
        for j in range(5):
            tiles = [
                halves[half][:, (5 * m + j) * COLS : (5 * m + j + 1) * COLS]
                for half in range(2)
                for m in range(4)
            ]
            start = pl.multiple_of(j * RUNS + 4 * first + 8 * pair, 8)
            out[pl.ds(start, 8), :] = reduce_eight(tiles, where)
        return carry

    lax.fori_loop(0, count // 2, body, 0, unroll=steps(count // 2))


def spread_ends(coarse, weights, begin, out, first, count):
    where = reduction_masks()

    def body(four, carry):
        tiles = []
        for layer in range(4):
            base = (4 * four + layer) * WINDOW + PART + begin
            both = combine(coarse, pl.multiple_of(base, 128), 2 * COLS, weights)
            tiles += [both[:, :COLS], both[:, COLS:]]
        start = pl.multiple_of(2 * first + 8 * four, 8)
        out[pl.ds(start, 8), :] = reduce_eight(tiles, where)
        return carry

    lax.fori_loop(0, count // 4, body, 0, unroll=steps(count // 4))


def widen(weights):
    return [
        jnp.concatenate([weights[8 * r : 8 * r + 8, :]] * (PART // COLS), axis=1) for r in range(4)
    ]


def solve(inverse, gathered, count, rhs):
    at = lanes(K)
    rows = jnp.zeros((K, COLS), F32)
    for e in range(4):
        rows = jnp.where(at // K == e, gathered[pl.ds(e, K, stride=4), :], rows)
    rhs[...] = rows
    total = jnp.zeros((K, COLS), F32)
    for i in range(K):
        total = total + inverse[:, i * COLS : (i + 1) * COLS] * rhs[i : i + 1, :]
    solved = jnp.sum(total, axis=1, keepdims=True)
    index = lax.broadcasted_iota(jnp.int32, (K, COLS), 0)
    return jnp.where(index < count[...], solved, 0.0).astype(BF16).astype(F32)


def spread_to(upper, early, late, solved, local, message, near, whole, ends):
    wide = widen(solved)
    part, begin = jnp.where(upper, 2, 0), jnp.where(upper, 18 * COLS, 0)
    for coarse, start, size in ((early, 0, EARLY), (late, EARLY, LAYERS - EARLY)):
        spread_part(coarse, wide, part, whole, start, size)
        spread_ends(coarse, wide, begin, ends, start, size)
    message[:FLAT, :] = whole[...].astype(BF16)

    def strip(ref, j, m):
        return ref[pl.ds(j * RUNS + m, LAYERS, stride=4), :]

    def both(first, second):
        return jnp.concatenate([first, second], axis=0)

    at = lanes(LAYERS)
    cut = jnp.where(upper, 112, 16)
    row = jnp.where(upper, strip(local, 3, 3), strip(local, 0, 0))
    ours = [ends[pl.ds(index, LAYERS, stride=2), :] for index in range(2)]
    message[FLAT:, :] = both(
        ours[0] + jnp.where(at >= cut, row, 0.0), ours[1] + jnp.where(at < cut, row, 0.0)
    ).astype(BF16)
    top = both(strip(whole, 0, 0), strip(whole, 1, 0))
    bottom = both(strip(whole, 3, 3), strip(whole, 4, 3))
    near[...] = jnp.where(upper, top, bottom)
    return jnp.where(upper, bottom, top)


def first_spread_kernel(
    early, late, inverse, gathered, count, local, weights, message, near, far, rhs, whole, ends
):
    solved = solve(inverse, gathered, count, rhs)
    weights[...] = solved
    upper = lax.axis_index("gx") % 2 == 0
    far[...] = spread_to(upper, early, late, solved, local, message, near, whole, ends)


def second_spread_kernel(
    early, late, weights, local, far, message, near, far_first, far_second, whole, ends
):
    place = lax.axis_index("gx")
    upper = place % 2 == 1
    own = spread_to(upper, early, late, weights[...], local, message, near, whole, ends)
    swapped = (place % 4 == 1) | (place % 4 == 2)
    far_first[...] = jnp.where(swapped, own, far[...]).astype(BF16)
    far_second[...] = jnp.where(swapped, far[...], own).astype(BF16)


def own_spread_kernel(early, late, weights, basis_in, own, basis, gram, ready):
    copy = pltpu.make_async_copy(basis_in, basis, ready)
    copy.start()
    wide = widen(weights[...])
    spread_part(early, wide, 1, own, 0, EARLY)
    spread_part(late, wide, 1, own, EARLY, LAYERS - EARLY)
    copy.wait()
    multiply_out(basis, gram)


def fold_rows_kernel(
    own,
    near_first,
    near_second,
    local,
    from_first,
    from_second,
    far_second,
    far_first,
    field,
    rim,
    up,
    dn,
    first,
    second,
):
    place = lax.axis_index("gx")
    last = lax.axis_size("gx") - 1
    even, lower = place % 2 == 0, place % 4 < 2
    at = lanes(RUNS)
    whole = []
    for j in range(5):
        cut = slice(j * RUNS, (j + 1) * RUNS)
        before, after = sides(even, from_first[cut, :].astype(F32), from_second[cut, :].astype(F32))
        part = own[cut, :] + jnp.where(place > 0, before, 0.0)
        part = part + jnp.where(place < last, after, 0.0)
        if j < 4:
            part = part + jnp.where(at >= 32 * j + 16, local[cut, :], 0.0)
        if j > 0:
            behind = local[(j - 1) * RUNS : j * RUNS, :]
            part = part + jnp.where(at < 32 * j - 16, behind, 0.0)
        whole.append(part)
    to_up = jnp.zeros((RUNS, COLS), F32)
    to_dn = to_up
    for q in range(4):
        field[q * RUNS : (q + 1) * RUNS, :] = jnp.where(
            at >= 32 * q + 16, whole[q], whole[q + 1]
        )
        band = (at >= 32 * q) & (at < 32 * q + 32)
        to_up = jnp.where(band, whole[q + 1], to_up)
        to_dn = jnp.where(band, whole[q], to_dn)
    up[:RUNS, :] = to_up
    dn[:RUNS, :] = to_dn

    before, after = sides(even, from_first[FLAT:, :].astype(F32), from_second[FLAT:, :].astype(F32))
    before2, after2 = sides(lower, far_first[...].astype(F32), far_second[...].astype(F32))
    near_before, near_after = sides(even, near_first[...], near_second[...])
    top = near_before + before + jnp.where(place > 1, before2, 0.0)
    bottom = near_after + after + jnp.where(place < last - 1, after2, 0.0)
    at = lanes(LAYERS)
    half = LAYERS
    rim[:half, :] = jnp.where(at >= 112, top[:half], top[half:])
    rim[half:, :] = jnp.where(at >= 16, bottom[:half], bottom[half:])
    up[RUNS:, :] = jnp.where(at >= 96, top[half:], bottom[half:])
    dn[RUNS:, :] = jnp.where(at >= 96, top[:half], bottom[:half])
    even = lax.axis_index("gy") % 2 == 0
    spare = jnp.zeros((SIDE - RUNS - LAYERS, COLS), F32)
    to_up = jnp.concatenate([up[...], spare], axis=0)
    to_dn = jnp.concatenate([dn[...], spare], axis=0)
    first[...] = jnp.where(even, to_up, to_dn).astype(BF16)
    second[...] = jnp.where(even, to_dn, to_up).astype(BF16)


def look_up(kind, table, rows):
    value = jnp.zeros(kind.shape, F32)
    for index in range(8):
        value = jnp.where(kind == index, table[rows[0], index], value)
        value = jnp.where(kind == index + 8, table[rows[1], index], value)
    return value


def solve_columns(basis, code, table, conduct, diagonal, above, local, ratio, value):
    def body(index, carry):
        cut = pl.ds(pl.multiple_of(index * 160, 160), 160)
        kind = code[cut, :]
        conduct[cut, :] = look_up(kind, table, (0, 1))
        diagonal[cut, :] = look_up(kind, table, (2, 3))
        return carry

    lax.fori_loop(0, CELLS // 160, body, 0)
    zero = jnp.zeros((ROWS, COLS), F32)
    below = zero
    last_ratio = zero
    last_value = zero
    for level in range(LAYERS):
        cut = slice(level * ROWS, (level + 1) * ROWS)
        own = conduct[cut, :]
        over = zero
        if level < LAYERS - 1:
            over = WEIGHT_V * harmonic(own, conduct[(level + 1) * ROWS : (level + 2) * ROWS, :])
        above[cut, :] = over
        sides = diagonal[cut, :] + below + over
        diagonal[cut, :] = sides
        denom = sides + 4.0 * WEIGHT_H * own + below * last_ratio
        inverse = 1.0 / denom
        last_ratio = -over * inverse
        last_value = (basis[cut, :] + below * last_value) * inverse
        ratio[cut, :] = last_ratio
        value[cut, :] = last_value
        below = over
    for level in range(LAYERS - 2, -1, -1):
        cut = slice(level * ROWS, (level + 1) * ROWS)
        last_value = value[cut, :] - ratio[cut, :] * last_value
        value[cut, :] = last_value
    for q in range(4):
        local[q * RUNS : (q + 1) * RUNS, :] = turn(value[pl.ds(q, RUNS, stride=4), :], 32 * q + 16)


def faces_kernel(
    conduct,
    diagonal,
    table,
    first_y,
    second_y,
    first_x,
    second_x,
    faces,
    total,
    side,
):
    gx, gy = lax.axis_index("gx"), lax.axis_index("gy")
    last_x, last_y = lax.axis_size("gx") - 1, lax.axis_size("gy") - 1
    at = lanes(RUNS)
    from_left, from_right = sides(
        gy % 2 == 0, first_y[...].astype(F32), second_y[...].astype(F32)
    )
    kinds = jnp.zeros((RUNS, COLS), F32)
    for q in range(4):
        kinds = jnp.where(at == 32 * q + 16, from_left, kinds)
        kinds = jnp.where(at == 32 * q + 15, from_right, kinds)
    known = look_up(kinds.astype(jnp.int32), table, (0, 1))
    for q in range(4):
        side[pl.ds(q, RUNS, stride=4), :] = turn(known, -(32 * q + 16))
    before, after = sides(
        gx % 2 == 0, first_x[FLAT:, :].astype(F32), second_x[FLAT:, :].astype(F32)
    )
    row_before = look_up(before.astype(jnp.int32), table, (0, 1))
    row_after = look_up(after.astype(jnp.int32), table, (0, 1))
    at = lanes(ROWS)
    row = lax.broadcasted_iota(jnp.int32, (ROWS, COLS), 0)
    for level in range(LAYERS):
        cut = slice(level * ROWS, (level + 1) * ROWS)
        own = conduct[cut, :]
        aside = side[cut, :]
        over = row_before[level : level + 1, :]
        under = row_after[level : level + 1, :]
        weights = [
            jnp.where((at > 0) | (gy > 0), harmonic(own, jnp.where(at == 0, aside, turn(own, 1))), 0.0),
            jnp.where(
                (at < COLS - 1) | (gy < last_y),
                harmonic(own, jnp.where(at == COLS - 1, aside, turn(own, -1))),
                0.0,
            ),
            jnp.where(
                (row > 0) | (gx > 0),
                harmonic(own, jnp.where(row == 0, over, pltpu.roll(own, 1, 0))),
                0.0,
            ),
            jnp.where(
                (row < ROWS - 1) | (gx < last_x),
                harmonic(own, jnp.where(row == ROWS - 1, under, pltpu.roll(own, ROWS - 1, 0))),
                0.0,
            ),
        ]
        for index in range(4):
            faces[index, cut, :] = WEIGHT_H * weights[index]
        total[cut, :] = diagonal[cut, :] + WEIGHT_H * (
            (weights[0] + weights[1]) + (weights[2] + weights[3])
        )


def image_kernel(
    field,
    rim,
    up,
    dn,
    from_first,
    from_second,
    basis,
    faces,
    total,
    above,
    gram,
    precond,
    image,
    sums,
    side,
):
    gy = lax.axis_index("gy")
    last_y = lax.axis_size("gy") - 1
    at = lanes(RUNS)
    from_left, from_right = sides(
        gy % 2 == 0,
        from_first[...].astype(F32)[: RUNS + LAYERS],
        from_second[...].astype(F32)[: RUNS + LAYERS],
    )
    from_left = jnp.where(gy > 0, from_left, 0.0)
    from_right = jnp.where(gy < last_y, from_right, 0.0)
    to_left = dn[...] + from_left
    to_right = up[...] + from_right
    for q in range(4):
        cut = 32 * q + 16
        turned = field[q * RUNS : (q + 1) * RUNS, :]
        turned = turned + jnp.where((at >= cut) & (at < cut + 16), from_left[:RUNS], 0.0)
        turned = turned + jnp.where((at >= cut - 16) & (at < cut), from_right[:RUNS], 0.0)
        precond[pl.ds(q, RUNS, stride=4), :] = turn(turned, -cut)
        edges = jnp.where(at == cut - 1, to_left[:RUNS], to_right[:RUNS])
        side[pl.ds(q, RUNS, stride=4), :] = turn(edges, -cut)
    at = lanes(LAYERS)
    rim_left, rim_right = from_left[RUNS:], from_right[RUNS:]
    over = rim[:LAYERS, :]
    over = over + jnp.where(at >= 112, rim_left, 0.0)
    over = turn(over + jnp.where((at >= 96) & (at < 112), rim_right, 0.0), -112)
    under = rim[LAYERS:, :]
    under = under + jnp.where((at >= 16) & (at < 32), rim_left, 0.0)
    under = turn(under + jnp.where(at < 16, rim_right, 0.0), -16)
    at = lanes(ROWS)
    row = lax.broadcasted_iota(jnp.int32, (ROWS, COLS), 0)
    totals = [jnp.zeros((8, COLS), F32) for _ in range(5)]
    for level in range(LAYERS):
        cut = slice(level * ROWS, (level + 1) * ROWS)
        own = precond[cut, :]
        aside = side[cut, :]
        result = total[cut, :] * own
        result = result - faces[0, cut, :] * turn(jnp.where(at == COLS - 1, aside, own), 1)
        result = result - faces[1, cut, :] * turn(jnp.where(at == 0, aside, own), -1)
        result = result - faces[2, cut, :] * jnp.where(
            row == 0, over[level : level + 1, :], pltpu.roll(own, 1, 0)
        )
        result = result - faces[3, cut, :] * jnp.where(
            row == ROWS - 1, under[level : level + 1, :], pltpu.roll(own, ROWS - 1, 0)
        )
        if level > 0:
            back = slice((level - 1) * ROWS, level * ROWS)
            result = result - above[back, :] * precond[back, :]
        if level < LAYERS - 1:
            ahead = slice((level + 1) * ROWS, (level + 2) * ROWS)
            result = result - above[cut, :] * precond[ahead, :]
        image[cut, :] = result
        for j in range(5):
            product = (basis[j, cut, :] if j < 4 else result) * result
            totals[j] = totals[j] + (product[:8] + product[8:])
    totals += [gram[8 * slot : 8 * slot + 8, :] for slot in range(10)]
    totals.append(jnp.zeros((8, COLS), F32))
    rows = jnp.concatenate([jnp.sum(part, axis=0, keepdims=True) for part in totals], axis=0)
    column = jnp.sum(rows, axis=1, keepdims=True)
    keep = lanes(ROWS) == lax.broadcasted_iota(jnp.int32, (ROWS, COLS), 0)
    line = jnp.sum(jnp.where(keep, column, 0.0), axis=0, keepdims=True)
    sums[...] = jnp.broadcast_to(line, sums.shape)


def next_kernel(gathered, image, basis, out, hessenberg):
    cells = float(CELLS * COLS * lax.axis_size("gx") * lax.axis_size("gy"))
    line = jnp.sum(gathered[...], axis=0, keepdims=True) / cells
    entry = [line[:, i : i + 1] for i in range(15)]
    project = entry[:4]
    square = entry[4]
    for j in range(4):
        square = square - 2.0 * project[j] * project[j]
    slot = 5
    for i in range(4):
        for j in range(i, 4):
            square = square + (1.0 if i == j else 2.0) * project[i] * project[j] * entry[slot]
            slot += 1
    length = jnp.sqrt(jnp.maximum(square, 0.0) + EPS)
    at = lanes(1)
    found = jnp.where(at == 4, length, jnp.where(at < 4, line, 0.0))
    for i in range(5):
        hessenberg[i] = found[0, i]
    inverse = 1.0 / length
    scaled = [project[j] * inverse for j in range(4)]
    for level in range(LAYERS):
        cut = slice(level * ROWS, (level + 1) * ROWS)
        value = image[cut, :] * inverse
        for j in range(4):
            value = value - scaled[j] * basis[j, cut, :]
        out[cut, :] = value


def swap(values, partner):
    across, along = lax.axis_size("gx"), lax.axis_size("gy")
    pairs = []
    for a in range(across):
        for b in range(along):
            c, d = partner(a, b)
            if not 0 <= d < along:
                c, d = a ^ 1, b
            if not 0 <= c < across:
                c, d = a, b ^ 1
            pairs.append((a * along + b, c * along + d))
    return lax.ppermute(values, ("gx", "gy"), pairs)


def swap_y(first, second):
    from_second = swap(second, lambda a, b: (a, ((b + 1) ^ 1) - 1))
    return swap(first, lambda a, b: (a, b ^ 1)), from_second


def swap_x_first(values):
    return swap(values, lambda a, b: (a ^ 1, b))


def swap_x_second(values):
    return swap(values, lambda a, b: (((a + 1) ^ 1) - 1, b))


def swap_far(first, second):
    from_second = swap(second, lambda a, b: (((a + 2) ^ 2) - 2, b))
    return swap(first, lambda a, b: (a ^ 2, b)), from_second


def exchange(lines):
    size = lines.shape[0]
    out = lax.all_to_all(lines.reshape(size, 1, COLS), ("gx", "gy"), 0, 0)
    return out.reshape(size, COLS)


def on_device(basis, soil, frozen, soil_table, coarse_basis, coarse_inverse, active_count):
    basis = basis.reshape(4, CELLS, COLS)
    soil, frozen = soil.reshape(CELLS, COLS), frozen.reshape(CELLS, COLS)
    source = pltpu.with_memory_space_constraint(coarse_basis.reshape(K, -1), pltpu.HBM)
    devices = lax.axis_size("gx") * lax.axis_size("gy")
    field_space = pltpu.VMEM((CELLS, COLS), F32)
    kinds = pltpu.VMEM((CELLS, COLS), jnp.int32)
    basis, soil, frozen = (
        pltpu.with_memory_space_constraint(x, pltpu.HBM) for x in (basis, soil, frozen)
    )
    first, second, flat, kinds_x, current, code = call(
        pack_kernel,
        [
            shape(RUNS, COLS, dtype=BF16),
            shape(RUNS, COLS, dtype=BF16),
            shape(FLAT, COLS, dtype=BF16),
            shape(2, PAD - FLAT, COLS),
            pltpu.VMEM((CELLS, COLS), F32),
            pltpu.VMEM((CELLS, COLS), F32),
        ],
        [HB] * 3,
        (basis, soil, frozen),
        [kinds, kinds, pltpu.SemaphoreType.DMA((3,))],
        out_specs=[VM] * 6,
        name="pack",
    )
    from_y = swap_y(first, second)
    early, conduct, diagonal, above, local = call(
        early_kernel,
        [pltpu.VMEM((K, EARLY * WINDOW), BF16)] + [shape(CELLS, COLS)] * 4,
        [HB, HB, VM, VM],
        (source, pltpu.with_memory_space_constraint(soil_table, pltpu.HBM), current, code),
        [
            field_space,
            field_space,
            pltpu.SMEM((4, 8), F32),
            pltpu.SemaphoreType.DMA((2,)),
        ],
        out_specs=[VM] * 5,
        moved=10_000_000,
        name="early",
    )
    early, flat = lax.optimization_barrier((early, flat))
    flat, second = call(
        flat_kernel, [shape(PAD, COLS, dtype=BF16)] * 2, [VM] * 4, (flat, kinds_x, *from_y), name="flat"
    )
    from_second = swap_x_second(second)
    from_x = swap_x_first(flat), from_second
    late, begun = call(
        load_kernel,
        [
            pltpu.VMEM((K, (LAYERS - EARLY) * WINDOW), BF16),
            shape(K, COLS),
        ],
        [HB, VM, VM],
        (source, early, flat),
        [
            pltpu.VMEM((FLAT, COLS), F32),
            pltpu.SemaphoreType.DMA(((LAYERS - EARLY) // CHUNK,)),
        ],
        out_specs=[VM] * 2,
        flops=16_000_000,
        moved=20_000_000,
        name="load",
    )
    vector = pltpu.VMEM((FLAT, COLS), F32)
    begun = call(
        first_rhs_kernel,
        shape(K, COLS),
        [VM] * 4,
        (early, late, begun, from_x[0]),
        [vector],
        flops=6_000_000,
        moved=6_000_000,
        name="first_rhs",
    )
    lines = call(
        second_rhs_kernel,
        shape(devices, COLS),
        [VM] * 5,
        (early, late, begun, from_x[1], active_count),
        [vector],
        flops=6_000_000,
        moved=6_000_000,
        name="second_rhs",
    )
    gathered = exchange(lines)
    message = shape(ENDS, COLS, dtype=BF16)
    ends = pltpu.VMEM((2 * LAYERS, COLS), F32)
    weights, first, near_first, far = call(
        first_spread_kernel,
        [shape(K, COLS), message, shape(80, COLS), shape(80, COLS)],
        [VM] * 6,
        (early, late, coarse_inverse, gathered, active_count, local),
        [pltpu.VMEM((K, COLS), F32), vector, ends],
        flops=20_000_000,
        moved=8_000_000,
        name="first_spread",
    )
    from_first = swap_x_first(first)
    second, near_second, far_first, far_second = call(
        second_spread_kernel,
        [message, shape(80, COLS)] + [shape(80, COLS, dtype=BF16)] * 2,
        [VM] * 5,
        (early, late, weights, local, far),
        [vector, ends],
        flops=20_000_000,
        moved=8_000_000,
        name="second_spread",
    )
    near = from_first, swap_x_second(second)
    far = swap_far(far_first, far_second)
    own, basis, gram = call(
        own_spread_kernel,
        [shape(FLAT, COLS), pltpu.VMEM((4, CELLS, COLS), F32), shape(80, COLS)],
        [VM] * 3 + [HB],
        (early, late, weights, basis),
        [pltpu.SemaphoreType.DMA],
        out_specs=[VM] * 3,
        flops=20_000_000,
        moved=7_000_000,
        name="own_spread",
    )
    conduct, diagonal, weights = lax.optimization_barrier((conduct, diagonal, weights))
    faces, total = call(
        faces_kernel,
        [shape(4, CELLS, COLS), shape(CELLS, COLS)],
        [VM, VM, SM, VM, VM, VM, VM],
        (conduct, diagonal, soil_table, *from_y, *from_x),
        [field_space],
        flops=4_000_000,
        moved=2_000_000,
        name="faces",
    )
    field, rim, up, dn, first, second = call(
        fold_rows_kernel,
        [shape(CELLS, COLS), shape(80, COLS)]
        + [shape(RUNS + LAYERS, COLS)] * 2
        + [shape(SIDE, COLS, dtype=BF16)] * 2,
        [VM] * 8,
        (own, near_first, near_second, local, *near, far[1], far[0]),
        name="fold_rows",
    )
    from_y = swap_y(first, second)
    precond, image, sums = call(
        image_kernel,
        [shape(CELLS, COLS), shape(CELLS, COLS), shape(devices, COLS)],
        [VM] * 11,
        (field, rim, up, dn, *from_y, basis, faces, total, above, gram),
        [field_space],
        name="image",
    )
    gathered = exchange(sums)
    following, hessenberg = call(
        next_kernel,
        [shape(CELLS, COLS), shape(5)],
        [VM] * 3,
        (gathered, image, basis),
        out_specs=[VM, SM],
        name="next",
    )
    tile = (LAYERS, ROWS, COLS)
    return precond.reshape(tile), following.reshape(tile), hessenberg


def solution(mesh):
    placed = (
        P(None, None, "gx", "gy"),
        P(None, "gx", "gy"),
        P(None, "gx", "gy"),
        P(),
        P("gx", "gy", None, None),
        P(("gx", "gy"), None),
        P("gx", "gy"),
    )
    return jax.shard_map(
        on_device,
        mesh=mesh,
        in_specs=placed,
        out_specs=(P(None, "gx", "gy"), P(None, "gx", "gy"), P()),
        check_vma=False,
    )
```

```python
import functools

import jax
import jax.numpy as jnp
from jax import lax
from jax.experimental import pallas as pl
from jax.experimental.pallas import tpu as pltpu
from jax.sharding import PartitionSpec as P

F32 = jnp.float32
BF16 = jnp.bfloat16

LAYERS, ROWS, COLS, OV, K = 40, 16, 128, 16, 32
CELLS = LAYERS * ROWS
RUNS = CELLS // 4
FLAT = 5 * RUNS
WINDOW = 7680
EARLY = 8
CHUNK = 16
PAD = FLAT + 48
SIDE = RUNS + 48
ENDS = FLAT + 80
PART = 2560
WEIGHT_V, WEIGHT_H, EPS = 4.0, 1.0, 1e-06

VM = pl.BlockSpec(memory_space=pltpu.VMEM)
SM = pl.BlockSpec(memory_space=pltpu.SMEM)
HB = pl.BlockSpec(memory_space=pltpu.HBM)


def shape(*dims, dtype=F32):
    return jax.ShapeDtypeStruct(dims, dtype)


def call(kernel, outs, specs, args, scratch=(), out_specs=None, flops=0, moved=0, name=None):
    return pl.pallas_call(
        kernel,
        out_shape=outs,
        in_specs=specs,
        out_specs=out_specs if out_specs is not None else jax.tree.map(lambda _: VM, outs),
        scratch_shapes=list(scratch),
        compiler_params=pltpu.CompilerParams(vmem_limit_bytes=16 * 2**20),
        cost_estimate=pl.CostEstimate(flops=flops, bytes_accessed=moved, transcendentals=0),
        name=name,
    )(*args)


def lanes(rows):
    return lax.broadcasted_iota(jnp.int32, (rows, COLS), 1)


def harmonic(first, second):
    return 2.0 * first * second / (first + second)


def steps(count):
    return max(n for n in range(1, 9) if count % n == 0)


def turn(values, amount):
    return pltpu.roll(values, amount % COLS, 1)


def pack_kernel(
    basis_in,
    soil_in,
    frozen_in,
    first,
    second,
    flat,
    kinds,
    basis,
    code,
    soil,
    frozen,
    arrived,
):
    copies = [
        pltpu.make_async_copy(basis_in.at[3], basis, arrived.at[0]),
        pltpu.make_async_copy(soil_in, soil, arrived.at[1]),
        pltpu.make_async_copy(frozen_in, frozen, arrived.at[2]),
    ]
    for copy in copies:
        copy.start()
    at = lanes(RUNS)
    to_up = jnp.zeros((RUNS, COLS), F32)
    to_dn = to_up
    flats = [jnp.zeros((RUNS, COLS), F32) for _ in range(5)]
    copies[0].wait()
    for q in range(4):
        cut = 32 * q + 16
        turned = turn(basis[pl.ds(q, RUNS, stride=4), :], cut)
        to_up = jnp.where((at >= cut - 16) & (at < cut), turned, to_up)
        to_dn = jnp.where((at >= cut) & (at < cut + 16), turned, to_dn)
        flats[q] = jnp.where(at >= cut, turned, flats[q])
        flats[q + 1] = jnp.where(at < cut, turned, flats[q + 1])
    for j in range(5):
        flat[j * RUNS : (j + 1) * RUNS, :] = flats[j].astype(BF16)
    for copy in copies[1:]:
        copy.wait()
    code[...] = (soil[...] + 8 * frozen[...]).astype(F32)
    for q in range(4):
        cut = 32 * q + 16
        kind = code[pl.ds(q, RUNS, stride=4), :]
        to_up = jnp.where(at == cut, turn(kind, cut + 1), to_up)
        to_dn = jnp.where(at == cut - 1, turn(kind, cut - 1), to_dn)
    even = lax.axis_index("gy") % 2 == 0
    first[...] = jnp.where(even, to_up, to_dn).astype(BF16)
    second[...] = jnp.where(even, to_dn, to_up).astype(BF16)
    spare = jnp.zeros((PAD - FLAT - LAYERS, COLS), F32)
    for index, row in enumerate((0, ROWS - 1)):
        line = jnp.concatenate([code[pl.ds(row, LAYERS, stride=ROWS), :], spare], axis=0)
        kinds[index] = line


def sides(even, first, second):
    return jnp.where(even, second, first), jnp.where(even, first, second)


def flat_kernel(own, kinds, from_first, from_second, first, second):
    place = lax.axis_index("gy")
    last = lax.axis_size("gy") - 1
    at = lanes(RUNS)
    from_left, from_right = sides(
        place % 2 == 0, from_first[...].astype(F32), from_second[...].astype(F32)
    )
    from_left = jnp.where(place > 0, from_left, 0.0)
    from_right = jnp.where(place < last, from_right, 0.0)
    for j in range(5):
        part = own[j * RUNS : (j + 1) * RUNS, :].astype(F32)
        if j < 4:
            part = jnp.where((at >= 32 * j) & (at < 32 * j + 16), from_left, part)
        if j > 0:
            part = jnp.where((at >= 32 * j - 16) & (at < 32 * j), from_right, part)
        first[j * RUNS : (j + 1) * RUNS, :] = part.astype(BF16)
        second[j * RUNS : (j + 1) * RUNS, :] = part.astype(BF16)
    even = lax.axis_index("gx") % 2 == 0
    first[FLAT:, :] = jnp.where(even, kinds[1], kinds[0]).astype(BF16)
    second[FLAT:, :] = jnp.where(even, kinds[0], kinds[1]).astype(BF16)


def project_part(coarse, vector, part, totals, first, begin, count):
    def body(layer, totals):
        totals = list(totals)
        base = pl.multiple_of((begin + layer) * WINDOW + part * PART, 128)
        row = (first + begin + layer) * 4
        wide = jnp.concatenate(
            [
                jnp.broadcast_to(vector[pl.ds(j * RUNS + row + m, 1), :], (8, COLS))
                for m in range(4)
                for j in range(5)
            ],
            axis=1,
        )
        for r in range(4):
            product = coarse[8 * r : 8 * r + 8, pl.ds(base, PART)].astype(F32) * wide
            for t in range(20):
                slot = 2 * r + t % 2
                totals[slot] = totals[slot] + product[:, t * COLS : (t + 1) * COLS]
        return tuple(totals)

    return lax.fori_loop(0, count, body, totals, unroll=steps(count))


def early_kernel(
    source,
    table_in,
    basis,
    code,
    out,
    conduct,
    diagonal,
    above,
    local,
    ratio,
    value,
    table,
    arrived,
):
    small = pltpu.make_async_copy(table_in, table, arrived.at[0])
    small.start()
    copy = pltpu.make_async_copy(source.at[:, : EARLY * WINDOW], out, arrived.at[1])
    copy.start()
    small.wait()
    solve_columns(basis, code, table, conduct, diagonal, above, local, ratio, value)
    copy.wait()


def multiply_out(basis, gram):
    def body(level, grams):
        grams = list(grams)
        cut = pl.ds(pl.multiple_of(level * ROWS, ROWS), ROWS)
        vectors = [basis[j, cut, :] for j in range(4)]
        slot = 0
        for i in range(4):
            for j in range(i, 4):
                square = vectors[i] * vectors[j]
                grams[slot] = grams[slot] + (square[:8] + square[8:])
                slot += 1
        return tuple(grams)

    zero = jnp.zeros((8, COLS), F32)
    grams = lax.fori_loop(0, LAYERS, body, (zero,) * 10, unroll=4)
    for slot in range(10):
        gram[8 * slot : 8 * slot + 8, :] = grams[slot]


def load_kernel(source, early, own, late, begun, vector, arrived):
    copies = []
    for index in range((LAYERS - EARLY) // CHUNK):
        begin, size = index * CHUNK * WINDOW, CHUNK * WINDOW
        copies.append(
            pltpu.make_async_copy(
                source.at[:, EARLY * WINDOW + begin : EARLY * WINDOW + begin + size],
                late.at[:, begin : begin + size],
                arrived.at[index],
            )
        )
    for copy in copies:
        copy.start()
    vector[...] = own[:FLAT, :].astype(F32)
    totals = (jnp.zeros((8, COLS), F32),) * 8
    totals = project_part(early, vector, 1, totals, 0, 0, EARLY)
    for index, copy in enumerate(copies):
        copy.wait()
        totals = project_part(late, vector, 1, totals, EARLY, index * CHUNK, CHUNK)
    for r in range(4):
        begun[8 * r : 8 * r + 8, :] = totals[2 * r] + totals[2 * r + 1]


def project_neighbour(early, late, whole, vector, upper, valid, totals):
    vector[...] = jnp.where(valid, whole[:FLAT, :].astype(F32), 0.0)
    part = jnp.where(upper, 2, 0)
    totals = project_part(early, vector, part, totals, 0, 0, EARLY)
    return project_part(late, vector, part, totals, EARLY, 0, LAYERS - EARLY)


def unfold(begun):
    zero = jnp.zeros((8, COLS), F32)
    return tuple(begun[4 * s : 4 * s + 8, :] if s % 2 == 0 else zero for s in range(8))


def first_rhs_kernel(early, late, begun, whole, out, vector):
    upper = lax.axis_index("gx") % 2 == 0
    totals = project_neighbour(early, late, whole, vector, upper, True, unfold(begun))
    for r in range(4):
        out[8 * r : 8 * r + 8, :] = totals[2 * r] + totals[2 * r + 1]


def second_rhs_kernel(early, late, begun, whole, count, out, vector):
    place = lax.axis_index("gx")
    valid = (place > 0) & (place < lax.axis_size("gx") - 1)
    totals = project_neighbour(early, late, whole, vector, place % 2 == 1, valid, unfold(begun))
    full = jnp.concatenate([totals[2 * r] + totals[2 * r + 1] for r in range(4)], axis=0)
    sums = jnp.sum(full, axis=1, keepdims=True)
    index = lax.broadcasted_iota(jnp.int32, (K, COLS), 0)
    keep = (lanes(K) % K == index) & (index < count[...])
    row = jnp.sum(jnp.where(keep, sums, 0.0), axis=0, keepdims=True)
    out[...] = jnp.broadcast_to(row, out.shape)


def reduce_eight(parts, where):
    four, two, one = where

    def merge(a, b, mask, step):
        kept = jnp.where(mask, a, b)
        moved = jnp.where(mask, b, a)
        if step == 4:
            return kept + pltpu.roll(moved, 4, 0)
        return kept + jnp.where(mask, pltpu.roll(moved, 8 - step, 0), pltpu.roll(moved, step, 0))

    parts = [merge(parts[t], parts[t + 4], four, 4) for t in range(4)]
    parts = [merge(parts[t], parts[t + 2], two, 2) for t in range(2)]
    return merge(parts[0], parts[1], one, 1)


def reduction_masks():
    row = lax.broadcasted_iota(jnp.int32, (8, COLS), 0)
    return row < 4, row % 4 < 2, row % 2 < 1


def combine(coarse, base, width, weights):
    terms = [
        coarse[8 * r : 8 * r + 8, pl.ds(base, width)].astype(F32) * weights[r][:, :width]
        for r in range(4)
    ]
    return (terms[0] + terms[1]) + (terms[2] + terms[3])


def spread_part(coarse, weights, part, out, first, count):
    where = reduction_masks()

    def body(pair, carry):
        halves = []
        for half in range(2):
            base = pl.multiple_of((2 * pair + half) * WINDOW + part * PART, 128)
            halves.append(combine(coarse, base, PART, weights))
        for j in range(5):
            tiles = [
                halves[half][:, (5 * m + j) * COLS : (5 * m + j + 1) * COLS]
                for half in range(2)
                for m in range(4)
            ]
            start = pl.multiple_of(j * RUNS + 4 * first + 8 * pair, 8)
            out[pl.ds(start, 8), :] = reduce_eight(tiles, where)
        return carry

    lax.fori_loop(0, count // 2, body, 0, unroll=steps(count // 2))


def spread_ends(coarse, weights, begin, out, first, count):
    where = reduction_masks()

    def body(four, carry):
        tiles = []
        for layer in range(4):
            base = (4 * four + layer) * WINDOW + PART + begin
            both = combine(coarse, pl.multiple_of(base, 128), 2 * COLS, weights)
            tiles += [both[:, :COLS], both[:, COLS:]]
        start = pl.multiple_of(2 * first + 8 * four, 8)
        out[pl.ds(start, 8), :] = reduce_eight(tiles, where)
        return carry

    lax.fori_loop(0, count // 4, body, 0, unroll=steps(count // 4))


def widen(weights):
    return [
        jnp.concatenate([weights[8 * r : 8 * r + 8, :]] * (PART // COLS), axis=1) for r in range(4)
    ]


def solve(inverse, gathered, count, rhs):
    at = lanes(K)
    rows = jnp.zeros((K, COLS), F32)
    for e in range(4):
        rows = jnp.where(at // K == e, gathered[pl.ds(e, K, stride=4), :], rows)
    rhs[...] = rows
    total = jnp.zeros((K, COLS), F32)
    for i in range(K):
        total = total + inverse[:, i * COLS : (i + 1) * COLS] * rhs[i : i + 1, :]
    solved = jnp.sum(total, axis=1, keepdims=True)
    index = lax.broadcasted_iota(jnp.int32, (K, COLS), 0)
    return jnp.where(index < count[...], solved, 0.0).astype(BF16).astype(F32)


def spread_to(upper, early, late, solved, local, message, near, whole, ends):
    wide = widen(solved)
    part, begin = jnp.where(upper, 2, 0), jnp.where(upper, 18 * COLS, 0)
    for coarse, start, size in ((early, 0, EARLY), (late, EARLY, LAYERS - EARLY)):
        spread_part(coarse, wide, part, whole, start, size)
        spread_ends(coarse, wide, begin, ends, start, size)
    message[:FLAT, :] = whole[...].astype(BF16)

    def strip(ref, j, m):
        return ref[pl.ds(j * RUNS + m, LAYERS, stride=4), :]

    def both(first, second):
        return jnp.concatenate([first, second], axis=0)

    at = lanes(LAYERS)
    cut = jnp.where(upper, 112, 16)
    row = jnp.where(upper, strip(local, 3, 3), strip(local, 0, 0))
    ours = [ends[pl.ds(index, LAYERS, stride=2), :] for index in range(2)]
    message[FLAT:, :] = both(
        ours[0] + jnp.where(at >= cut, row, 0.0), ours[1] + jnp.where(at < cut, row, 0.0)
    ).astype(BF16)
    top = both(strip(whole, 0, 0), strip(whole, 1, 0))
    bottom = both(strip(whole, 3, 3), strip(whole, 4, 3))
    near[...] = jnp.where(upper, top, bottom)
    return jnp.where(upper, bottom, top)


def first_spread_kernel(
    early, late, inverse, gathered, count, local, weights, message, near, far, rhs, whole, ends
):
    solved = solve(inverse, gathered, count, rhs)
    weights[...] = solved
    upper = lax.axis_index("gx") % 2 == 0
    far[...] = spread_to(upper, early, late, solved, local, message, near, whole, ends)


def second_spread_kernel(
    early, late, weights, local, far, message, near, far_first, far_second, whole, ends
):
    place = lax.axis_index("gx")
    upper = place % 2 == 1
    own = spread_to(upper, early, late, weights[...], local, message, near, whole, ends)
    swapped = (place % 4 == 1) | (place % 4 == 2)
    far_first[...] = jnp.where(swapped, own, far[...]).astype(BF16)
    far_second[...] = jnp.where(swapped, far[...], own).astype(BF16)


def own_spread_kernel(early, late, weights, basis_in, own, basis, gram, ready):
    copy = pltpu.make_async_copy(basis_in, basis, ready)
    copy.start()
    wide = widen(weights[...])
    spread_part(early, wide, 1, own, 0, EARLY)
    spread_part(late, wide, 1, own, EARLY, LAYERS - EARLY)
    copy.wait()
    multiply_out(basis, gram)


def fold_rows_kernel(
    own,
    near_first,
    near_second,
    local,
    from_first,
    from_second,
    far_second,
    far_first,
    field,
    rim,
    up,
    dn,
    first,
    second,
):
    place = lax.axis_index("gx")
    last = lax.axis_size("gx") - 1
    even, lower = place % 2 == 0, place % 4 < 2
    at = lanes(RUNS)
    whole = []
    for j in range(5):
        cut = slice(j * RUNS, (j + 1) * RUNS)
        before, after = sides(even, from_first[cut, :].astype(F32), from_second[cut, :].astype(F32))
        part = own[cut, :] + jnp.where(place > 0, before, 0.0)
        part = part + jnp.where(place < last, after, 0.0)
        if j < 4:
            part = part + jnp.where(at >= 32 * j + 16, local[cut, :], 0.0)
        if j > 0:
            behind = local[(j - 1) * RUNS : j * RUNS, :]
            part = part + jnp.where(at < 32 * j - 16, behind, 0.0)
        whole.append(part)
    to_up = jnp.zeros((RUNS, COLS), F32)
    to_dn = to_up
    for q in range(4):
        field[q * RUNS : (q + 1) * RUNS, :] = jnp.where(
            at >= 32 * q + 16, whole[q], whole[q + 1]
        )
        band = (at >= 32 * q) & (at < 32 * q + 32)
        to_up = jnp.where(band, whole[q + 1], to_up)
        to_dn = jnp.where(band, whole[q], to_dn)
    up[:RUNS, :] = to_up
    dn[:RUNS, :] = to_dn

    before, after = sides(even, from_first[FLAT:, :].astype(F32), from_second[FLAT:, :].astype(F32))
    before2, after2 = sides(lower, far_first[...].astype(F32), far_second[...].astype(F32))
    near_before, near_after = sides(even, near_first[...], near_second[...])
    top = near_before + before + jnp.where(place > 1, before2, 0.0)
    bottom = near_after + after + jnp.where(place < last - 1, after2, 0.0)
    at = lanes(LAYERS)
    half = LAYERS
    rim[:half, :] = jnp.where(at >= 112, top[:half], top[half:])
    rim[half:, :] = jnp.where(at >= 16, bottom[:half], bottom[half:])
    up[RUNS:, :] = jnp.where(at >= 96, top[half:], bottom[half:])
    dn[RUNS:, :] = jnp.where(at >= 96, top[:half], bottom[:half])
    even = lax.axis_index("gy") % 2 == 0
    spare = jnp.zeros((SIDE - RUNS - LAYERS, COLS), F32)
    to_up = jnp.concatenate([up[...], spare], axis=0)
    to_dn = jnp.concatenate([dn[...], spare], axis=0)
    first[...] = jnp.where(even, to_up, to_dn).astype(BF16)
    second[...] = jnp.where(even, to_dn, to_up).astype(BF16)


def look_up(kind, table, rows):
    value = jnp.zeros(kind.shape, F32)
    for index in range(8):
        value = jnp.where(kind == index, table[rows[0], index], value)
        value = jnp.where(kind == index + 8, table[rows[1], index], value)
    return value


def solve_columns(basis, code, table, conduct, diagonal, above, local, ratio, value):
    def body(index, carry):
        cut = pl.ds(pl.multiple_of(index * 160, 160), 160)
        kind = code[cut, :]
        conduct[cut, :] = look_up(kind, table, (0, 1))
        diagonal[cut, :] = look_up(kind, table, (2, 3))
        return carry

    lax.fori_loop(0, CELLS // 160, body, 0)
    zero = jnp.zeros((ROWS, COLS), F32)
    half = LAYERS // 2

    def piece(level):
        return slice(level * ROWS, (level + 1) * ROWS)

    def face(level):
        return WEIGHT_V * harmonic(conduct[piece(level), :], conduct[piece(level + 1), :])

    def eliminate(level, below, over, outer, inner, last_ratio, last_value):
        cut = piece(level)
        middle = diagonal[cut, :] + below + over
        diagonal[cut, :] = middle
        inverse = 1.0 / (middle + 4.0 * WEIGHT_H * conduct[cut, :] + outer * last_ratio)
        next_ratio = -inner * inverse
        next_value = (basis[cut, :] + outer * last_value) * inverse
        ratio[cut, :] = next_ratio
        value[cut, :] = next_value
        return next_ratio, next_value

    low_ratio, low_value, below = zero, zero, zero
    high_ratio, high_value, over = zero, zero, zero
    above[piece(LAYERS - 1), :] = zero
    for step in range(half):
        low, high = step, LAYERS - 1 - step
        low_over, high_below = face(low), face(high - 1)
        above[piece(low), :] = low_over
        if step < half - 1:
            above[piece(high - 1), :] = high_below
        low_ratio, low_value = eliminate(
            low, below, low_over, below, low_over, low_ratio, low_value
        )
        high_ratio, high_value = eliminate(
            high, high_below, over, over, high_below, high_ratio, high_value
        )
        below, over = low_over, high_below
    low_value = (low_value - low_ratio * high_value) / (1.0 - low_ratio * high_ratio)
    high_value = high_value - high_ratio * low_value
    value[piece(half - 1), :] = low_value
    value[piece(half), :] = high_value
    for step in range(1, half):
        low, high = piece(half - 1 - step), piece(half + step)
        low_value = value[low, :] - ratio[low, :] * low_value
        high_value = value[high, :] - ratio[high, :] * high_value
        value[low, :] = low_value
        value[high, :] = high_value
    for q in range(4):
        local[q * RUNS : (q + 1) * RUNS, :] = turn(value[pl.ds(q, RUNS, stride=4), :], 32 * q + 16)


def faces_kernel(
    conduct,
    diagonal,
    table,
    first_y,
    second_y,
    first_x,
    second_x,
    faces,
    total,
    side,
):
    gx, gy = lax.axis_index("gx"), lax.axis_index("gy")
    last_x, last_y = lax.axis_size("gx") - 1, lax.axis_size("gy") - 1
    at = lanes(RUNS)
    from_left, from_right = sides(
        gy % 2 == 0, first_y[...].astype(F32), second_y[...].astype(F32)
    )
    kinds = jnp.zeros((RUNS, COLS), F32)
    for q in range(4):
        kinds = jnp.where(at == 32 * q + 16, from_left, kinds)
        kinds = jnp.where(at == 32 * q + 15, from_right, kinds)
    known = look_up(kinds.astype(jnp.int32), table, (0, 1))
    for q in range(4):
        side[pl.ds(q, RUNS, stride=4), :] = turn(known, -(32 * q + 16))
    before, after = sides(
        gx % 2 == 0, first_x[FLAT:, :].astype(F32), second_x[FLAT:, :].astype(F32)
    )
    row_before = look_up(before.astype(jnp.int32), table, (0, 1))
    row_after = look_up(after.astype(jnp.int32), table, (0, 1))
    at = lanes(ROWS)
    row = lax.broadcasted_iota(jnp.int32, (ROWS, COLS), 0)
    for level in range(LAYERS):
        cut = slice(level * ROWS, (level + 1) * ROWS)
        own = conduct[cut, :]
        aside = side[cut, :]
        over = row_before[level : level + 1, :]
        under = row_after[level : level + 1, :]
        weights = [
            jnp.where((at > 0) | (gy > 0), harmonic(own, jnp.where(at == 0, aside, turn(own, 1))), 0.0),
            jnp.where(
                (at < COLS - 1) | (gy < last_y),
                harmonic(own, jnp.where(at == COLS - 1, aside, turn(own, -1))),
                0.0,
            ),
            jnp.where(
                (row > 0) | (gx > 0),
                harmonic(own, jnp.where(row == 0, over, pltpu.roll(own, 1, 0))),
                0.0,
            ),
            jnp.where(
                (row < ROWS - 1) | (gx < last_x),
                harmonic(own, jnp.where(row == ROWS - 1, under, pltpu.roll(own, ROWS - 1, 0))),
                0.0,
            ),
        ]
        for index in range(4):
            faces[index, cut, :] = WEIGHT_H * weights[index]
        total[cut, :] = diagonal[cut, :] + WEIGHT_H * (
            (weights[0] + weights[1]) + (weights[2] + weights[3])
        )


def image_kernel(
    field,
    rim,
    up,
    dn,
    from_first,
    from_second,
    basis,
    faces,
    total,
    above,
    gram,
    precond,
    image,
    sums,
    side,
):
    gy = lax.axis_index("gy")
    last_y = lax.axis_size("gy") - 1
    at = lanes(RUNS)
    from_left, from_right = sides(
        gy % 2 == 0,
        from_first[...].astype(F32)[: RUNS + LAYERS],
        from_second[...].astype(F32)[: RUNS + LAYERS],
    )
    from_left = jnp.where(gy > 0, from_left, 0.0)
    from_right = jnp.where(gy < last_y, from_right, 0.0)
    to_left = dn[...] + from_left
    to_right = up[...] + from_right
    for q in range(4):
        cut = 32 * q + 16
        turned = field[q * RUNS : (q + 1) * RUNS, :]
        turned = turned + jnp.where((at >= cut) & (at < cut + 16), from_left[:RUNS], 0.0)
        turned = turned + jnp.where((at >= cut - 16) & (at < cut), from_right[:RUNS], 0.0)
        precond[pl.ds(q, RUNS, stride=4), :] = turn(turned, -cut)
        edges = jnp.where(at == cut - 1, to_left[:RUNS], to_right[:RUNS])
        side[pl.ds(q, RUNS, stride=4), :] = turn(edges, -cut)
    at = lanes(LAYERS)
    rim_left, rim_right = from_left[RUNS:], from_right[RUNS:]
    over = rim[:LAYERS, :]
    over = over + jnp.where(at >= 112, rim_left, 0.0)
    over = turn(over + jnp.where((at >= 96) & (at < 112), rim_right, 0.0), -112)
    under = rim[LAYERS:, :]
    under = under + jnp.where((at >= 16) & (at < 32), rim_left, 0.0)
    under = turn(under + jnp.where(at < 16, rim_right, 0.0), -16)
    at = lanes(ROWS)
    row = lax.broadcasted_iota(jnp.int32, (ROWS, COLS), 0)
    totals = [jnp.zeros((8, COLS), F32) for _ in range(5)]
    for level in range(LAYERS):
        cut = slice(level * ROWS, (level + 1) * ROWS)
        own = precond[cut, :]
        aside = side[cut, :]
        result = total[cut, :] * own
        result = result - faces[0, cut, :] * turn(jnp.where(at == COLS - 1, aside, own), 1)
        result = result - faces[1, cut, :] * turn(jnp.where(at == 0, aside, own), -1)
        result = result - faces[2, cut, :] * jnp.where(
            row == 0, over[level : level + 1, :], pltpu.roll(own, 1, 0)
        )
        result = result - faces[3, cut, :] * jnp.where(
            row == ROWS - 1, under[level : level + 1, :], pltpu.roll(own, ROWS - 1, 0)
        )
        if level > 0:
            back = slice((level - 1) * ROWS, level * ROWS)
            result = result - above[back, :] * precond[back, :]
        if level < LAYERS - 1:
            ahead = slice((level + 1) * ROWS, (level + 2) * ROWS)
            result = result - above[cut, :] * precond[ahead, :]
        image[cut, :] = result
        for j in range(5):
            product = (basis[j, cut, :] if j < 4 else result) * result
            totals[j] = totals[j] + (product[:8] + product[8:])
    totals += [gram[8 * slot : 8 * slot + 8, :] for slot in range(10)]
    totals.append(jnp.zeros((8, COLS), F32))
    rows = jnp.concatenate([jnp.sum(part, axis=0, keepdims=True) for part in totals], axis=0)
    column = jnp.sum(rows, axis=1, keepdims=True)
    keep = lanes(ROWS) == lax.broadcasted_iota(jnp.int32, (ROWS, COLS), 0)
    line = jnp.sum(jnp.where(keep, column, 0.0), axis=0, keepdims=True)
    sums[...] = jnp.broadcast_to(line, sums.shape)


def next_kernel(gathered, image, basis, out, hessenberg):
    cells = float(CELLS * COLS * lax.axis_size("gx") * lax.axis_size("gy"))
    line = jnp.sum(gathered[...], axis=0, keepdims=True) / cells
    entry = [line[:, i : i + 1] for i in range(15)]
    project = entry[:4]
    square = entry[4]
    for j in range(4):
        square = square - 2.0 * project[j] * project[j]
    slot = 5
    for i in range(4):
        for j in range(i, 4):
            square = square + (1.0 if i == j else 2.0) * project[i] * project[j] * entry[slot]
            slot += 1
    length = jnp.sqrt(jnp.maximum(square, 0.0) + EPS)
    at = lanes(1)
    found = jnp.where(at == 4, length, jnp.where(at < 4, line, 0.0))
    for i in range(5):
        hessenberg[i] = found[0, i]
    inverse = 1.0 / length
    scaled = [project[j] * inverse for j in range(4)]
    for level in range(LAYERS):
        cut = slice(level * ROWS, (level + 1) * ROWS)
        value = image[cut, :] * inverse
        for j in range(4):
            value = value - scaled[j] * basis[j, cut, :]
        out[cut, :] = value


def swap(values, partner):
    across, along = lax.axis_size("gx"), lax.axis_size("gy")
    pairs = []
    for a in range(across):
        for b in range(along):
            c, d = partner(a, b)
            if not 0 <= d < along:
                c, d = a ^ 1, b
            if not 0 <= c < across:
                c, d = a, b ^ 1
            pairs.append((a * along + b, c * along + d))
    return lax.ppermute(values, ("gx", "gy"), pairs)


def swap_y(first, second):
    from_second = swap(second, lambda a, b: (a, ((b + 1) ^ 1) - 1))
    return swap(first, lambda a, b: (a, b ^ 1)), from_second


def swap_x_first(values):
    return swap(values, lambda a, b: (a ^ 1, b))


def swap_x_second(values):
    return swap(values, lambda a, b: (((a + 1) ^ 1) - 1, b))


def swap_far(first, second):
    from_second = swap(second, lambda a, b: (((a + 2) ^ 2) - 2, b))
    return swap(first, lambda a, b: (a ^ 2, b)), from_second


def exchange(lines):
    size = lines.shape[0]
    out = lax.all_to_all(lines.reshape(size, 1, COLS), ("gx", "gy"), 0, 0)
    return out.reshape(size, COLS)


def on_device(basis, soil, frozen, soil_table, coarse_basis, coarse_inverse, active_count):
    basis = basis.reshape(4, CELLS, COLS)
    soil, frozen = soil.reshape(CELLS, COLS), frozen.reshape(CELLS, COLS)
    source = pltpu.with_memory_space_constraint(coarse_basis.reshape(K, -1), pltpu.HBM)
    devices = lax.axis_size("gx") * lax.axis_size("gy")
    field_space = pltpu.VMEM((CELLS, COLS), F32)
    kinds = pltpu.VMEM((CELLS, COLS), jnp.int32)
    basis, soil, frozen = (
        pltpu.with_memory_space_constraint(x, pltpu.HBM) for x in (basis, soil, frozen)
    )
    first, second, flat, kinds_x, current, code = call(
        pack_kernel,
        [
            shape(RUNS, COLS, dtype=BF16),
            shape(RUNS, COLS, dtype=BF16),
            shape(FLAT, COLS, dtype=BF16),
            shape(2, PAD - FLAT, COLS),
            pltpu.VMEM((CELLS, COLS), F32),
            pltpu.VMEM((CELLS, COLS), F32),
        ],
        [HB] * 3,
        (basis, soil, frozen),
        [kinds, kinds, pltpu.SemaphoreType.DMA((3,))],
        out_specs=[VM] * 6,
        name="pack",
    )
    from_y = swap_y(first, second)
    early, conduct, diagonal, above, local = call(
        early_kernel,
        [pltpu.VMEM((K, EARLY * WINDOW), BF16)] + [shape(CELLS, COLS)] * 4,
        [HB, HB, VM, VM],
        (source, pltpu.with_memory_space_constraint(soil_table, pltpu.HBM), current, code),
        [
            field_space,
            field_space,
            pltpu.SMEM((4, 8), F32),
            pltpu.SemaphoreType.DMA((2,)),
        ],
        out_specs=[VM] * 5,
        moved=10_000_000,
        name="early",
    )
    early, flat = lax.optimization_barrier((early, flat))
    flat, second = call(
        flat_kernel, [shape(PAD, COLS, dtype=BF16)] * 2, [VM] * 4, (flat, kinds_x, *from_y), name="flat"
    )
    from_second = swap_x_second(second)
    from_x = swap_x_first(flat), from_second
    late, begun = call(
        load_kernel,
        [
            pltpu.VMEM((K, (LAYERS - EARLY) * WINDOW), BF16),
            shape(K, COLS),
        ],
        [HB, VM, VM],
        (source, early, flat),
        [
            pltpu.VMEM((FLAT, COLS), F32),
            pltpu.SemaphoreType.DMA(((LAYERS - EARLY) // CHUNK,)),
        ],
        out_specs=[VM] * 2,
        flops=16_000_000,
        moved=20_000_000,
        name="load",
    )
    vector = pltpu.VMEM((FLAT, COLS), F32)
    begun = call(
        first_rhs_kernel,
        shape(K, COLS),
        [VM] * 4,
        (early, late, begun, from_x[0]),
        [vector],
        flops=6_000_000,
        moved=6_000_000,
        name="first_rhs",
    )
    lines = call(
        second_rhs_kernel,
        shape(devices, COLS),
        [VM] * 5,
        (early, late, begun, from_x[1], active_count),
        [vector],
        flops=6_000_000,
        moved=6_000_000,
        name="second_rhs",
    )
    gathered = exchange(lines)
    message = shape(ENDS, COLS, dtype=BF16)
    ends = pltpu.VMEM((2 * LAYERS, COLS), F32)
    weights, first, near_first, far = call(
        first_spread_kernel,
        [shape(K, COLS), message, shape(80, COLS), shape(80, COLS)],
        [VM] * 6,
        (early, late, coarse_inverse, gathered, active_count, local),
        [pltpu.VMEM((K, COLS), F32), vector, ends],
        flops=20_000_000,
        moved=8_000_000,
        name="first_spread",
    )
    from_first = swap_x_first(first)
    second, near_second, far_first, far_second = call(
        second_spread_kernel,
        [message, shape(80, COLS)] + [shape(80, COLS, dtype=BF16)] * 2,
        [VM] * 5,
        (early, late, weights, local, far),
        [vector, ends],
        flops=20_000_000,
        moved=8_000_000,
        name="second_spread",
    )
    near = from_first, swap_x_second(second)
    far = swap_far(far_first, far_second)
    own, basis, gram = call(
        own_spread_kernel,
        [shape(FLAT, COLS), pltpu.VMEM((4, CELLS, COLS), F32), shape(80, COLS)],
        [VM] * 3 + [HB],
        (early, late, weights, basis),
        [pltpu.SemaphoreType.DMA],
        out_specs=[VM] * 3,
        flops=20_000_000,
        moved=7_000_000,
        name="own_spread",
    )
    conduct, diagonal, weights = lax.optimization_barrier((conduct, diagonal, weights))
    faces, total = call(
        faces_kernel,
        [shape(4, CELLS, COLS), shape(CELLS, COLS)],
        [VM, VM, SM, VM, VM, VM, VM],
        (conduct, diagonal, soil_table, *from_y, *from_x),
        [field_space],
        flops=4_000_000,
        moved=2_000_000,
        name="faces",
    )
    field, rim, up, dn, first, second = call(
        fold_rows_kernel,
        [shape(CELLS, COLS), shape(80, COLS)]
        + [shape(RUNS + LAYERS, COLS)] * 2
        + [shape(SIDE, COLS, dtype=BF16)] * 2,
        [VM] * 8,
        (own, near_first, near_second, local, *near, far[1], far[0]),
        name="fold_rows",
    )
    from_y = swap_y(first, second)
    precond, image, sums = call(
        image_kernel,
        [shape(CELLS, COLS), shape(CELLS, COLS), shape(devices, COLS)],
        [VM] * 11,
        (field, rim, up, dn, *from_y, basis, faces, total, above, gram),
        [field_space],
        name="image",
    )
    gathered = exchange(sums)
    following, hessenberg = call(
        next_kernel,
        [shape(CELLS, COLS), shape(5)],
        [VM] * 3,
        (gathered, image, basis),
        out_specs=[VM, SM],
        name="next",
    )
    tile = (LAYERS, ROWS, COLS)
    return precond.reshape(tile), following.reshape(tile), hessenberg


def solution(mesh):
    placed = (
        P(None, None, "gx", "gy"),
        P(None, "gx", "gy"),
        P(None, "gx", "gy"),
        P(),
        P("gx", "gy", None, None),
        P(("gx", "gy"), None),
        P("gx", "gy"),
    )
    return jax.shard_map(
        on_device,
        mesh=mesh,
        in_specs=placed,
        out_specs=(P(None, "gx", "gy"), P(None, "gx", "gy"), P()),
        check_vma=False,
    )
```
